32 devices in a mesh: seq: 4 (over y, core), shard: 4 (over z), replica: 2 (over x).
Axes of the slice: x: 2, y: 2, z: 4, core: 2. Of those that a mesh axis runs over, the one named last changes fastest.
Arguments:
- inputs: bfloat16 [8, 1024, 2048], P(('shard', 'replica'), 'seq'), may hold values from -6 to 6
- cotangent: bfloat16 [8, 1024, 2048], P(('shard', 'replica'), 'seq'), may hold values from -6 to 6
- norm1_gain: float32 [2048], P(('seq', 'shard')), may hold values from 0.5 to 1.5
- norm1_bias: float32 [2048], P(('seq', 'shard')), may hold values from -1.5 to 1.5
- w_qkv: float32 [2048, 6144], P(('seq', 'shard')), may hold values from -0.125 to 0.125
- query_bias: float32 [2048], P(('seq', 'shard')), may hold values from -1.5 to 1.5
- value_bias: float32 [2048], P(('seq', 'shard')), may hold values from -1.5 to 1.5
- w_attn_out: float32 [2048, 2048], P(('seq', 'shard')), may hold values from -0.5 to 0.5
- attn_out_bias: float32 [2048], P(('seq', 'shard')), may hold values from -1.5 to 1.5
- norm2_gain: float32 [2048], P(('seq', 'shard')), may hold values from 0.5 to 1.5
- norm2_bias: float32 [2048], P(('seq', 'shard')), may hold values from -1.5 to 1.5
- w_hidden: float32 [2048, 8192], P(('seq', 'shard')), may hold values from -0.125 to 0.125
- hidden_bias: float32 [8192], P(('seq', 'shard')), may hold values from -1.5 to 1.5
- w_output: float32 [8192, 2048], P(('seq', 'shard')), may hold values from -0.0625 to 0.0625
- output_bias: float32 [2048], P(('seq', 'shard')), may hold values from -1.5 to 1.5
Outputs:
- output: bfloat16 [8, 1024, 2048], P(('shard', 'replica'), 'seq')
- grad_inputs: float32 [8, 1024, 2048], P(('shard', 'replica'), 'seq')
- grad_norm1_gain: float32 [2048], P(('seq', 'shard'))
- grad_norm1_bias: float32 [2048], P(('seq', 'shard'))
- grad_w_qkv: float32 [2048, 6144], P(('seq', 'shard'))
- grad_query_bias: float32 [2048], P(('seq', 'shard'))
- grad_value_bias: float32 [2048], P(('seq', 'shard'))
- grad_w_attn_out: float32 [2048, 2048], P(('seq', 'shard'))
- grad_attn_out_bias: float32 [2048], P(('seq', 'shard'))
- grad_norm2_gain: float32 [2048], P(('seq', 'shard'))
- grad_norm2_bias: float32 [2048], P(('seq', 'shard'))
- grad_w_hidden: float32 [2048, 8192], P(('seq', 'shard'))
- grad_hidden_bias: float32 [8192], P(('seq', 'shard'))
- grad_w_output: float32 [8192, 2048], P(('seq', 'shard'))
- grad_output_bias: float32 [2048], P(('seq', 'shard'))
The draws below stay inside these ranges and needn't reach their ends.
All inputs are finite; a program needn't handle non-finite values.
Results may differ from the reference program's by a relative error of at most 0.015.
Values may be sent and summed in bfloat16 or wider, within the bound.
No kernel may reach another device: no remote copies, remote signals or barrier semaphores. Data moves between devices by JAX's collectives and lax.ppermute only.
A program may use at most 512 MiB of HBM per device.

```python
import jax
import jax.numpy as jnp
from jax import lax

D = 2048
HEAD_DIM = 128
FF = 8192
BLOCK = 256
LEN = 1024
SEQS = 8


def block_scale(key, shape, cuts, smallest, high):
    level = 1.0
    for dim, parts in cuts:
        steps = jax.random.uniform(jax.random.fold_in(jax.random.fold_in(key, 6), dim), (parts,), jnp.float32, smallest / len(cuts), high / len(cuts))
        level = level * jnp.repeat(jnp.exp(steps), shape[dim] // parts).reshape((-1,) + (1,) * (len(shape) - 1 - dim))
    return level


def noise(stream_key, extent, spread, most, split=(), kind=jnp.bfloat16):
    values = jax.random.normal(stream_key, extent, jnp.float32) * spread
    if len(split) > 0:
        values = block_scale(stream_key, extent, split, -0.22, 0.18) * values
    return jnp.clip(values, min=-most, max=most).astype(kind)


def setup_inputs(seed: int = 0) -> dict:
    key_list = jax.random.split(jax.random.key(seed), 16)
    return {
        "inputs": noise(key_list[0], (SEQS, LEN, D), 1.0, 6.0, ((0, 8), (1, 4))),
        "cotangent": noise(key_list[1], (SEQS, LEN, D), 1.0, 6.0, ((0, 8), (1, 4))),
        "norm1_gain": jnp.clip(1.0 + 0.1 * jax.random.normal(key_list[2], (D,), jnp.float32), 0.5, 1.5),
        "norm1_bias": noise(key_list[3], (D,), 0.3, 1.5, ((0, 16),), jnp.float32),
        "w_qkv": noise(key_list[4], (D, 3 * D), D ** -0.5, 0.125, ((0, 16),), jnp.float32),
        "query_bias": noise(key_list[5], (D,), 0.3, 1.5, ((0, 16),), jnp.float32),
        "value_bias": noise(key_list[6], (D,), 0.3, 1.5, ((0, 16),), jnp.float32),
        "w_attn_out": noise(key_list[7], (D, D), (D // 16) ** -0.5, 0.5, ((0, 16),), jnp.float32),
        "attn_out_bias": noise(key_list[8], (D,), 0.3, 1.5, ((0, 16),), jnp.float32),
        "norm2_gain": jnp.clip(1.0 + 0.1 * jax.random.normal(key_list[9], (D,), jnp.float32), 0.5, 1.5),
        "norm2_bias": noise(key_list[10], (D,), 0.3, 1.5, ((0, 16),), jnp.float32),
        "w_hidden": noise(key_list[11], (D, FF), D ** -0.5, 0.125, ((0, 16),), jnp.float32),
        "hidden_bias": noise(key_list[12], (FF,), 0.3, 1.5, ((0, 16),), jnp.float32),
        "w_output": noise(key_list[13], (FF, D), FF ** -0.5, 0.0625, ((0, 16),), jnp.float32),
        "output_bias": noise(key_list[14], (D,), 0.3, 1.5, ((0, 16),), jnp.float32),
    }


@jax.custom_vjp
def low(v):
    return lax.optimization_barrier(v.astype(jnp.bfloat16)).astype(jnp.float32)

@jax.custom_vjp
def low_back(v):
    return v

def low_keep(v):
    return (low(v), None)

def low_pass(kept, grad):
    return (grad,)

def back_keep(v):
    return (v, None)

def back_low(kept, grad):
    return (low(grad),)
low.defvjp(low_keep, low_pass)
low_back.defvjp(back_keep, back_low)
precise = lax.Precision.HIGHEST

def normalize(values, gain, shift):
    mean_row = lax.optimization_barrier(jnp.mean(values, axis=-1, keepdims=True))
    centred = values - mean_row
    scale_row = lax.rsqrt(lax.optimization_barrier(jnp.mean(centred * centred, axis=-1, keepdims=True)) + 1e-05)
    return centred * scale_row * gain + shift

def sequence_layer(weights, tokens):
    gain_one, shift_one, qkv_matrix, query_shift, value_shift, attn_matrix, attn_shift, gain_two, shift_two, hidden_matrix, hidden_shift, output_matrix, output_shift = weights
    length = tokens.shape[0]
    model_width = tokens.shape[1]
    head_count = model_width // HEAD_DIM
    hidden_in = low(normalize(tokens, gain_one, shift_one))
    bias_row = jnp.concatenate([query_shift, jnp.zeros_like(query_shift), value_shift])
    qkv_rows = low(low_back(jnp.dot(hidden_in, qkv_matrix, precision=precise) + bias_row))
    queries = qkv_rows[:, :model_width].reshape(length, head_count, HEAD_DIM)
    key_rows = qkv_rows[:, model_width:2 * model_width].reshape(length, head_count, HEAD_DIM)
    value_rows = qkv_rows[:, 2 * model_width:].reshape(length, head_count, HEAD_DIM)
    scores = jnp.einsum('qhd,khd->hqk', queries, key_rows, precision=precise) * HEAD_DIM ** (-0.5)
    scores = low_back(scores)
    blocks = jnp.arange(length) // BLOCK
    allowed = blocks[None, :] <= blocks[:, None]
    scores = jnp.where(allowed[None, :, :], scores, -1e+30)
    row_top = lax.optimization_barrier(jnp.max(scores, axis=-1, keepdims=True))
    expons = jnp.exp(scores - row_top)
    soft_probs = low(expons / lax.optimization_barrier(jnp.sum(expons, axis=-1, keepdims=True)))
    attended = jnp.einsum('hqk,khd->qhd', soft_probs, value_rows, precision=precise).reshape(length, model_width)
    attended = low(low_back(attended))
    mid_rows = tokens + low_back(jnp.dot(attended, attn_matrix, precision=precise) + attn_shift)
    hidden_two = low(normalize(mid_rows, gain_two, shift_two))
    preactive = low_back(jnp.dot(hidden_two, hidden_matrix, precision=precise) + hidden_shift)
    activated = low(jax.nn.gelu(preactive, approximate=False))
    return mid_rows + low_back(jnp.dot(activated, output_matrix, precision=precise) + output_shift)

def forward(weights, tokens_all):
    layer = jax.checkpoint(sequence_layer)

    def advance(carry, tokens):
        return (carry, layer(weights, tokens))
    unused, outputs = lax.scan(advance, jnp.zeros((), jnp.float32), tokens_all)
    return outputs

def reference(inputs, cotangent, norm1_gain, norm1_bias, w_qkv, query_bias, value_bias, w_attn_out, attn_out_bias, norm2_gain, norm2_bias, w_hidden, hidden_bias, w_output, output_bias):

    def whole(tokens_all, masters):
        weights = tuple((low(master) for master in masters))
        return forward(weights, tokens_all)
    masters = (norm1_gain, norm1_bias, w_qkv, query_bias, value_bias, w_attn_out, attn_out_bias, norm2_gain, norm2_bias, w_hidden, hidden_bias, w_output, output_bias)
    output, pull = jax.vjp(whole, inputs.astype(jnp.float32), masters)
    grad_inputs, grads = pull(cotangent.astype(jnp.float32))
    return (output.astype(jnp.bfloat16), grad_inputs, grads[0], grads[1], grads[2], grads[3], grads[4], grads[5], grads[6], grads[7], grads[8], grads[9], grads[10], grads[11], grads[12])
```

```python
import jax
import jax.numpy as jnp
from jax import lax
from jax.experimental import pallas as pl
from jax.experimental.pallas import tpu as pltpu
from jax.sharding import PartitionSpec as P

HEAD_DIM = 128
bf16 = jnp.bfloat16
fp32 = jnp.float32

CORE = ("seq", 1)
ROW = ("seq", 2)
COL = ("replica", 1)


def normalize(values):
    mean_row = jnp.mean(values, axis=1, keepdims=True)
    centred = values - mean_row
    scale_row = lax.rsqrt(jnp.mean(centred * centred, axis=1, keepdims=True) + 1e-05)
    return (centred * scale_row, scale_row)


def norm_back(grad_normed, normed, scale_row):
    first_mean = jnp.mean(grad_normed, axis=1, keepdims=True)
    second_mean = jnp.mean(grad_normed * normed, axis=1, keepdims=True)
    return scale_row * (grad_normed - first_mean - normed * second_mean)


def gelu_slope(values):
    normal_cdf = 0.5 * (1.0 + lax.erf(values * 0.7071067811865476))
    return normal_cdf + values * jnp.exp(-0.5 * values * values) * 0.3989422804014327


def column_sums(values):
    return jnp.sum(values.astype(fp32), axis=0)


def flip(v, link):
    axis, bit = link
    return lax.ppermute(v, axis, [(i, i ^ bit) for i in range(lax.axis_size(axis))])


def hop(v, seq_bits, rep_bit):
    if rep_bit == 0:
        return flip(v, ("seq", seq_bits)) if seq_bits else v
    if seq_bits == 0:
        return flip(v, COL)
    S, R = lax.axis_size("seq"), lax.axis_size("replica")
    pairs = [(s * R + r, (s ^ seq_bits) * R + (r ^ rep_bit)) for s in range(S) for r in range(R)]
    return lax.ppermute(v, ("seq", "replica"), pairs)


def plane_gather(v):
    h = v.shape[0] // 2
    near = flip(v, CORE)
    py, px = flip(v, ROW), flip(v, COL)
    da, db = flip(py[:h], COL), flip(px[h:], ROW)
    cy, cx = flip(py, CORE), flip(px, CORE)
    ca, cb = flip(da, CORE), flip(db, CORE)
    return [jnp.concatenate(p) for p in ([v, near], [py, cy], [px, cx], [da, db, ca, cb])]


def plane_scatter(parts):
    n = parts[0].shape[0] // 2
    h = n // 2
    got = [flip(p[n:], CORE) for p in parts]
    sums = [p[:n].astype(fp32) + g.astype(fp32) for p, g in zip(parts, got)]
    py, px, pd = (v.astype(bf16) for v in sums[1:])
    ra, rb = flip(pd[:h], COL), flip(pd[h:], ROW)
    x_top, y_bot = flip(px[:h], COL), flip(py[h:], ROW)
    x_bot = flip((sums[2][h:] + rb.astype(fp32)).astype(bf16), COL)
    y_top = flip((sums[1][:h] + ra.astype(fp32)).astype(bf16), ROW)
    top = sums[0][:h] + x_top.astype(fp32) + y_top.astype(fp32)
    bot = sums[0][h:] + x_bot.astype(fp32) + y_bot.astype(fp32)
    return jnp.concatenate([top, bot])


def line_gather(v):
    Z, z = lax.axis_size("shard"), lax.axis_index("shard")
    up, down = [v], [v]
    for k in range(1, Z):
        up.append(lax.ppermute(up[-1], "shard", [(i, i + 1) for i in range(k - 1, Z - 1)]))
        down.append(lax.ppermute(down[-1], "shard", [(i, i - 1) for i in range(1, Z - k + 1)]))
    out = jnp.zeros((Z,) + v.shape, v.dtype)
    out = lax.dynamic_update_index_in_dim(out, v, z, 0)
    for k in range(1, Z):
        piece = jnp.where(z >= k, up[k], down[Z - k])
        out = lax.dynamic_update_index_in_dim(out, piece, lax.rem(z - k + Z, Z), 0)
    return out


def line_scatter(v):
    Z, z = lax.axis_size("shard"), lax.axis_index("shard")
    up = down = 0.0
    for k in range(1, Z):
        send_up = lax.dynamic_index_in_dim(v, jnp.minimum(z + Z - k, Z - 1), 0, keepdims=False)
        send_down = lax.dynamic_index_in_dim(v, jnp.maximum(z - (Z - k), 0), 0, keepdims=False)
        if k > 1:
            send_up = send_up.astype(fp32) + up
            send_down = send_down.astype(fp32) + down
        up = lax.ppermute(send_up.astype(bf16), "shard", [(i, i + 1) for i in range(0, k)]).astype(fp32)
        down = lax.ppermute(send_down.astype(bf16), "shard", [(i, i - 1) for i in range(Z - k, Z)]).astype(fp32)
    own = lax.dynamic_index_in_dim(v, z, 0, keepdims=False)
    return own.astype(fp32) + up + down


def in_order(pieces, index):
    bit = 1
    while bit < len(pieces):
        odd = (index & bit) != 0
        pieces = [jnp.where(odd, pieces[j ^ bit], pieces[j]) for j in range(len(pieces))]
        bit *= 2
    return jnp.stack(pieces)


def seq_exchange(v):
    S, s = lax.axis_size("seq"), lax.axis_index("seq")
    got = [hop(lax.dynamic_index_in_dim(v, s ^ j, 0, keepdims=False), j, 0) for j in range(S)]
    return in_order(got, s)


def gather_table(v):
    table = v[None]
    for axis in ("shard", "seq"):
        index, bit = lax.axis_index(axis), 1
        while bit < lax.axis_size(axis):
            other = flip(table, (axis, bit))
            odd = (index & bit) != 0
            table = jnp.concatenate([jnp.where(odd, other, table), jnp.where(odd, table, other)])
            bit *= 2
    return table


def total(v):
    for axis in ("seq", "replica", "shard"):
        bit = 1
        while bit < lax.axis_size(axis):
            v = v + flip(v, (axis, bit))
            bit *= 2
    return v


def attend_kernel(heads, own_ref, qkv_ref, out_ref, k_ref, v_ref):
    own = own_ref[0]
    _, blocks, length, _ = qkv_ref.shape
    width = heads * HEAD_DIM
    for h in range(heads):
        cols = slice(h * HEAD_DIM, (h + 1) * HEAD_DIM)
        for b in range(blocks):
            rows = slice(b * length, (b + 1) * length)
            k_ref[rows, :] = qkv_ref[0, own ^ b, :, width + h * HEAD_DIM : width + (h + 1) * HEAD_DIM]
            v_ref[rows, :] = qkv_ref[0, own ^ b, :, 2 * width + h * HEAD_DIM : 2 * width + (h + 1) * HEAD_DIM]
        for a in range(blocks):
            upto = (a + 1) * length
            q = qkv_ref[0, own ^ a, :, cols]
            scores = lax.dot_general(q, k_ref[:upto, :], (((1,), (1,)), ((), ())), preferred_element_type=fp32)
            scores = scores * HEAD_DIM ** (-0.5)
            expons = jnp.exp(scores - jnp.max(scores, axis=-1, keepdims=True))
            probs = (expons / jnp.sum(expons, axis=-1, keepdims=True)).astype(bf16)
            out_ref[0, own ^ a, :, cols] = jnp.dot(probs, v_ref[:upto, :], preferred_element_type=fp32).astype(bf16)


def attend_back_kernel(heads, own_ref, qkv_ref, grad_ref, out_ref, k_ref, v_ref, gk_ref, gv_ref):
    own = own_ref[0]
    _, blocks, length, _ = qkv_ref.shape
    width = heads * HEAD_DIM
    scaling = HEAD_DIM ** (-0.5)
    across = (((1,), (1,)), ((), ()))
    down = (((0,), (0,)), ((), ()))
    for h in range(heads):
        cols = slice(h * HEAD_DIM, (h + 1) * HEAD_DIM)
        k_cols = slice(width + h * HEAD_DIM, width + (h + 1) * HEAD_DIM)
        v_cols = slice(2 * width + h * HEAD_DIM, 2 * width + (h + 1) * HEAD_DIM)
        for b in range(blocks):
            rows = slice(b * length, (b + 1) * length)
            k_ref[rows, :] = qkv_ref[0, own ^ b, :, k_cols]
            v_ref[rows, :] = qkv_ref[0, own ^ b, :, v_cols]
        for a in reversed(range(blocks)):
            upto = (a + 1) * length
            q = qkv_ref[0, own ^ a, :, cols]
            g = grad_ref[0, own ^ a, :, cols]
            k = k_ref[:upto, :]
            v = v_ref[:upto, :]
            scores = lax.dot_general(q, k, across, preferred_element_type=fp32) * scaling
            expons = jnp.exp(scores - jnp.max(scores, axis=-1, keepdims=True))
            probs = expons / jnp.sum(expons, axis=-1, keepdims=True)
            grad_probs = lax.dot_general(g, v, across, preferred_element_type=fp32)
            inner = jnp.sum(probs * grad_probs, axis=-1, keepdims=True)
            grad_scores = (probs * (grad_probs - inner)).astype(bf16)
            gq = jnp.dot(grad_scores, k, preferred_element_type=fp32) * scaling
            out_ref[0, own ^ a, :, cols] = gq.astype(bf16)
            gk = lax.dot_general(grad_scores, q, down, preferred_element_type=fp32)
            gv = lax.dot_general(probs.astype(bf16), g, down, preferred_element_type=fp32)
            if a == blocks - 1:
                gk_ref[...] = gk
                gv_ref[...] = gv
            else:
                gk_ref[:upto, :] += gk
                gv_ref[:upto, :] += gv
        for b in range(blocks):
            rows = slice(b * length, (b + 1) * length)
            out_ref[0, own ^ b, :, k_cols] = (gk_ref[rows, :] * scaling).astype(bf16)
            out_ref[0, own ^ b, :, v_cols] = gv_ref[rows, :].astype(bf16)


def attention_call(kernel, own, operands, out_width, scratch, flops):
    seqs, blocks, length, _ = operands[0].shape

    def block(width):
        return pl.BlockSpec((1, blocks, length, width), lambda i, own_ref: (i, 0, 0, 0))

    return pl.pallas_call(
        kernel,
        out_shape=jax.ShapeDtypeStruct((seqs, blocks, length, out_width), bf16),
        grid_spec=pltpu.PrefetchScalarGridSpec(
            num_scalar_prefetch=1,
            grid=(seqs,),
            in_specs=[block(v.shape[-1]) for v in operands],
            out_specs=block(out_width),
            scratch_shapes=[pltpu.VMEM((blocks * length, HEAD_DIM), kind) for kind in scratch],
        ),
        compiler_params=pltpu.CompilerParams(vmem_limit_bytes=40 * 2**20),
        cost_estimate=pl.CostEstimate(flops=flops, bytes_accessed=sum(v.size * 2 for v in operands), transcendentals=0),
    )(own.reshape(1), *operands)


def on_device(
    inputs,
    cotangent,
    norm1_gain,
    norm1_bias,
    w_qkv,
    query_bias,
    value_bias,
    w_attn_out,
    attn_out_bias,
    norm2_gain,
    norm2_bias,
    w_hidden,
    hidden_bias,
    w_output,
    output_bias,
):
    S, Z, R = lax.axis_size("seq"), lax.axis_size("shard"), lax.axis_size("replica")
    s, z, r = lax.axis_index("seq"), lax.axis_index("shard"), lax.axis_index("replica")
    odd = r != 0
    _, n, D = inputs.shape
    rows = norm1_gain.shape[0]
    F = hidden_bias.shape[0] * S * Z
    T = S * R
    hw = D // T
    fw = F // T
    fr = fw // Z
    heads = hw // HEAD_DIM

    def by_shard(v):
        return v.reshape(-1, S, Z, rows).swapaxes(1, 2).reshape(-1, D)

    def by_seq(v):
        return v.reshape(-1, Z, S, rows).swapaxes(1, 2).reshape(-1, D)

    small = (norm1_gain, norm1_bias, query_bias, value_bias, attn_out_bias, norm2_gain, norm2_bias, output_bias, hidden_bias)
    table = gather_table(jnp.concatenate([v.astype(bf16) for v in small])).astype(fp32)
    gain_one, shift_one, query_shift, value_shift, attn_shift, gain_two, shift_two, output_shift = (
        table[:, i * rows : (i + 1) * rows].reshape(D) for i in range(8)
    )
    hidden_shift = lax.dynamic_index_in_dim(
        lax.dynamic_index_in_dim(table[:, 8 * rows :].reshape(S, Z, R, fr), s, 0, keepdims=False), r, 1, keepdims=False
    ).reshape(fw)

    t = s * R + r
    qkv_pieces = lax.dynamic_index_in_dim(w_qkv.astype(bf16).reshape(rows, 3, S, R, hw), r, 3, keepdims=False)
    qkv_matrix = seq_exchange(qkv_pieces.transpose(2, 0, 1, 3).reshape(S, rows, 3 * hw))
    qkv_matrix = line_gather(qkv_matrix.reshape(S * rows, 3 * hw)).reshape(D, 3 * hw)
    attn_part = lax.dynamic_index_in_dim(w_attn_out.astype(bf16).reshape(rows, R, D // R), r, 1, keepdims=False)
    attn_part = plane_gather(line_gather(attn_part).reshape(D // S, D // R))
    attn_matrix = jnp.concatenate([jnp.concatenate(attn_part[:2]), jnp.concatenate(attn_part[2:])], axis=1)
    hidden_pieces = lax.dynamic_index_in_dim(w_hidden.astype(bf16).reshape(rows, S, Z, R, fr), r, 3, keepdims=False)
    hidden_matrix = seq_exchange(hidden_pieces.transpose(1, 0, 2, 3).reshape(S, rows, fw))
    hidden_matrix = line_gather(hidden_matrix.reshape(S * rows, fw)).reshape(D, fw)
    output_part = lax.dynamic_index_in_dim(w_output.astype(bf16).reshape(R, fr, D), r, 0, keepdims=False)
    output_matrix = line_gather(output_part).reshape(fw, D)

    flat_in = inputs.reshape(n, D).astype(fp32)
    normed_one, inverse_one = normalize(flat_in)
    hidden_in = (normed_one * gain_one + shift_one).astype(bf16)
    hidden_in_parts = plane_gather(by_shard(hidden_in))
    grad_low = cotangent.reshape(n, D)
    grad_low_parts = plane_gather(grad_low)
    bias_row = jnp.concatenate(
        [
            lax.dynamic_slice_in_dim(query_shift, t * hw, hw),
            jnp.zeros((hw,), fp32),
            lax.dynamic_slice_in_dim(value_shift, t * hw, hw),
        ]
    )
    qkv_parts = [
        (jnp.dot(v, qkv_matrix, preferred_element_type=fp32) + bias_row).astype(bf16) for v in hidden_in_parts
    ]
    qkv = jnp.concatenate(qkv_parts).reshape(R, S, n, 3 * hw)
    half_pairs = R * heads * (S * (S + 1) // 2) * n * n * HEAD_DIM * 2
    attended_heads = attention_call(
        lambda *refs: attend_kernel(heads, *refs), s, (qkv,), hw, (bf16, bf16), 2 * half_pairs
    )
    att = [[hop(attended_heads[jr, js], js, jr) for jr in range(R)] for js in range(S)]
    attended = jnp.concatenate(
        [jnp.where(odd, att[js][1 - i], att[js][i]) for js in range(S) for i in range(R)], axis=1
    )

    def swap_halves(v):
        first, second = v[:, : D // R], v[:, D // R :]
        return jnp.concatenate([jnp.where(odd, second, first), jnp.where(odd, first, second)], axis=1)

    mid_rows = flat_in + (
        swap_halves(jnp.dot(attended, attn_matrix, preferred_element_type=fp32)) + attn_shift
    )

    normed_two, inverse_two = normalize(mid_rows)
    hidden_two = (normed_two * gain_two + shift_two).astype(bf16)
    hidden_two_parts = plane_gather(by_shard(hidden_two))
    activated_parts, grad_pre_parts, grad_hidden_two_parts, out_parts = [], [], [], []
    for h2, g in zip(hidden_two_parts, grad_low_parts):
        preactive = jnp.dot(h2, hidden_matrix, preferred_element_type=fp32) + hidden_shift
        grad_activated = lax.dot_general(g, output_matrix, (((1,), (1,)), ((), ())), preferred_element_type=fp32)
        grad_pre = (grad_activated * gelu_slope(preactive)).astype(bf16)
        grad_hidden_two_parts.append(
            lax.dot_general(grad_pre, hidden_matrix, (((1,), (1,)), ((), ())), preferred_element_type=fp32).astype(bf16)
        )
        activated = jax.nn.gelu(preactive, approximate=False).astype(bf16)
        activated_parts.append(activated)
        grad_pre_parts.append(grad_pre)
    for activated in activated_parts:
        out_parts.append(jnp.dot(activated, output_matrix, preferred_element_type=fp32).astype(bf16))
    grad_hidden_two = by_seq(plane_scatter(grad_hidden_two_parts))
    out_rows = mid_rows + (plane_scatter(out_parts) + output_shift)
    layer_out = out_rows.astype(bf16).reshape(inputs.shape)

    down = (((0,), (0,)), ((), ()))
    grad_pre_all = jnp.concatenate(grad_pre_parts)
    grad_output = lax.dot_general(
        jnp.concatenate(activated_parts), jnp.concatenate(grad_low_parts), down, preferred_element_type=fp32
    ).astype(bf16)
    grad_output = line_scatter(grad_output.reshape(Z, fr, D)).astype(bf16)
    other = flip(grad_output, COL)
    grad_output_matrix = jnp.concatenate(
        [jnp.where(odd, other, grad_output), jnp.where(odd, grad_output, other)]
    ).astype(fp32)

    def to_rows(v, width):
        v = line_scatter(v.reshape(Z, S, rows, width)).astype(bf16)
        v = seq_exchange(v)
        other = flip(v, COL)
        return jnp.stack([jnp.where(odd, other, v), jnp.where(odd, v, other)])

    grad_hidden = lax.dot_general(
        jnp.concatenate(hidden_two_parts), grad_pre_all, down, preferred_element_type=fp32
    ).astype(bf16)
    grad_hidden_matrix = (
        to_rows(grad_hidden, fw).reshape(R, S, rows, Z, fr).transpose(2, 1, 3, 0, 4).reshape(rows, F).astype(fp32)
    )

    grad_out = grad_low.astype(fp32)
    grad_mid = grad_out + norm_back(grad_hidden_two * gain_two, normed_two, inverse_two)
    grad_mid_low = grad_mid.astype(bf16)
    grad_mid_swapped = swap_halves(grad_mid_low)
    grad_attended = lax.dot_general(
        grad_mid_swapped, attn_matrix, (((1,), (1,)), ((), ())), preferred_element_type=fp32
    ).astype(bf16)
    grad_attended = grad_attended.reshape(n, S, R, hw)
    sent = [
        [jnp.where(odd, grad_attended[:, js, 1 - jr], grad_attended[:, js, jr]) for js in range(S)] for jr in range(R)
    ]
    grad_heads = jnp.stack([jnp.stack([hop(sent[jr][js], js, jr) for js in range(S)]) for jr in range(R)])
    grad_qkv = attention_call(
        lambda *refs: attend_back_kernel(heads, *refs),
        s,
        (qkv, grad_heads),
        3 * hw,
        (bf16, bf16, fp32, fp32),
        5 * half_pairs,
    )
    pairs = grad_qkv.reshape(2 * R, 2 * n, 3 * hw)
    grad_hidden_in = by_seq(
        plane_scatter(
            [
                lax.dot_general(pairs[i], qkv_matrix, (((1,), (1,)), ((), ())), preferred_element_type=fp32).astype(bf16)
                for i in range(2 * R)
            ]
        )
    )
    grad_qkv = grad_qkv.reshape(T * n, 3 * hw)
    grad_qkv_cols = lax.dot_general(
        jnp.concatenate(hidden_in_parts), grad_qkv, down, preferred_element_type=fp32
    ).astype(bf16)
    grad_qkv_matrix = (
        to_rows(grad_qkv_cols, 3 * hw)
        .reshape(R, S, rows, 3, hw)
        .transpose(2, 3, 1, 0, 4)
        .reshape(rows, 3 * D)
        .astype(fp32)
    )
    grad_attn = lax.dot_general(attended, grad_mid_swapped, down, preferred_element_type=fp32).astype(bf16)
    top, bot = slice(0, D // 2), slice(D // 2, D)
    left, right = slice(0, D // R), slice(D // R, D)
    grad_attn = plane_scatter([grad_attn[top, left], grad_attn[bot, left], grad_attn[top, right], grad_attn[bot, right]])
    grad_attn = line_scatter(grad_attn.astype(bf16).reshape(Z, rows, D // R)).astype(bf16)
    other = flip(grad_attn, COL)
    grad_attn_matrix = jnp.concatenate(
        [jnp.where(odd, other, grad_attn), jnp.where(odd, grad_attn, other)], axis=1
    ).astype(fp32)
    grad_input_rows = grad_mid + norm_back(grad_hidden_in * gain_one, normed_one, inverse_one)
    grad_input_out = grad_input_rows.reshape(inputs.shape)

    hidden_sums = column_sums(grad_pre_all).reshape(1, Z, 1, fr)
    hidden_sums = lax.dynamic_update_slice(jnp.zeros((S, Z, R, fr), fp32), hidden_sums, (s, 0, r, 0))
    early = total(
        jnp.concatenate(
            [
                jnp.sum(grad_hidden_two * normed_two, axis=0).reshape(S * Z, rows),
                jnp.sum(grad_hidden_two, axis=0).reshape(S * Z, rows),
                column_sums(grad_mid_low).reshape(S * Z, rows),
                column_sums(grad_low).reshape(S * Z, rows),
                hidden_sums.reshape(S * Z, R * fr),
            ],
            axis=1,
        )
    )
    qkv_sums = column_sums(grad_qkv)
    none = jnp.zeros((D,), fp32)
    late = total(
        jnp.concatenate(
            [
                jnp.sum(grad_hidden_in * normed_one, axis=0).reshape(S * Z, rows),
                jnp.sum(grad_hidden_in, axis=0).reshape(S * Z, rows),
                lax.dynamic_update_slice_in_dim(none, qkv_sums[:hw], t * hw, 0).reshape(S * Z, rows),
                lax.dynamic_update_slice_in_dim(none, qkv_sums[2 * hw :], t * hw, 0).reshape(S * Z, rows),
            ],
            axis=1,
        )
    )
    early = lax.dynamic_index_in_dim(early, s * Z + z, 0, keepdims=False)
    late = lax.dynamic_index_in_dim(late, s * Z + z, 0, keepdims=False)

    def part(v, i):
        return v[i * rows : (i + 1) * rows]

    return (
        layer_out,
        grad_input_out,
        part(late, 0),
        part(late, 1),
        grad_qkv_matrix,
        part(late, 2),
        part(late, 3),
        grad_attn_matrix,
        part(early, 2),
        part(early, 0),
        part(early, 1),
        grad_hidden_matrix,
        early[4 * rows :],
        grad_output_matrix,
        part(early, 3),
    )


def solution(mesh):
    tokens = P(("shard", "replica"), "seq", None)
    vector = P(("seq", "shard"))
    matrix = P(("seq", "shard"), None)
    weights = (
        vector,
        vector,
        matrix,
        vector,
        vector,
        matrix,
        vector,
        vector,
        vector,
        matrix,
        vector,
        matrix,
        vector,
    )
    return jax.shard_map(
        on_device,
        mesh=mesh,
        in_specs=(tokens, tokens) + weights,
        out_specs=(tokens, tokens) + weights,
        check_vma=False,
    )
```

```python
import jax
import jax.numpy as jnp
from jax import lax
from jax.experimental import pallas as pl
from jax.experimental.pallas import tpu as pltpu
from jax.sharding import PartitionSpec as P

HEAD_DIM = 128
bf16 = jnp.bfloat16
fp32 = jnp.float32

CORE = ("seq", 1)
ROW = ("seq", 2)
COL = ("replica", 1)


PARTS = ((0, 2, 4), (1, 3, 5), (6,), (7,))
ACROSS = (((1,), (1,)), ((), ()))
DOWN = (((0,), (0,)), ((), ()))
WHOLE = pl.BlockSpec(memory_space=pltpu.VMEM)
SCALARS = pl.BlockSpec(memory_space=pltpu.SMEM)


def place(j):
    return next((i, part.index(j)) for i, part in enumerate(PARTS) if j in part)


def gelu_slope(values):
    normal_cdf = 0.5 * (1.0 + lax.erf(values * 0.7071067811865476))
    return normal_cdf + values * jnp.exp(-0.5 * values * values) * 0.3989422804014327


def after(v, *others):
    return lax.optimization_barrier((v, others))[0]


def flip(v, link):
    axis, bit = link
    return lax.ppermute(v, axis, [(i, i ^ bit) for i in range(lax.axis_size(axis))])


def plane_gather(v):
    h = v.shape[0] // 2
    py, px = flip(v, ROW), flip(v, COL)
    first = jnp.concatenate([v, py, px])
    da, db = flip(py[:h], COL), flip(px[h:], ROW)
    second = jnp.concatenate([da, db])
    return first, flip(first, CORE), second, flip(second, CORE)


def relay_kernel(y_ref, gy_ref, x_ref, gx_ref, ra_ref, rb_ref, ys_ref, xs_ref):
    h = ra_ref.shape[0]
    top, bot = slice(0, h), slice(h, 2 * h)
    ys_ref[top, :] = (
        y_ref[top, :].astype(fp32) + gy_ref[top, :].astype(fp32) + ra_ref[...].astype(fp32)
    ).astype(bf16)
    ys_ref[bot, :] = (y_ref[bot, :].astype(fp32) + gy_ref[bot, :].astype(fp32)).astype(bf16)
    xs_ref[top, :] = (x_ref[top, :].astype(fp32) + gx_ref[top, :].astype(fp32)).astype(bf16)
    xs_ref[bot, :] = (
        x_ref[bot, :].astype(fp32) + gx_ref[bot, :].astype(fp32) + rb_ref[...].astype(fp32)
    ).astype(bf16)


def plane_scatter(parts):
    mine, theirs, far, far_theirs = parts
    n, width = far.shape
    h = n // 2
    far_got = flip(far_theirs, CORE)
    got = flip(theirs, CORE)
    far = (far.astype(fp32) + far_got.astype(fp32)).astype(bf16)
    ra, rb = flip(far[:h], COL), flip(far[h:], ROW)

    def rows(i):
        return pl.BlockSpec((n, width), lambda g: (i, 0))

    half = pl.BlockSpec((h, width), lambda g: (0, 0))
    y_send, x_send = pl.pallas_call(
        relay_kernel,
        grid=(1,),
        in_specs=[rows(1), rows(1), rows(2), rows(2), half, half],
        out_specs=[rows(0), rows(0)],
        out_shape=[jax.ShapeDtypeStruct((n, width), bf16)] * 2,
        compiler_params=pltpu.CompilerParams(vmem_limit_bytes=40 * 2**20),
        cost_estimate=pl.CostEstimate(flops=6 * n * width, bytes_accessed=14 * n * width, transcendentals=0),
    )(mine, got, mine, got, ra, rb)
    return mine, got, flip(y_send, ROW), flip(x_send, COL)


def line_gather(v):
    return lax.all_gather(v, "shard", axis=0, tiled=True)


def line_scatter(v):
    return lax.psum_scatter(v, "shard", scatter_dimension=0, tiled=True)


def in_order(pieces, index):
    bit = 1
    while bit < len(pieces):
        odd = (index & bit) != 0
        pieces = [jnp.where(odd, pieces[j ^ bit], pieces[j]) for j in range(len(pieces))]
        bit *= 2
    return jnp.stack(pieces)


def seq_exchange(v):
    S, s = lax.axis_size("seq"), lax.axis_index("seq")
    pieces = [lax.dynamic_index_in_dim(v, s ^ j, 0, keepdims=False) for j in range(S)]
    got = [flip(v, ("seq", j)) if j else v for j, v in enumerate(pieces)]
    return in_order(got, s)


def gather_table(v):
    table = v[None]
    for axis in ("shard", "seq"):
        index, bit = lax.axis_index(axis), 1
        while bit < lax.axis_size(axis):
            other = flip(table, (axis, bit))
            odd = (index & bit) != 0
            table = jnp.concatenate([jnp.where(odd, other, table), jnp.where(odd, table, other)])
            bit *= 2
    return table


def total(v):
    for axis in ("seq", "replica", "shard"):
        bit = 1
        while bit < lax.axis_size(axis):
            v = v + flip(v, (axis, bit))
            bit *= 2
    return v


def row_loop(n):
    step = 32 if n % 32 == 0 else n
    return pl.loop(0, n, step=step), step


def statistics(v):
    centred = v - jnp.mean(v, axis=1, keepdims=True)
    scale = lax.rsqrt(jnp.mean(centred * centred, axis=1, keepdims=True) + 1e-05)
    return centred * scale, scale


def norm_back(grad, normed, scale):
    first = jnp.mean(grad, axis=1, keepdims=True)
    second = jnp.mean(grad * normed, axis=1, keepdims=True)
    return scale * (grad - first - normed * second)


def transposed_columns(v, grid, rows):
    a, b = grid
    if rows % 128 or a == 1 or b == 1:
        return v
    return jnp.concatenate(
        [v[:, (i * b + k) * rows : (i * b + k + 1) * rows] for k in range(b) for i in range(a)], axis=1
    )


def norm_kernel(grid, rows, x_ref, gain_ref, shift_ref, out_ref):
    loop, step = row_loop(x_ref.shape[0])

    @loop
    def _(i):
        at = pl.ds(pl.multiple_of(i, step), step)
        normed, _ = statistics(x_ref[at, :].astype(fp32))
        hidden = (normed * gain_ref[...] + shift_ref[...]).astype(bf16)
        out_ref[at, :] = transposed_columns(hidden, grid, rows)


def mid_kernel(
    grid, rows, own_ref, att_ref, a_ref, b_ref, c_ref, d_ref, x_ref, bias_ref, gain_ref, shift_ref,
    mid_ref, hidden_ref, rel_ref,
):
    S = grid[0]
    T, n, hw = att_ref.shape
    R = T // S
    s, r = own_ref[0], own_ref[1]
    parts = (a_ref, b_ref, c_ref, d_ref)
    deep, wide = d_ref.shape
    for js in range(S):
        for i in range(R):
            rel_ref[:, (js * R + i) * hw : (js * R + i + 1) * hw] = att_ref[(s ^ js) * R + i]
    for jr in range(R):
        acc = jnp.zeros((n, wide), fp32)
        for js in range(S):
            part, k = place(js + 4 * jr)
            acc += jnp.dot(
                rel_ref[:, js * deep : (js + 1) * deep],
                parts[part][k * deep : (k + 1) * deep, :],
                preferred_element_type=fp32,
            )
        mid_ref[:, pl.ds(pl.multiple_of((r ^ jr) * wide, 128), wide)] = acc
    loop, step = row_loop(n)

    @loop
    def _(i):
        at = pl.ds(pl.multiple_of(i, step), step)
        mid = x_ref[at, :].astype(fp32) + (mid_ref[at, :] + bias_ref[...])
        mid_ref[at, :] = mid
        normed, _ = statistics(mid)
        hidden = (normed * gain_ref[...] + shift_ref[...]).astype(bf16)
        hidden_ref[at, :] = transposed_columns(hidden, grid, rows)


def back_mid_kernel(
    grid, rows, own_ref, p_ref, q_ref, u_ref, w_ref, mid_ref, g_ref, gain_ref, a_ref, b_ref, c_ref, d_ref,
    grad_ref, rel_ref, att_ref, sums_ref,
):
    S = grid[0]
    T, n, hw = att_ref.shape
    R = T // S
    s, r = own_ref[0], own_ref[1]
    parts = (a_ref, b_ref, c_ref, d_ref)
    deep, wide = d_ref.shape
    sums_ref[...] = jnp.zeros_like(sums_ref)
    loop, step = row_loop(n)

    @loop
    def _(i):
        at = pl.ds(pl.multiple_of(i, step), step)
        grad = p_ref[at, :].astype(fp32) + q_ref[at, :].astype(fp32)
        grad += u_ref[at, :].astype(fp32) + w_ref[at, :].astype(fp32)
        grad = transposed_columns(grad, grid[::-1], rows)
        normed, scale = statistics(mid_ref[at, :])
        g = g_ref[at, :].astype(fp32)
        sums_ref[0:1, :] += jnp.sum(grad * normed, axis=0, keepdims=True)
        sums_ref[1:2, :] += jnp.sum(grad, axis=0, keepdims=True)
        grad_mid = g + norm_back(grad * gain_ref[...], normed, scale)
        grad_ref[at, :] = grad_mid
        low = grad_mid.astype(bf16)
        sums_ref[2:3, :] += jnp.sum(low.astype(fp32), axis=0, keepdims=True)
        sums_ref[3:4, :] += jnp.sum(g, axis=0, keepdims=True)
        for k in range(R):
            rel_ref[at, pl.ds(pl.multiple_of((r ^ k) * wide, 128), wide)] = low[:, k * wide : (k + 1) * wide]

    for js in range(S):
        acc = jnp.zeros((n, deep), fp32)
        for jr in range(R):
            part, k = place(js + 4 * jr)
            acc += lax.dot_general(
                rel_ref[:, jr * wide : (jr + 1) * wide],
                parts[part][k * deep : (k + 1) * deep, :],
                ACROSS,
                preferred_element_type=fp32,
            )
        for i in range(R):
            att_ref[(s ^ js) * R + i] = acc[:, i * hw : (i + 1) * hw].astype(bf16)


def back_in_kernel(grid, rows, p_ref, q_ref, u_ref, w_ref, x_ref, g_ref, gain_ref, out_ref, sums_ref):
    sums_ref[...] = jnp.zeros_like(sums_ref)
    loop, step = row_loop(x_ref.shape[0])

    @loop
    def _(i):
        at = pl.ds(pl.multiple_of(i, step), step)
        grad = p_ref[at, :].astype(fp32) + q_ref[at, :].astype(fp32)
        grad += u_ref[at, :].astype(fp32) + w_ref[at, :].astype(fp32)
        grad = transposed_columns(grad, grid[::-1], rows)
        normed, scale = statistics(x_ref[at, :].astype(fp32))
        sums_ref[0:1, :] += jnp.sum(grad * normed, axis=0, keepdims=True)
        sums_ref[1:2, :] += jnp.sum(grad, axis=0, keepdims=True)
        out_ref[at, :] = g_ref[at, :] + norm_back(grad * gain_ref[...], normed, scale)


def out_kernel(p_ref, q_ref, u_ref, w_ref, mid_ref, bias_ref, out_ref):
    loop, step = row_loop(mid_ref.shape[0])

    @loop
    def _(i):
        at = pl.ds(pl.multiple_of(i, step), step)
        term = p_ref[at, :].astype(fp32) + q_ref[at, :].astype(fp32)
        term += u_ref[at, :].astype(fp32) + w_ref[at, :].astype(fp32)
        out_ref[at, :] = (mid_ref[at, :] + (term + bias_ref[...])).astype(bf16)


def outer_kernel(rel_ref, low_ref, *outs):
    deep, wide = outs[3].shape
    for out_ref, part in zip(outs, PARTS):
        for k, j in enumerate(part):
            js, jr = j & 3, j >> 2
            out_ref[k * deep : (k + 1) * deep, :] = lax.dot_general(
                rel_ref[:, js * deep : (js + 1) * deep],
                low_ref[:, jr * wide : (jr + 1) * wide],
                DOWN,
                preferred_element_type=fp32,
            ).astype(bf16)


def tall_kernel(*refs):
    half = len(refs) // 2
    acc = 0.0
    for left, right in zip(refs[:half], refs[half:-1]):
        acc += lax.dot_general(left[...], right[...], DOWN, preferred_element_type=fp32)
    refs[-1][...] = acc.astype(bf16)


def tall_product(lefts, rights):
    deep, wide = lefts[0].shape[1], rights[0].shape[1]
    tokens = sum(v.shape[0] for v in lefts)
    tile = min(256, deep)
    return pl.pallas_call(
        tall_kernel,
        grid=(deep // tile,),
        in_specs=[pl.BlockSpec((v.shape[0], tile), lambda i: (0, i)) for v in lefts]
        + [pl.BlockSpec(v.shape, lambda i: (0, 0)) for v in rights],
        out_specs=pl.BlockSpec((tile, wide), lambda i: (i, 0)),
        out_shape=jax.ShapeDtypeStruct((deep, wide), bf16),
        compiler_params=pltpu.CompilerParams(vmem_limit_bytes=48 * 2**20),
        cost_estimate=pl.CostEstimate(
            flops=2 * tokens * deep * wide,
            bytes_accessed=2 * (tokens * (deep + wide) + deep * wide),
            transcendentals=0,
        ),
    )(*lefts, *rights)


def attend_kernel(heads, own_ref, a_ref, b_ref, c_ref, d_ref, out_ref, q_ref, k_ref, v_ref):
    s, r = own_ref[0], own_ref[1]
    T, n, width = out_ref.shape
    S = q_ref.shape[0] // n
    parts = (a_ref, b_ref, c_ref, d_ref)
    for jr in range(T // S):
        for h in range(heads):
            cols = slice(h * HEAD_DIM, (h + 1) * HEAD_DIM)
            for js in range(S):
                part, k = place(js + 4 * jr)
                at = pl.ds(pl.multiple_of((s ^ js) * n, n), n)
                for i, ref in enumerate((q_ref, k_ref, v_ref)):
                    first = i * width + h * HEAD_DIM
                    ref[at, :] = parts[part][k * n : (k + 1) * n, first : first + HEAD_DIM]
            for a in range(S):
                upto = (a + 1) * n
                q = q_ref[a * n : upto, :]
                scores = lax.dot_general(q, k_ref[:upto, :], ACROSS, preferred_element_type=fp32)
                scores = scores * HEAD_DIM ** (-0.5)
                expons = jnp.exp(scores - jnp.max(scores, axis=-1, keepdims=True))
                probs = (expons / jnp.sum(expons, axis=-1, keepdims=True)).astype(bf16)
                out_ref[a * (T // S) + (r ^ jr), :, cols] = jnp.dot(
                    probs, v_ref[:upto, :], preferred_element_type=fp32
                ).astype(bf16)


def attend_back_kernel(
    heads, own_ref, a_ref, b_ref, c_ref, d_ref, grad_ref, oa_ref, ob_ref, oc_ref, od_ref, sums_ref,
    q_ref, k_ref, v_ref, gq_ref, gk_ref, gv_ref,
):
    s, r = own_ref[0], own_ref[1]
    T, n, width = grad_ref.shape
    S = q_ref.shape[0] // n
    parts = (a_ref, b_ref, c_ref, d_ref)
    outs = (oa_ref, ob_ref, oc_ref, od_ref)
    scaling = HEAD_DIM ** (-0.5)
    sums_ref[...] = jnp.zeros_like(sums_ref)
    for jr in range(T // S):
        for h in range(heads):
            cols = slice(h * HEAD_DIM, (h + 1) * HEAD_DIM)
            for js in range(S):
                part, k = place(js + 4 * jr)
                at = pl.ds(pl.multiple_of((s ^ js) * n, n), n)
                for i, ref in enumerate((q_ref, k_ref, v_ref)):
                    first = i * width + h * HEAD_DIM
                    ref[at, :] = parts[part][k * n : (k + 1) * n, first : first + HEAD_DIM]
            for a in reversed(range(S)):
                upto = (a + 1) * n
                q = q_ref[a * n : upto, :]
                g = grad_ref[a * (T // S) + (r ^ jr), :, cols]
                k = k_ref[:upto, :]
                v = v_ref[:upto, :]
                scores = lax.dot_general(q, k, ACROSS, preferred_element_type=fp32) * scaling
                expons = jnp.exp(scores - jnp.max(scores, axis=-1, keepdims=True))
                probs = expons / jnp.sum(expons, axis=-1, keepdims=True)
                grad_probs = lax.dot_general(g, v, ACROSS, preferred_element_type=fp32)
                inner = jnp.sum(probs * grad_probs, axis=-1, keepdims=True)
                grad_scores = (probs * (grad_probs - inner)).astype(bf16)
                gq_ref[a * n : upto, :] = jnp.dot(grad_scores, k, preferred_element_type=fp32)
                gk = lax.dot_general(grad_scores, q, DOWN, preferred_element_type=fp32)
                gv = lax.dot_general(probs.astype(bf16), g, DOWN, preferred_element_type=fp32)
                if a == S - 1:
                    gk_ref[...] = gk
                    gv_ref[...] = gv
                else:
                    gk_ref[:upto, :] += gk
                    gv_ref[:upto, :] += gv
            for js in range(S):
                part, k = place(js + 4 * jr)
                at = pl.ds(pl.multiple_of((s ^ js) * n, n), n)
                for i, (ref, factor) in enumerate(((gq_ref, scaling), (gk_ref, scaling), (gv_ref, 1.0))):
                    first = i * width + h * HEAD_DIM
                    low = (ref[at, :] * factor).astype(bf16)
                    outs[part][k * n : (k + 1) * n, first : first + HEAD_DIM] = low
                    sums_ref[0:1, first : first + HEAD_DIM] += jnp.sum(low.astype(fp32), axis=0, keepdims=True)


def small_call(kernel, out_shape, operands, scratch=(), flops=0, first_rows=()):
    specs = []
    for i, v in enumerate(operands):
        if v.dtype == jnp.int32:
            specs.append(SCALARS)
        elif dict(first_rows).get(i, v.shape[0]) != v.shape[0]:
            specs.append(pl.BlockSpec((dict(first_rows)[i], v.shape[1]), lambda g: (0, 0)))
        else:
            specs.append(pl.BlockSpec(v.shape, lambda g, rank=v.ndim: (0,) * rank))
    many = isinstance(out_shape, list)
    outs = out_shape if many else [out_shape]
    out_specs = [pl.BlockSpec(v.shape, lambda g, rank=len(v.shape): (0,) * rank) for v in outs]
    moved = sum(v.size * v.dtype.itemsize for v in operands) + sum(
        v.size * jnp.dtype(v.dtype).itemsize for v in outs
    )
    return pl.pallas_call(
        kernel,
        grid=(1,),
        in_specs=specs,
        out_specs=out_specs if many else out_specs[0],
        out_shape=out_shape,
        scratch_shapes=scratch,
        compiler_params=pltpu.CompilerParams(vmem_limit_bytes=56 * 2**20),
        cost_estimate=pl.CostEstimate(flops=flops, bytes_accessed=moved, transcendentals=0),
    )(*operands)


def on_device(
    inputs,
    cotangent,
    norm1_gain,
    norm1_bias,
    w_qkv,
    query_bias,
    value_bias,
    w_attn_out,
    attn_out_bias,
    norm2_gain,
    norm2_bias,
    w_hidden,
    hidden_bias,
    w_output,
    output_bias,
):
    S, Z, R = lax.axis_size("seq"), lax.axis_size("shard"), lax.axis_size("replica")
    s, z, r = lax.axis_index("seq"), lax.axis_index("shard"), lax.axis_index("replica")
    odd = r != 0
    _, n, D = inputs.shape
    rows = norm1_gain.shape[0]
    F = hidden_bias.shape[0] * S * Z
    T = S * R
    hw = D // T
    fw = F // T
    fr = fw // Z
    heads = hw // HEAD_DIM
    grid = (S, Z)
    own = jnp.stack([s, r]).astype(jnp.int32)

    def shape(*dims, kind=bf16):
        return jax.ShapeDtypeStruct(dims, kind)

    def by_shard(v):
        return v if rows % 128 == 0 else v.reshape(-1, S, Z, rows).swapaxes(1, 2).reshape(-1, D)

    def by_seq(v):
        return v if rows % 128 == 0 else v.reshape(-1, Z, S, rows).swapaxes(1, 2).reshape(-1, D)

    t = s * R + r
    attn_part = lax.dynamic_index_in_dim(w_attn_out.reshape(rows, R, D // R), r, 1, keepdims=False).astype(bf16)
    attn_part = line_gather(attn_part)
    qkv_pieces = lax.dynamic_index_in_dim(w_qkv.reshape(rows, 3, S, R, hw), r, 3, keepdims=False).astype(bf16)
    qkv_rows = seq_exchange(qkv_pieces.transpose(2, 0, 1, 3).reshape(S, rows, 3 * hw)).reshape(S * rows, 3 * hw)
    qkv_matrix = line_gather(qkv_rows)
    hidden_pieces = lax.dynamic_index_in_dim(w_hidden.reshape(rows, S, Z, R, fr), r, 3, keepdims=False).astype(bf16)
    hidden_pieces = after(hidden_pieces.transpose(1, 0, 2, 3).reshape(S, rows, fw), qkv_rows)
    hidden_rows = seq_exchange(hidden_pieces).reshape(S * rows, fw)
    hidden_matrix = line_gather(hidden_rows)
    output_part = lax.dynamic_index_in_dim(w_output.reshape(R, fr, D), r, 0, keepdims=False).astype(bf16)
    output_matrix = line_gather(after(output_part, hidden_rows))

    small = (norm1_gain, norm1_bias, query_bias, value_bias, attn_out_bias, norm2_gain, norm2_bias, output_bias, hidden_bias)
    table = gather_table(jnp.concatenate([v.astype(bf16) for v in small])).astype(fp32)
    gain_one, shift_one, query_shift, value_shift, attn_shift, gain_two, shift_two, output_shift = (
        table[:, i * rows : (i + 1) * rows].reshape(1, D) for i in range(8)
    )
    hidden_shift = lax.dynamic_index_in_dim(
        lax.dynamic_index_in_dim(table[:, 8 * rows :].reshape(S, Z, R, fr), s, 0, keepdims=False), r, 1, keepdims=False
    ).reshape(fw)
    bias_row = jnp.concatenate(
        [
            lax.dynamic_slice_in_dim(query_shift[0], t * hw, hw),
            jnp.zeros((hw,), fp32),
            lax.dynamic_slice_in_dim(value_shift[0], t * hw, hw),
        ]
    )

    x = inputs.reshape(n, D)
    g_low = cotangent.reshape(n, D)
    hidden_in = small_call(
        lambda *refs: norm_kernel(grid, rows, *refs), shape(n, D), (x, gain_one, shift_one), flops=10 * n * D
    )
    hidden_in_parts = plane_gather(by_shard(hidden_in))
    attn_parts = plane_gather(after(attn_part, hidden_in_parts[2]))
    qkv_parts = [
        (jnp.dot(v, qkv_matrix, preferred_element_type=fp32) + bias_row).astype(bf16) for v in hidden_in_parts
    ]
    half_pairs = R * heads * (S * (S + 1) // 2) * n * n * HEAD_DIM * 2
    head_block = pltpu.VMEM((S * n, HEAD_DIM), bf16)
    head_sums = pltpu.VMEM((S * n, HEAD_DIM), fp32)
    attended = small_call(
        lambda *refs: attend_kernel(heads, *refs),
        shape(T, n, hw),
        (own, *qkv_parts),
        [head_block] * 3,
        flops=2 * half_pairs,
    )
    attended = lax.all_to_all(attended, ("seq", "replica"), 0, 0, tiled=True)
    mid_rows, hidden_two, attended_rel = small_call(
        lambda *refs: mid_kernel(grid, rows, *refs),
        [shape(n, D, kind=fp32), shape(n, D), shape(n, D)],
        (own, attended, *attn_parts, x, attn_shift, gain_two, shift_two),
        flops=2 * n * D * D,
    )

    hidden_two_parts = plane_gather(by_shard(hidden_two))
    g_parts = plane_gather(after(g_low, hidden_two_parts[2]))
    activated_parts, grad_pre_parts, grad_two_parts = [], [], []
    for h2, g in zip(hidden_two_parts, g_parts):
        preactive = jnp.dot(h2, hidden_matrix, preferred_element_type=fp32) + hidden_shift
        activated_parts.append(jax.nn.gelu(preactive, approximate=False).astype(bf16))
        grad_activated = lax.dot_general(g, output_matrix, ACROSS, preferred_element_type=fp32)
        grad_pre = (grad_activated * gelu_slope(preactive)).astype(bf16)
        grad_pre_parts.append(grad_pre)
        grad_two_parts.append(
            lax.dot_general(grad_pre, hidden_matrix, ACROSS, preferred_element_type=fp32).astype(bf16)
        )
    grad_output = line_scatter(tall_product(activated_parts, g_parts))
    grad_two = plane_scatter(grad_two_parts)
    grad_hidden = line_scatter(tall_product(hidden_two_parts, grad_pre_parts))

    first = ((1, n), (2, n))
    grad_mid, grad_mid_rel, grad_heads, sums_two = small_call(
        lambda *refs: back_mid_kernel(grid, rows, *refs),
        [shape(n, D, kind=fp32), shape(n, D), shape(T, n, hw), shape(8, D, kind=fp32)],
        (own, *map(by_seq, grad_two), mid_rows, g_low, gain_two, *attn_parts),
        flops=2 * n * D * D,
        first_rows=first,
    )
    grad_heads = lax.all_to_all(grad_heads, ("seq", "replica"), 0, 0, tiled=True)
    *grad_qkv_parts, sums_qkv = small_call(
        lambda *refs: attend_back_kernel(heads, *refs),
        [shape(v.shape[0], 3 * hw) for v in qkv_parts] + [shape(8, 3 * hw, kind=fp32)],
        (own, *qkv_parts, grad_heads),
        [head_block] * 3 + [head_sums] * 3,
        flops=5 * half_pairs,
    )
    grad_attn_parts = small_call(
        outer_kernel,
        [shape(*v.shape) for v in attn_parts],
        (after(attended_rel, grad_heads), grad_mid_rel),
        flops=2 * n * D * D,
    )
    grad_attn = plane_scatter(grad_attn_parts)
    grad_in_parts = [
        lax.dot_general(v, qkv_matrix, ACROSS, preferred_element_type=fp32).astype(bf16) for v in grad_qkv_parts
    ]
    grad_qkv = line_scatter(tall_product(hidden_in_parts, grad_qkv_parts)).reshape(S, rows, 3 * hw)
    grad_in = plane_scatter(grad_in_parts)
    grad_inputs, sums_one = small_call(
        lambda *refs: back_in_kernel(grid, rows, *refs),
        [shape(n, D, kind=fp32), shape(8, D, kind=fp32)],
        (*map(by_seq, grad_in), x, grad_mid, gain_one),
        flops=20 * n * D,
        first_rows=((0, n), (1, n)),
    )

    out_parts = [
        jnp.dot(after(v, grad_qkv_parts[3]), output_matrix, preferred_element_type=fp32).astype(bf16)
        for v in activated_parts
    ]
    layer_out = small_call(
        out_kernel,
        shape(n, D),
        (*plane_scatter(out_parts), mid_rows, output_shift),
        flops=6 * n * D,
        first_rows=((0, n), (1, n)),
    )

    def both(v):
        other = flip(v, COL)
        return jnp.where(odd, other, v), jnp.where(odd, v, other)

    grad_output_matrix = jnp.concatenate(both(grad_output)).astype(fp32)
    grad_hidden = jnp.stack(both(seq_exchange(grad_hidden.reshape(S, rows, fw)))).reshape(R, S, rows, Z, fr)
    grad_hidden_matrix = grad_hidden.transpose(2, 1, 3, 0, 4).reshape(rows, F).astype(fp32)
    grad_qkv = jnp.stack(both(seq_exchange(grad_qkv))).reshape(R, S, rows, 3, hw)
    grad_qkv_matrix = grad_qkv.transpose(2, 3, 1, 0, 4).reshape(rows, 3 * D).astype(fp32)
    deep = D // S
    p, q, u, w = (v[:deep].astype(fp32) for v in grad_attn)
    grad_attn = line_scatter((p + q + u + w).astype(bf16))
    grad_attn_matrix = jnp.concatenate(both(grad_attn), axis=1).astype(fp32)

    hidden_sums = sum(jnp.sum(v.astype(fp32), axis=0) for v in grad_pre_parts).reshape(1, Z, 1, fr)
    hidden_sums = lax.dynamic_update_slice(jnp.zeros((S, Z, R, fr), fp32), hidden_sums, (s, 0, r, 0))
    none = jnp.zeros((D,), fp32)
    sums = total(
        jnp.concatenate(
            [sums_one[i].reshape(S * Z, rows) for i in range(2)]
            + [
                lax.dynamic_update_slice_in_dim(none, sums_qkv[0, i * hw : (i + 1) * hw], t * hw, 0).reshape(S * Z, rows)
                for i in (0, 2)
            ]
            + [sums_two[i].reshape(S * Z, rows) for i in range(4)]
            + [hidden_sums.reshape(S * Z, R * fr)],
            axis=1,
        )
    )
    sums = lax.dynamic_index_in_dim(sums, s * Z + z, 0, keepdims=False)

    def part(i):
        return sums[i * rows : (i + 1) * rows]

    return (
        layer_out.reshape(inputs.shape),
        grad_inputs.reshape(inputs.shape),
        part(0),
        part(1),
        grad_qkv_matrix,
        part(2),
        part(3),
        grad_attn_matrix,
        part(6),
        part(4),
        part(5),
        grad_hidden_matrix,
        sums[8 * rows :],
        grad_output_matrix,
        part(7),
    )


def solution(mesh):
    tokens = P(("shard", "replica"), "seq", None)
    vector = P(("seq", "shard"))
    matrix = P(("seq", "shard"), None)
    weights = (
        vector,
        vector,
        matrix,
        vector,
        vector,
        matrix,
        vector,
        vector,
        vector,
        matrix,
        vector,
        matrix,
        vector,
    )
    return jax.shard_map(
        on_device,
        mesh=mesh,
        in_specs=(tokens, tokens) + weights,
        out_specs=(tokens, tokens) + weights,
        check_vma=False,
    )
```

```python
import jax
import jax.numpy as jnp
from jax import lax
from jax.experimental import pallas as pl
from jax.experimental.pallas import tpu as pltpu
from jax.sharding import PartitionSpec as P

HEAD_DIM = 128
bf16 = jnp.bfloat16
fp32 = jnp.float32

CORE = ("seq", 1)
ROW = ("seq", 2)
COL = ("replica", 1)


PARTS = ((0, 2, 4), (1, 3, 5), (6,), (7,))
ACROSS = (((1,), (1,)), ((), ()))
DOWN = (((0,), (0,)), ((), ()))
WHOLE = pl.BlockSpec(memory_space=pltpu.VMEM)
SCALARS = pl.BlockSpec(memory_space=pltpu.SMEM)


LIGHT = pl.CostEstimate(flops=1, bytes_accessed=1, transcendentals=0)


def place(j):
    return next((i, part.index(j)) for i, part in enumerate(PARTS) if j in part)


def tie(*groups):
    return lax.optimization_barrier(groups)


def ordered(kernel, count, deps):
    return lambda *refs: kernel(*refs[:count], *refs[count + len(deps) :])


UNREAD = pl.BlockSpec(memory_space=pl.ANY)


def flip(v, link):
    axis, bit = link
    return lax.ppermute(v, axis, [(i, i ^ bit) for i in range(lax.axis_size(axis))])


def gather_near(v):
    return v, flip(v, ROW), flip(v, COL)


def gather_diagonal(v, py, px):
    h = v.shape[0] // 2
    return flip(py[:h], COL), flip(px[h:], ROW)


def gather_parts(near, diagonal):
    first, second = jnp.concatenate(near), jnp.concatenate(diagonal)
    return first, flip(first, CORE), second, flip(second, CORE)


def relay_kernel(y_ref, gy_ref, x_ref, gx_ref, ra_ref, rb_ref, ys_ref, xs_ref):
    h = ra_ref.shape[0]
    top, bot = slice(0, h), slice(h, 2 * h)
    ys_ref[top, :] = (
        y_ref[top, :].astype(fp32) + gy_ref[top, :].astype(fp32) + ra_ref[...].astype(fp32)
    ).astype(bf16)
    ys_ref[bot, :] = (y_ref[bot, :].astype(fp32) + gy_ref[bot, :].astype(fp32)).astype(bf16)
    xs_ref[top, :] = (x_ref[top, :].astype(fp32) + gx_ref[top, :].astype(fp32)).astype(bf16)
    xs_ref[bot, :] = (
        x_ref[bot, :].astype(fp32) + gx_ref[bot, :].astype(fp32) + rb_ref[...].astype(fp32)
    ).astype(bf16)


def relay_by_row_kernel(y_ref, gy_ref, x_ref, gx_ref, rb_ref, ys_ref, xs_ref):
    ys_ref[...] = (y_ref[...].astype(fp32) + gy_ref[...].astype(fp32)).astype(bf16)
    xs_ref[...] = (x_ref[...].astype(fp32) + gx_ref[...].astype(fp32) + rb_ref[...].astype(fp32)).astype(bf16)


def far_sum(far, far_theirs):
    return (far.astype(fp32) + flip(far_theirs, CORE).astype(fp32)).astype(bf16)


def scatter_diagonal(far):
    h = far.shape[0] // 2
    return flip(far[:h], COL), flip(far[h:], ROW)


def scatter_diagonal_by_row(far):
    return (flip(far, ROW),)


def scatter_relay(mine, got, diagonal):
    width = diagonal[0].shape[1]
    n = sum(v.shape[0] for v in diagonal)

    def rows(i):
        return pl.BlockSpec((n, width), lambda g: (i, 0))

    diagonal_specs = [pl.BlockSpec(v.shape, lambda g: (0, 0)) for v in diagonal]
    y_send, x_send = pl.pallas_call(
        relay_kernel if len(diagonal) == 2 else relay_by_row_kernel,
        grid=(1,),
        in_specs=[rows(1), rows(1), rows(2), rows(2), *diagonal_specs],
        out_specs=[rows(0), rows(0)],
        out_shape=[jax.ShapeDtypeStruct((n, width), bf16)] * 2,
        compiler_params=pltpu.CompilerParams(vmem_limit_bytes=40 * 2**20),
        cost_estimate=LIGHT,
    )(mine, got, mine, got, *diagonal)
    return mine, got, y_send, x_send


def scatter_last(mine, got, y_send, x_send):
    return mine, got, flip(y_send, ROW), flip(x_send, COL)


def line_gather(v):
    return lax.all_gather(v, "shard", axis=0, tiled=True)


def line_scatter(v):
    return lax.psum_scatter(v, "shard", scatter_dimension=0, tiled=True)


def seq_exchange(v):
    return lax.all_to_all(v, "seq", 0, 0, tiled=True)


def gather_table(table, axis):
    index, bit = lax.axis_index(axis), 1
    while bit < lax.axis_size(axis):
        other = flip(table, (axis, bit))
        odd = (index & bit) != 0
        table = jnp.concatenate([jnp.where(odd, other, table), jnp.where(odd, table, other)])
        bit *= 2
    return table


def total(v):
    for axis in ("shard", "seq", "replica"):
        bit = 1
        while bit < lax.axis_size(axis):
            v = v + flip(v, (axis, bit))
            bit *= 2
    return v


def row_loop(n):
    step = 32 if n % 32 == 0 else n
    return pl.loop(0, n, step=step), step


def statistics(v):
    centred = v - jnp.mean(v, axis=1, keepdims=True)
    scale = lax.rsqrt(jnp.mean(centred * centred, axis=1, keepdims=True) + 1e-05)
    return centred * scale, scale


def norm_back(grad, normed, scale):
    first = jnp.mean(grad, axis=1, keepdims=True)
    second = jnp.mean(grad * normed, axis=1, keepdims=True)
    return scale * (grad - first - normed * second)


def transposed_columns(v, grid, rows):
    a, b = grid
    if rows % 128 or a == 1 or b == 1:
        return v
    return jnp.concatenate(
        [v[:, (i * b + k) * rows : (i * b + k + 1) * rows] for k in range(b) for i in range(a)], axis=1
    )


def norm_kernel(grid, rows, x_ref, gain_ref, shift_ref, out_ref):
    loop, step = row_loop(x_ref.shape[0])

    @loop
    def _(i):
        at = pl.ds(pl.multiple_of(i, step), step)
        normed, _ = statistics(x_ref[at, :].astype(fp32))
        hidden = (normed * gain_ref[...] + shift_ref[...]).astype(bf16)
        out_ref[at, :] = transposed_columns(hidden, grid, rows)


def mid_kernel(
    grid, rows, own_ref, att_ref, a_ref, b_ref, c_ref, d_ref, x_ref, bias_ref, gain_ref, shift_ref,
    mid_ref, hidden_ref, rel_ref,
):
    S = grid[0]
    T, n, hw = att_ref.shape
    R = T // S
    s, r = own_ref[0], own_ref[1]
    parts = (a_ref, b_ref, c_ref, d_ref)
    deep, wide = d_ref.shape
    for js in range(S):
        for i in range(R):
            rel_ref[:, (js * R + i) * hw : (js * R + i + 1) * hw] = att_ref[(s ^ js) * R + i]
    for jr in range(R):
        acc = jnp.zeros((n, wide), fp32)
        for js in range(S):
            part, k = place(js + 4 * jr)
            acc += jnp.dot(
                rel_ref[:, js * deep : (js + 1) * deep],
                parts[part][k * deep : (k + 1) * deep, :],
                preferred_element_type=fp32,
            )
        mid_ref[:, pl.ds(pl.multiple_of((r ^ jr) * wide, 128), wide)] = acc
    loop, step = row_loop(n)

    @loop
    def _(i):
        at = pl.ds(pl.multiple_of(i, step), step)
        mid = x_ref[at, :].astype(fp32) + (mid_ref[at, :] + bias_ref[...])
        mid_ref[at, :] = mid
        normed, _ = statistics(mid)
        hidden = (normed * gain_ref[...] + shift_ref[...]).astype(bf16)
        hidden_ref[at, :] = transposed_columns(hidden, grid, rows)


def back_mid_kernel(
    grid, rows, own_ref, p_ref, q_ref, u_ref, w_ref, mid_ref, g_ref, gain_ref, a_ref, b_ref, c_ref, d_ref,
    grad_ref, rel_ref, att_ref, sums_ref,
):
    S = grid[0]
    T, n, hw = att_ref.shape
    R = T // S
    s, r = own_ref[0], own_ref[1]
    parts = (a_ref, b_ref, c_ref, d_ref)
    deep, wide = d_ref.shape
    sums_ref[...] = jnp.zeros_like(sums_ref)
    loop, step = row_loop(n)

    @loop
    def _(i):
        at = pl.ds(pl.multiple_of(i, step), step)
        grad = p_ref[at, :].astype(fp32) + q_ref[at, :].astype(fp32)
        grad += u_ref[at, :].astype(fp32) + w_ref[at, :].astype(fp32)
        grad = transposed_columns(grad, grid[::-1], rows)
        normed, scale = statistics(mid_ref[at, :])
        g = g_ref[at, :].astype(fp32)
        sums_ref[0:1, :] += jnp.sum(grad * normed, axis=0, keepdims=True)
        sums_ref[1:2, :] += jnp.sum(grad, axis=0, keepdims=True)
        grad_mid = g + norm_back(grad * gain_ref[...], normed, scale)
        grad_ref[at, :] = grad_mid
        low = grad_mid.astype(bf16)
        sums_ref[2:3, :] += jnp.sum(low.astype(fp32), axis=0, keepdims=True)
        sums_ref[3:4, :] += jnp.sum(g, axis=0, keepdims=True)
        for k in range(R):
            rel_ref[at, pl.ds(pl.multiple_of((r ^ k) * wide, 128), wide)] = low[:, k * wide : (k + 1) * wide]

    for js in range(S):
        acc = jnp.zeros((n, deep), fp32)
        for jr in range(R):
            part, k = place(js + 4 * jr)
            acc += lax.dot_general(
                rel_ref[:, jr * wide : (jr + 1) * wide],
                parts[part][k * deep : (k + 1) * deep, :],
                ACROSS,
                preferred_element_type=fp32,
            )
        for i in range(R):
            att_ref[(s ^ js) * R + i] = acc[:, i * hw : (i + 1) * hw].astype(bf16)


def back_in_kernel(grid, rows, p_ref, q_ref, u_ref, w_ref, x_ref, g_ref, gain_ref, out_ref, sums_ref):
    sums_ref[...] = jnp.zeros_like(sums_ref)
    loop, step = row_loop(x_ref.shape[0])

    @loop
    def _(i):
        at = pl.ds(pl.multiple_of(i, step), step)
        grad = p_ref[at, :].astype(fp32) + q_ref[at, :].astype(fp32)
        grad += u_ref[at, :].astype(fp32) + w_ref[at, :].astype(fp32)
        grad = transposed_columns(grad, grid[::-1], rows)
        normed, scale = statistics(x_ref[at, :].astype(fp32))
        sums_ref[0:1, :] += jnp.sum(grad * normed, axis=0, keepdims=True)
        sums_ref[1:2, :] += jnp.sum(grad, axis=0, keepdims=True)
        out_ref[at, :] = g_ref[at, :] + norm_back(grad * gain_ref[...], normed, scale)


def out_kernel(p_ref, q_ref, u_ref, w_ref, mid_ref, bias_ref, out_ref):
    loop, step = row_loop(mid_ref.shape[0])

    @loop
    def _(i):
        at = pl.ds(pl.multiple_of(i, step), step)
        term = p_ref[at, :].astype(fp32) + q_ref[at, :].astype(fp32)
        term += u_ref[at, :].astype(fp32) + w_ref[at, :].astype(fp32)
        out_ref[at, :] = (mid_ref[at, :] + (term + bias_ref[...])).astype(bf16)


def outer_kernel(rel_ref, low_ref, *outs):
    deep, wide = outs[3].shape
    for out_ref, part in zip(outs, PARTS):
        for k, j in enumerate(part):
            js, jr = j & 3, j >> 2
            out_ref[k * deep : (k + 1) * deep, :] = lax.dot_general(
                rel_ref[:, js * deep : (js + 1) * deep],
                low_ref[:, jr * wide : (jr + 1) * wide],
                DOWN,
                preferred_element_type=fp32,
            ).astype(bf16)


def tall_kernel(*refs):
    half = len(refs) // 2
    acc = 0.0
    for left, right in zip(refs[:half], refs[half:-1]):
        acc += lax.dot_general(left[...], right[...], DOWN, preferred_element_type=fp32)
    refs[-1][...] = acc.astype(bf16)


def tall_product(lefts, rights, deps=()):
    deep, wide = lefts[0].shape[1], rights[0].shape[1]
    tokens = sum(v.shape[0] for v in lefts)
    tile = min(256, deep)
    return pl.pallas_call(
        ordered(tall_kernel, 2 * len(lefts), deps),
        grid=(deep // tile,),
        in_specs=[pl.BlockSpec((v.shape[0], tile), lambda i: (0, i)) for v in lefts]
        + [pl.BlockSpec(v.shape, lambda i: (0, 0)) for v in rights]
        + [UNREAD] * len(deps),
        out_specs=pl.BlockSpec((tile, wide), lambda i: (i, 0)),
        out_shape=jax.ShapeDtypeStruct((deep, wide), bf16),
        compiler_params=pltpu.CompilerParams(vmem_limit_bytes=48 * 2**20),
        cost_estimate=LIGHT,
    )(*lefts, *rights, *deps)


def up_kernel(h_ref, w_ref, bias_ref, act_ref, slope_ref):
    u = jnp.dot(h_ref[...], w_ref[...], preferred_element_type=fp32) + bias_ref[...]
    cdf = 0.5 * (1.0 + lax.erf(u * 0.7071067811865476))
    act_ref[...] = (u * cdf).astype(bf16)
    slope_ref[...] = cdf + u * jnp.exp(-0.5 * u * u) * 0.3989422804014327


def up_product(h, w, bias):
    tile = min(256, h.shape[0])
    deep, wide = w.shape
    return pl.pallas_call(
        up_kernel,
        grid=(h.shape[0] // tile,),
        in_specs=[
            pl.BlockSpec((tile, deep), lambda i: (i, 0)),
            pl.BlockSpec((deep, wide), lambda i: (0, 0)),
            pl.BlockSpec((1, wide), lambda i: (0, 0)),
        ],
        out_specs=[pl.BlockSpec((tile, wide), lambda i: (i, 0))] * 2,
        out_shape=[jax.ShapeDtypeStruct((h.shape[0], wide), kind) for kind in (bf16, fp32)],
        compiler_params=pltpu.CompilerParams(vmem_limit_bytes=48 * 2**20),
        cost_estimate=LIGHT,
    )(h, w, bias)


def product_kernel(dims, *refs):
    term = lax.dot_general(refs[0][...], refs[1][...], dims, preferred_element_type=fp32)
    refs[-1][...] = (term + refs[2][...] if len(refs) == 4 else term).astype(bf16)


def product(v, w, dims=(((1,), (0,)), ((), ())), bias=(), deps=()):
    tile = min(256, v.shape[0])
    wide = w.shape[1 - dims[0][1][0]]
    return pl.pallas_call(
        ordered(lambda *refs: product_kernel(dims, *refs), 2 + len(bias), deps),
        grid=(v.shape[0] // tile,),
        in_specs=[pl.BlockSpec((tile, v.shape[1]), lambda i: (i, 0)), pl.BlockSpec(w.shape, lambda i: (0, 0))]
        + [pl.BlockSpec((1, wide), lambda i: (0, 0))] * len(bias)
        + [UNREAD] * len(deps),
        out_specs=pl.BlockSpec((tile, wide), lambda i: (i, 0)),
        out_shape=jax.ShapeDtypeStruct((v.shape[0], wide), bf16),
        compiler_params=pltpu.CompilerParams(vmem_limit_bytes=48 * 2**20),
        cost_estimate=LIGHT,
    )(v, w, *bias, *deps)


def down_kernel(g_ref, out_w_ref, slope_ref, up_w_ref, pre_ref, two_ref, sums_ref):
    grad = lax.dot_general(g_ref[...], out_w_ref[...], ACROSS, preferred_element_type=fp32)
    low = (grad * slope_ref[...]).astype(bf16)
    pre_ref[...] = low
    two_ref[...] = lax.dot_general(low, up_w_ref[...], ACROSS, preferred_element_type=fp32).astype(bf16)

    @pl.when(pl.program_id(0) == 0)
    def _():
        sums_ref[...] = jnp.zeros_like(sums_ref)

    sums_ref[0:1, :] += jnp.sum(low.astype(fp32), axis=0, keepdims=True)


def down_product(g, out_w, slope, up_w, deps=()):
    tile = min(256, g.shape[0])
    wide, deep = out_w.shape
    tokens = g.shape[0]

    def tiles(width):
        return pl.BlockSpec((tile, width), lambda i: (i, 0))

    def whole(a, b):
        return pl.BlockSpec((a, b), lambda i: (0, 0))

    return pl.pallas_call(
        ordered(down_kernel, 4, deps),
        grid=(tokens // tile,),
        in_specs=[tiles(deep), whole(wide, deep), tiles(wide), whole(deep, wide)] + [UNREAD] * len(deps),
        out_specs=[tiles(wide), tiles(deep), whole(8, wide)],
        out_shape=[
            jax.ShapeDtypeStruct((tokens, wide), bf16),
            jax.ShapeDtypeStruct((tokens, deep), bf16),
            jax.ShapeDtypeStruct((8, wide), fp32),
        ],
        compiler_params=pltpu.CompilerParams(vmem_limit_bytes=48 * 2**20),
        cost_estimate=LIGHT,
    )(g, out_w, slope, up_w, *deps)


def attend_kernel(heads, own_ref, a_ref, b_ref, c_ref, d_ref, out_ref, q_ref, k_ref, v_ref):
    s, r = own_ref[0], own_ref[1]
    T, n, width = out_ref.shape
    S = q_ref.shape[0] // n
    parts = (a_ref, b_ref, c_ref, d_ref)
    for jr in range(T // S):
        for h in range(heads):
            cols = slice(h * HEAD_DIM, (h + 1) * HEAD_DIM)
            for js in range(S):
                part, k = place(js + 4 * jr)
                at = pl.ds(pl.multiple_of((s ^ js) * n, n), n)
                for i, ref in enumerate((q_ref, k_ref, v_ref)):
                    first = i * width + h * HEAD_DIM
                    ref[at, :] = parts[part][k * n : (k + 1) * n, first : first + HEAD_DIM]
            for a in range(S):
                upto = (a + 1) * n
                q = q_ref[a * n : upto, :]
                scores = lax.dot_general(q, k_ref[:upto, :], ACROSS, preferred_element_type=fp32)
                expons = jnp.exp((scores - jnp.max(scores, axis=-1, keepdims=True)) * HEAD_DIM ** (-0.5))
                probs = (expons * (1.0 / jnp.sum(expons, axis=-1, keepdims=True))).astype(bf16)
                out_ref[a * (T // S) + (r ^ jr), :, cols] = jnp.dot(
                    probs, v_ref[:upto, :], preferred_element_type=fp32
                ).astype(bf16)


def attend_back_kernel(
    heads, own_ref, a_ref, b_ref, c_ref, d_ref, grad_ref, oa_ref, ob_ref, oc_ref, od_ref, sums_ref,
    q_ref, k_ref, v_ref, gq_ref, gk_ref, gv_ref,
):
    s, r = own_ref[0], own_ref[1]
    T, n, width = grad_ref.shape
    S = q_ref.shape[0] // n
    parts = (a_ref, b_ref, c_ref, d_ref)
    outs = (oa_ref, ob_ref, oc_ref, od_ref)
    scaling = HEAD_DIM ** (-0.5)
    sums_ref[...] = jnp.zeros_like(sums_ref)
    for jr in range(T // S):
        for h in range(heads):
            cols = slice(h * HEAD_DIM, (h + 1) * HEAD_DIM)
            for js in range(S):
                part, k = place(js + 4 * jr)
                at = pl.ds(pl.multiple_of((s ^ js) * n, n), n)
                for i, ref in enumerate((q_ref, k_ref, v_ref)):
                    first = i * width + h * HEAD_DIM
                    ref[at, :] = parts[part][k * n : (k + 1) * n, first : first + HEAD_DIM]
            for a in reversed(range(S)):
                upto = (a + 1) * n
                q = q_ref[a * n : upto, :]
                g = grad_ref[a * (T // S) + (r ^ jr), :, cols]
                k = k_ref[:upto, :]
                v = v_ref[:upto, :]
                scores = lax.dot_general(q, k, ACROSS, preferred_element_type=fp32)
                expons = jnp.exp((scores - jnp.max(scores, axis=-1, keepdims=True)) * scaling)
                probs = expons * (1.0 / jnp.sum(expons, axis=-1, keepdims=True))
                grad_probs = lax.dot_general(g, v, ACROSS, preferred_element_type=fp32)
                inner = jnp.sum(probs * grad_probs, axis=-1, keepdims=True)
                grad_scores = (probs * (grad_probs - inner)).astype(bf16)
                gq_ref[a * n : upto, :] = jnp.dot(grad_scores, k, preferred_element_type=fp32)
                gk = lax.dot_general(grad_scores, q, DOWN, preferred_element_type=fp32)
                gv = lax.dot_general(probs.astype(bf16), g, DOWN, preferred_element_type=fp32)
                if a == S - 1:
                    gk_ref[...] = gk
                    gv_ref[...] = gv
                else:
                    gk_ref[:upto, :] += gk
                    gv_ref[:upto, :] += gv
            for js in range(S):
                part, k = place(js + 4 * jr)
                at = pl.ds(pl.multiple_of((s ^ js) * n, n), n)
                for i, (ref, factor) in enumerate(((gq_ref, scaling), (gk_ref, scaling), (gv_ref, 1.0))):
                    first = i * width + h * HEAD_DIM
                    low = (ref[at, :] * factor).astype(bf16)
                    outs[part][k * n : (k + 1) * n, first : first + HEAD_DIM] = low
                    sums_ref[0:1, first : first + HEAD_DIM] += jnp.sum(low.astype(fp32), axis=0, keepdims=True)


def unpack_rows_kernel(own_ref, mine_ref, other_ref, out_ref):
    r, n = own_ref[1], mine_ref.shape[0]
    out_ref[pl.ds(pl.multiple_of(r * n, n), n), :] = mine_ref[...].astype(fp32)
    out_ref[pl.ds(pl.multiple_of((r ^ 1) * n, n), n), :] = other_ref[...].astype(fp32)


def unpack_columns_kernel(groups, S, R, own_ref, mine_ref, other_ref, out_ref):
    r = own_ref[1]
    a, c = groups
    width = mine_ref.shape[-1] // (a * c)
    for s in range(S):
        for i in range(a):
            for k in range(c):
                cols = slice((i * c + k) * width, (i * c + k + 1) * width)
                base = ((i * S + s) * c + k) * R
                for ref, at in ((mine_ref, r), (other_ref, r ^ 1)):
                    out_ref[:, pl.ds(pl.multiple_of((base + at) * width, 128), width)] = ref[s, :, cols].astype(fp32)


def small_call(kernel, out_shape, operands, scratch=(), first_rows=(), deps=()):
    specs = []
    for i, v in enumerate(operands):
        if v.dtype == jnp.int32:
            specs.append(SCALARS)
        elif dict(first_rows).get(i, v.shape[0]) != v.shape[0]:
            specs.append(pl.BlockSpec((dict(first_rows)[i], v.shape[1]), lambda g: (0, 0)))
        else:
            specs.append(pl.BlockSpec(v.shape, lambda g, rank=v.ndim: (0,) * rank))
    many = isinstance(out_shape, list)
    outs = out_shape if many else [out_shape]
    out_specs = [pl.BlockSpec(v.shape, lambda g, rank=len(v.shape): (0,) * rank) for v in outs]
    return pl.pallas_call(
        ordered(kernel, len(operands), deps),
        grid=(1,),
        in_specs=specs + [UNREAD] * len(deps),
        out_specs=out_specs if many else out_specs[0],
        out_shape=out_shape,
        scratch_shapes=scratch,
        compiler_params=pltpu.CompilerParams(vmem_limit_bytes=56 * 2**20),
        cost_estimate=LIGHT,
    )(*operands, *deps)


def on_device(
    inputs,
    cotangent,
    norm1_gain,
    norm1_bias,
    w_qkv,
    query_bias,
    value_bias,
    w_attn_out,
    attn_out_bias,
    norm2_gain,
    norm2_bias,
    w_hidden,
    hidden_bias,
    w_output,
    output_bias,
):
    S, Z, R = lax.axis_size("seq"), lax.axis_size("shard"), lax.axis_size("replica")
    s, z, r = lax.axis_index("seq"), lax.axis_index("shard"), lax.axis_index("replica")
    odd = r != 0
    _, n, D = inputs.shape
    rows = norm1_gain.shape[0]
    F = hidden_bias.shape[0] * S * Z
    T = S * R
    hw = D // T
    fw = F // T
    fr = fw // Z
    heads = hw // HEAD_DIM
    grid = (S, Z)
    own = jnp.stack([s, r]).astype(jnp.int32)

    def shape(*dims, kind=bf16):
        return jax.ShapeDtypeStruct(dims, kind)

    def by_shard(v):
        return v if rows % 128 == 0 else v.reshape(-1, S, Z, rows).swapaxes(1, 2).reshape(-1, D)

    def by_seq(v):
        return v if rows % 128 == 0 else v.reshape(-1, Z, S, rows).swapaxes(1, 2).reshape(-1, D)

    x = inputs.reshape(n, D)
    g_low = cotangent.reshape(n, D)
    t = s * R + r
    attn_part = lax.dynamic_index_in_dim(w_attn_out.reshape(rows, R, D // R), r, 1, keepdims=False).astype(bf16)
    small = (norm1_gain, norm1_bias, query_bias, value_bias, attn_out_bias, norm2_gain, norm2_bias, output_bias, hidden_bias)
    attn_part, *small = tie(attn_part, *small)
    attn_part = line_gather(attn_part)
    table = jnp.concatenate([v.astype(bf16) for v in small])[None]
    table = gather_table(gather_table(table, "shard"), "seq")
    qkv_pieces = lax.dynamic_index_in_dim(w_qkv.reshape(rows, 3, S, R, hw), r, 3, keepdims=False).astype(bf16)
    qkv_rows = seq_exchange(qkv_pieces.transpose(2, 0, 1, 3).reshape(S, rows, 3 * hw)).reshape(S * rows, 3 * hw)
    hidden_pieces = lax.dynamic_index_in_dim(w_hidden.reshape(rows, S, Z, R, fr), r, 3, keepdims=False).astype(bf16)
    hidden_pieces, qkv_rows = tie(hidden_pieces.transpose(1, 0, 2, 3).reshape(S, rows, fw), qkv_rows)
    qkv_matrix = line_gather(qkv_rows)
    hidden_rows = seq_exchange(hidden_pieces).reshape(S * rows, fw)
    output_part = lax.dynamic_index_in_dim(w_output.reshape(R, fr, D), r, 0, keepdims=False).astype(bf16)

    table = table.astype(fp32)
    gain_one, shift_one, query_shift, value_shift, attn_shift, gain_two, shift_two, output_shift = (
        table[:, i * rows : (i + 1) * rows].reshape(1, D) for i in range(8)
    )
    hidden_shift = lax.dynamic_index_in_dim(
        lax.dynamic_index_in_dim(table[:, 8 * rows :].reshape(S, Z, R, fr), s, 0, keepdims=False), r, 1, keepdims=False
    ).reshape(1, fw)
    bias_row = jnp.concatenate(
        [
            lax.dynamic_slice_in_dim(query_shift[0], t * hw, hw),
            jnp.zeros((hw,), fp32),
            lax.dynamic_slice_in_dim(value_shift[0], t * hw, hw),
        ]
    ).reshape(1, 3 * hw)

    hidden_in = by_shard(
        small_call(lambda *refs: norm_kernel(grid, rows, *refs), shape(n, D), (x, gain_one, shift_one), deps=(qkv_rows,))
    )
    in_near = gather_near(hidden_in)
    hidden_rows, output_part, in_near = tie(hidden_rows, output_part, in_near)
    hidden_matrix = line_gather(hidden_rows)
    output_matrix = line_gather(output_part)
    hidden_in_parts = gather_parts(in_near, gather_diagonal(*in_near))
    hidden_in_parts, attn_part = tie(hidden_in_parts, attn_part)
    attn_near = gather_near(attn_part)
    qkv_parts = [product(v, qkv_matrix, bias=(bias_row,)) for v in hidden_in_parts]
    qkv_parts, attn_near = tie(qkv_parts, attn_near)
    attn_far = gather_diagonal(*attn_near)
    head_block = pltpu.VMEM((S * n, HEAD_DIM), bf16)
    head_sums = pltpu.VMEM((S * n, HEAD_DIM), fp32)
    attended = small_call(
        lambda *refs: attend_kernel(heads, *refs), shape(T, n, hw), (own, *qkv_parts), [head_block] * 3
    )
    attended, attn_far, attn_near = tie(attended, attn_far, attn_near)
    attn_parts = gather_parts(attn_near, attn_far)
    attended = lax.all_to_all(attended, ("seq", "replica"), 0, 0, tiled=True)
    attended, g_low = tie(attended, g_low)
    g_near = gather_near(g_low)
    mid_rows, hidden_two, attended_rel = small_call(
        lambda *refs: mid_kernel(grid, rows, *refs),
        [shape(n, D, kind=fp32), shape(n, D), shape(n, D)],
        (own, attended, *attn_parts, x, attn_shift, gain_two, shift_two),
    )

    two_near = gather_near(by_shard(hidden_two))
    two_near, g_near = tie(two_near, g_near)
    two_diagonal = gather_diagonal(*two_near)
    two_first = jnp.concatenate(two_near)
    up_first = up_product(two_first, hidden_matrix, hidden_shift)
    up_first, two_diagonal = tie(up_first, two_diagonal)
    two_second = jnp.concatenate(two_diagonal)
    hidden_two_parts = (two_first, flip(two_first, CORE), two_second, flip(two_second, CORE))
    two_second, g_near = tie(two_second, g_near)
    g_far = gather_diagonal(*g_near)
    ups = [up_first] + [up_product(v, hidden_matrix, hidden_shift) for v in hidden_two_parts[1:]]
    ups[1:], g_far = tie(ups[1:], g_far)
    activated_parts, slope_parts = zip(*ups)
    g_parts = gather_parts(g_near, g_far)
    grad_output = tall_product(activated_parts, g_parts)
    down = [None] * 4
    down[3] = down_product(g_parts[3], output_matrix, slope_parts[3], hidden_matrix, (grad_output,))
    down[2] = down_product(g_parts[2], output_matrix, slope_parts[2], hidden_matrix, (down[3][0],))
    two_far = far_sum(down[2][1], down[3][1])
    down[1] = down_product(g_parts[1], output_matrix, slope_parts[1], hidden_matrix, (two_far,))
    two_got = flip(down[1][1], CORE)
    down[0] = down_product(g_parts[0], output_matrix, slope_parts[0], hidden_matrix, (down[1][0],))
    grad_pre_parts, grad_two_parts, hidden_sums = zip(*down)
    grad_output = line_scatter(grad_output)
    grad_two = scatter_relay(grad_two_parts[0], two_got, scatter_diagonal(two_far))
    out_parts = [None] * 4
    deps = ()
    for i in (3, 2):
        out_parts[i] = product(activated_parts[i], output_matrix, deps=(grad_two[3], *deps))
        deps = (out_parts[i],)
    grad_hidden = tall_product(hidden_two_parts, grad_pre_parts, deps)
    out_far = far_sum(out_parts[2], out_parts[3])
    grad_two = scatter_last(*grad_two)

    grad_mid, grad_mid_rel, grad_heads, sums_two = small_call(
        lambda *refs: back_mid_kernel(grid, rows, *refs),
        [shape(n, D, kind=fp32), shape(n, D), shape(T, n, hw), shape(8, D, kind=fp32)],
        (own, *map(by_seq, grad_two), mid_rows, g_low, gain_two, *attn_parts),
        first_rows=((1, n), (2, n)),
        deps=(out_far, grad_hidden),
    )
    grad_hidden, grad_mid = tie(grad_hidden, grad_mid)
    grad_hidden = line_scatter(grad_hidden)
    out_parts[1] = product(activated_parts[1], output_matrix, deps=(grad_mid,))
    grad_heads = lax.all_to_all(grad_heads, ("seq", "replica"), 0, 0, tiled=True)
    grad_heads, out_theirs, grad_output, out_far = tie(grad_heads, out_parts[1], grad_output, out_far)
    out_diagonal = scatter_diagonal_by_row(out_far)
    *grad_qkv_parts, sums_qkv = small_call(
        lambda *refs: attend_back_kernel(heads, *refs),
        [shape(v.shape[0], 3 * hw) for v in qkv_parts] + [shape(8, 3 * hw, kind=fp32)],
        (own, *qkv_parts, grad_heads),
        [head_block] * 3 + [head_sums] * 3,
        deps=(out_parts[1],),
    )
    out_got = flip(out_theirs, CORE)
    other_output = flip(grad_output, COL)
    into = [None] * 4
    into[3] = product(grad_qkv_parts[3], qkv_matrix, ACROSS, deps=(other_output, *out_diagonal))
    into[2] = product(grad_qkv_parts[2], qkv_matrix, ACROSS, deps=(into[3],))
    into_far = far_sum(into[2], into[3])
    into[1] = product(grad_qkv_parts[1], qkv_matrix, ACROSS, deps=(into_far,))
    into[0] = product(grad_qkv_parts[0], qkv_matrix, ACROSS, deps=(into[1],))
    into_got = flip(into[1], CORE)
    grad_qkv = tall_product(hidden_in_parts, grad_qkv_parts, (into[0],))
    grad_in = scatter_relay(into[0], into_got, scatter_diagonal(into_far))
    *grad_in, grad_qkv = tie(*grad_in, grad_qkv)
    grad_qkv = line_scatter(grad_qkv).reshape(S, rows, 3 * hw)
    grad_attn_parts = small_call(
        outer_kernel, [shape(*v.shape) for v in attn_parts], (attended_rel, grad_mid_rel), deps=(grad_in[3],)
    )
    attn_got = flip(grad_attn_parts[1], CORE)
    attn_far = far_sum(grad_attn_parts[2], grad_attn_parts[3])
    attn_diagonal = scatter_diagonal(attn_far)
    grad_in = scatter_last(*grad_in)
    grad_inputs, sums_one = small_call(
        lambda *refs: back_in_kernel(grid, rows, *refs),
        [shape(n, D, kind=fp32), shape(8, D, kind=fp32)],
        (*map(by_seq, grad_in), x, grad_mid, gain_one),
        first_rows=((0, n), (1, n)),
        deps=(),
    )
    out_parts[0] = product(activated_parts[0], output_matrix, deps=(sums_one,))
    sums_one, attn_got, grad_hidden = tie(sums_one, attn_got, grad_hidden)
    grad_attn = scatter_relay(grad_attn_parts[0], attn_got, attn_diagonal)
    grad_attn = scatter_last(*grad_attn)
    out_terms = scatter_last(*scatter_relay(out_parts[0], out_got, out_diagonal))
    layer_out = small_call(
        out_kernel, shape(n, D), (*out_terms, mid_rows, output_shift), first_rows=((0, n), (1, n))
    )

    def columns_of_both(v, groups):
        v = v.reshape(-1, rows, v.shape[-1])
        other = flip(v, COL)
        a, c = groups
        count, width = v.shape[0], v.shape[-1] // (a * c)
        if width % 128 == 0:
            return small_call(
                lambda *refs: unpack_columns_kernel(groups, count, R, *refs),
                shape(rows, count * R * v.shape[-1], kind=fp32),
                (own, v, other),
            )
        pair = jnp.stack([jnp.where(odd, other, v), jnp.where(odd, v, other)]).reshape(R, count, rows, a, c, width)
        return pair.transpose(2, 3, 1, 4, 0, 5).reshape(rows, -1).astype(fp32)

    grad_output_matrix = small_call(
        unpack_rows_kernel, shape(R * fr, D, kind=fp32), (own, grad_output, other_output)
    )
    grad_hidden_matrix = columns_of_both(seq_exchange(grad_hidden.reshape(S, rows, fw)), (1, Z))
    grad_qkv_matrix = columns_of_both(seq_exchange(grad_qkv), (3, 1))
    deep = D // S
    p, q, u, w = (v[:deep].astype(fp32) for v in grad_attn)
    grad_attn = line_scatter((p + q + u + w).astype(bf16))
    grad_attn_matrix = columns_of_both(grad_attn, (1, 1))

    hidden_sums = sum(v[0] for v in hidden_sums).reshape(1, Z, 1, fr)
    hidden_sums = lax.dynamic_update_slice(jnp.zeros((S, Z, R, fr), fp32), hidden_sums, (s, 0, r, 0))
    none = jnp.zeros((D,), fp32)
    sums = total(
        jnp.concatenate(
            [sums_one[i].reshape(S * Z, rows) for i in range(2)]
            + [
                lax.dynamic_update_slice_in_dim(none, sums_qkv[0, i * hw : (i + 1) * hw], t * hw, 0).reshape(S * Z, rows)
                for i in (0, 2)
            ]
            + [sums_two[i].reshape(S * Z, rows) for i in range(4)]
            + [hidden_sums.reshape(S * Z, R * fr)],
            axis=1,
        )
    )
    sums = lax.dynamic_index_in_dim(sums, s * Z + z, 0, keepdims=False)

    def part(i):
        return sums[i * rows : (i + 1) * rows]

    return (
        layer_out.reshape(inputs.shape),
        grad_inputs.reshape(inputs.shape),
        part(0),
        part(1),
        grad_qkv_matrix,
        part(2),
        part(3),
        grad_attn_matrix,
        part(6),
        part(4),
        part(5),
        grad_hidden_matrix,
        sums[8 * rows :],
        grad_output_matrix,
        part(7),
    )


def solution(mesh):
    tokens = P(("shard", "replica"), "seq", None)
    vector = P(("seq", "shard"))
    matrix = P(("seq", "shard"), None)
    weights = (
        vector,
        vector,
        matrix,
        vector,
        vector,
        matrix,
        vector,
        vector,
        vector,
        matrix,
        vector,
        matrix,
        vector,
    )
    return jax.shard_map(
        on_device,
        mesh=mesh,
        in_specs=(tokens, tokens) + weights,
        out_specs=(tokens, tokens) + weights,
        check_vma=False,
    )
```

```python
import jax
import jax.numpy as jnp
from jax import lax
from jax.experimental import pallas as pl
from jax.experimental.pallas import tpu as pltpu
from jax.sharding import PartitionSpec as P

HEAD_DIM = 128
bf16 = jnp.bfloat16
fp32 = jnp.float32

CORE = ("seq", 1)
ROW = ("seq", 2)
COL = ("replica", 1)


PARTS = ((0, 2, 4), (1, 3, 5), (6,), (7,))
ACROSS = (((1,), (1,)), ((), ()))
DOWN = (((0,), (0,)), ((), ()))
WHOLE = pl.BlockSpec(memory_space=pltpu.VMEM)
SCALARS = pl.BlockSpec(memory_space=pltpu.SMEM)


LIGHT = pl.CostEstimate(flops=1, bytes_accessed=1, transcendentals=0)


def place(j):
    return next((i, part.index(j)) for i, part in enumerate(PARTS) if j in part)


def tie(*groups):
    return lax.optimization_barrier(groups)


def ordered(kernel, count, deps):
    return lambda *refs: kernel(*refs[:count], *refs[count + len(deps) :])


UNREAD = pl.BlockSpec(memory_space=pl.ANY)


def flip(v, link):
    axis, bit = link
    return lax.ppermute(v, axis, [(i, i ^ bit) for i in range(lax.axis_size(axis))])


def gather_near(v):
    return v, flip(v, ROW), flip(v, COL)


def gather_diagonal(v, py, px):
    h = v.shape[0] // 2
    return flip(py[:h], COL), flip(px[h:], ROW)


def gather_parts(near, diagonal):
    first, second = jnp.concatenate(near), jnp.concatenate(diagonal)
    return first, flip(first, CORE), second, flip(second, CORE)


def relay_kernel(y_ref, gy_ref, x_ref, gx_ref, ra_ref, rb_ref, ys_ref, xs_ref):
    h = ra_ref.shape[0]
    top, bot = slice(0, h), slice(h, 2 * h)
    ys_ref[top, :] = (
        y_ref[top, :].astype(fp32) + gy_ref[top, :].astype(fp32) + ra_ref[...].astype(fp32)
    ).astype(bf16)
    ys_ref[bot, :] = (y_ref[bot, :].astype(fp32) + gy_ref[bot, :].astype(fp32)).astype(bf16)
    xs_ref[top, :] = (x_ref[top, :].astype(fp32) + gx_ref[top, :].astype(fp32)).astype(bf16)
    xs_ref[bot, :] = (
        x_ref[bot, :].astype(fp32) + gx_ref[bot, :].astype(fp32) + rb_ref[...].astype(fp32)
    ).astype(bf16)


def relay_by_row_kernel(y_ref, gy_ref, x_ref, gx_ref, rb_ref, ys_ref, xs_ref):
    ys_ref[...] = (y_ref[...].astype(fp32) + gy_ref[...].astype(fp32)).astype(bf16)
    xs_ref[...] = (x_ref[...].astype(fp32) + gx_ref[...].astype(fp32) + rb_ref[...].astype(fp32)).astype(bf16)


def far_sum(far, far_theirs):
    return (far.astype(fp32) + flip(far_theirs, CORE).astype(fp32)).astype(bf16)


def scatter_diagonal(far):
    h = far.shape[0] // 2
    return flip(far[:h], COL), flip(far[h:], ROW)


def scatter_diagonal_by_row(far):
    return (flip(far, ROW),)


def scatter_relay(mine, got, diagonal, deps=()):
    width = diagonal[0].shape[1]
    n = sum(v.shape[0] for v in diagonal)

    def rows(i):
        return pl.BlockSpec((n, width), lambda g: (i, 0))

    diagonal_specs = [pl.BlockSpec(v.shape, lambda g: (0, 0)) for v in diagonal]
    y_send, x_send = pl.pallas_call(
        ordered(relay_kernel if len(diagonal) == 2 else relay_by_row_kernel, 4 + len(diagonal), deps),
        grid=(1,),
        in_specs=[rows(1), rows(1), rows(2), rows(2), *diagonal_specs] + [UNREAD] * len(deps),
        out_specs=[rows(0), rows(0)],
        out_shape=[jax.ShapeDtypeStruct((n, width), bf16)] * 2,
        compiler_params=pltpu.CompilerParams(vmem_limit_bytes=40 * 2**20),
        cost_estimate=LIGHT,
    )(mine, got, mine, got, *diagonal, *deps)
    return mine, got, y_send, x_send


def scatter_last(mine, got, y_send, x_send):
    return mine, got, flip(y_send, ROW), flip(x_send, COL)


def line_gather(v):
    return lax.all_gather(v, "shard", axis=0, tiled=True)


def line_scatter(v):
    return lax.psum_scatter(v, "shard", scatter_dimension=0, tiled=True)


def seq_exchange(v):
    return lax.all_to_all(v, "seq", 0, 0, tiled=True)


def gather_table(table, axis):
    index, bit = lax.axis_index(axis), 1
    while bit < lax.axis_size(axis):
        other = flip(table, (axis, bit))
        odd = (index & bit) != 0
        table = jnp.concatenate([jnp.where(odd, other, table), jnp.where(odd, table, other)])
        bit *= 2
    return table


def total(v):
    for axis in ("shard", "seq", "replica"):
        bit = 1
        while bit < lax.axis_size(axis):
            v = v + flip(v, (axis, bit))
            bit *= 2
    return v


def row_loop(n):
    step = 64 if n % 64 == 0 else n
    return pl.loop(0, n, step=step), step


def statistics(v):
    centred = v - jnp.mean(v, axis=1, keepdims=True)
    scale = lax.rsqrt(jnp.mean(centred * centred, axis=1, keepdims=True) + 1e-05)
    return centred * scale, scale


def norm_back(grad, normed, scale):
    first = jnp.mean(grad, axis=1, keepdims=True)
    second = jnp.mean(grad * normed, axis=1, keepdims=True)
    return scale * (grad - first - normed * second)


def transposed_columns(v, grid, rows):
    a, b = grid
    if rows % 128 or a == 1 or b == 1:
        return v
    return jnp.concatenate(
        [v[:, (i * b + k) * rows : (i * b + k + 1) * rows] for k in range(b) for i in range(a)], axis=1
    )


def norm_kernel(grid, rows, x_ref, gain_ref, shift_ref, out_ref):
    loop, step = row_loop(x_ref.shape[0])

    @loop
    def _(i):
        at = pl.ds(pl.multiple_of(i, step), step)
        normed, _ = statistics(x_ref[at, :].astype(fp32))
        hidden = (normed * gain_ref[...] + shift_ref[...]).astype(bf16)
        out_ref[at, :] = transposed_columns(hidden, grid, rows)


def mid_kernel(
    grid, rows, own_ref, att_ref, a_ref, b_ref, c_ref, d_ref, x_ref, bias_ref, gain_ref, shift_ref,
    mid_ref, hidden_ref, rel_ref,
):
    S = grid[0]
    T, n, hw = att_ref.shape
    R = T // S
    s, r = own_ref[0], own_ref[1]
    parts = (a_ref, b_ref, c_ref, d_ref)
    deep, wide = d_ref.shape
    for js in range(S):
        for i in range(R):
            rel_ref[:, (js * R + i) * hw : (js * R + i + 1) * hw] = att_ref[(s ^ js) * R + i]
    for jr in range(R):
        acc = jnp.zeros((n, wide), fp32)
        for js in range(S):
            part, k = place(js + 4 * jr)
            acc += jnp.dot(
                rel_ref[:, js * deep : (js + 1) * deep],
                parts[part][k * deep : (k + 1) * deep, :],
                preferred_element_type=fp32,
            )
        mid_ref[:, pl.ds(pl.multiple_of((r ^ jr) * wide, 128), wide)] = acc
    loop, step = row_loop(n)

    @loop
    def _(i):
        at = pl.ds(pl.multiple_of(i, step), step)
        mid = x_ref[at, :].astype(fp32) + (mid_ref[at, :] + bias_ref[...])
        mid_ref[at, :] = mid
        normed, _ = statistics(mid)
        hidden = (normed * gain_ref[...] + shift_ref[...]).astype(bf16)
        hidden_ref[at, :] = transposed_columns(hidden, grid, rows)


def back_mid_kernel(
    grid, rows, own_ref, p_ref, q_ref, u_ref, w_ref, mid_ref, g_ref, gain_ref, a_ref, b_ref, c_ref, d_ref,
    grad_ref, rel_ref, att_ref, sums_ref,
):
    S = grid[0]
    T, n, hw = att_ref.shape
    R = T // S
    s, r = own_ref[0], own_ref[1]
    parts = (a_ref, b_ref, c_ref, d_ref)
    deep, wide = d_ref.shape
    sums_ref[...] = jnp.zeros_like(sums_ref)
    loop, step = row_loop(n)

    @loop
    def _(i):
        at = pl.ds(pl.multiple_of(i, step), step)
        grad = p_ref[at, :].astype(fp32) + q_ref[at, :].astype(fp32)
        grad += u_ref[at, :].astype(fp32) + w_ref[at, :].astype(fp32)
        grad = transposed_columns(grad, grid[::-1], rows)
        normed, scale = statistics(mid_ref[at, :])
        g = g_ref[at, :].astype(fp32)
        sums_ref[0:1, :] += jnp.sum(grad * normed, axis=0, keepdims=True)
        sums_ref[1:2, :] += jnp.sum(grad, axis=0, keepdims=True)
        grad_mid = g + norm_back(grad * gain_ref[...], normed, scale)
        grad_ref[at, :] = grad_mid
        low = grad_mid.astype(bf16)
        sums_ref[2:3, :] += jnp.sum(low.astype(fp32), axis=0, keepdims=True)
        sums_ref[3:4, :] += jnp.sum(g, axis=0, keepdims=True)
        for k in range(R):
            rel_ref[at, pl.ds(pl.multiple_of((r ^ k) * wide, 128), wide)] = low[:, k * wide : (k + 1) * wide]

    for js in range(S):
        acc = jnp.zeros((n, deep), fp32)
        for jr in range(R):
            part, k = place(js + 4 * jr)
            acc += lax.dot_general(
                rel_ref[:, jr * wide : (jr + 1) * wide],
                parts[part][k * deep : (k + 1) * deep, :],
                ACROSS,
                preferred_element_type=fp32,
            )
        for i in range(R):
            att_ref[(s ^ js) * R + i] = acc[:, i * hw : (i + 1) * hw].astype(bf16)


def back_in_kernel(grid, rows, p_ref, q_ref, u_ref, w_ref, x_ref, g_ref, gain_ref, out_ref, sums_ref):
    sums_ref[...] = jnp.zeros_like(sums_ref)
    loop, step = row_loop(x_ref.shape[0])

    @loop
    def _(i):
        at = pl.ds(pl.multiple_of(i, step), step)
        grad = p_ref[at, :].astype(fp32) + q_ref[at, :].astype(fp32)
        grad += u_ref[at, :].astype(fp32) + w_ref[at, :].astype(fp32)
        grad = transposed_columns(grad, grid[::-1], rows)
        normed, scale = statistics(x_ref[at, :].astype(fp32))
        sums_ref[0:1, :] += jnp.sum(grad * normed, axis=0, keepdims=True)
        sums_ref[1:2, :] += jnp.sum(grad, axis=0, keepdims=True)
        out_ref[at, :] = g_ref[at, :] + norm_back(grad * gain_ref[...], normed, scale)


def out_kernel(p_ref, q_ref, u_ref, w_ref, mid_ref, bias_ref, out_ref):
    loop, step = row_loop(mid_ref.shape[0])

    @loop
    def _(i):
        at = pl.ds(pl.multiple_of(i, step), step)
        term = p_ref[at, :].astype(fp32) + q_ref[at, :].astype(fp32)
        term += u_ref[at, :].astype(fp32) + w_ref[at, :].astype(fp32)
        out_ref[at, :] = (mid_ref[at, :] + (term + bias_ref[...])).astype(bf16)


def outer_kernel(rel_ref, low_ref, *outs):
    deep, wide = outs[3].shape
    for out_ref, part in zip(outs, PARTS):
        for k, j in enumerate(part):
            js, jr = j & 3, j >> 2
            out_ref[k * deep : (k + 1) * deep, :] = lax.dot_general(
                rel_ref[:, js * deep : (js + 1) * deep],
                low_ref[:, jr * wide : (jr + 1) * wide],
                DOWN,
                preferred_element_type=fp32,
            ).astype(bf16)


def tall_kernel(*refs):
    half = len(refs) // 2
    acc = 0.0
    for left, right in zip(refs[:half], refs[half:-1]):
        acc += lax.dot_general(left[...], right[...], DOWN, preferred_element_type=fp32)
    refs[-1][...] = acc.astype(bf16)


def tall_product(lefts, rights, deps=()):
    deep, wide = lefts[0].shape[1], rights[0].shape[1]
    tokens = sum(v.shape[0] for v in lefts)
    tile = min(256, deep)
    return pl.pallas_call(
        ordered(tall_kernel, 2 * len(lefts), deps),
        grid=(deep // tile,),
        in_specs=[pl.BlockSpec((v.shape[0], tile), lambda i: (0, i)) for v in lefts]
        + [pl.BlockSpec(v.shape, lambda i: (0, 0)) for v in rights]
        + [UNREAD] * len(deps),
        out_specs=pl.BlockSpec((tile, wide), lambda i: (i, 0)),
        out_shape=jax.ShapeDtypeStruct((deep, wide), bf16),
        compiler_params=pltpu.CompilerParams(vmem_limit_bytes=48 * 2**20),
        cost_estimate=LIGHT,
    )(*lefts, *rights, *deps)


def up_kernel(h_ref, w_ref, bias_ref, act_ref, slope_ref):
    u = jnp.dot(h_ref[...], w_ref[...], preferred_element_type=fp32) + bias_ref[...]
    cdf = 0.5 * (1.0 + lax.erf(u * 0.7071067811865476))
    act_ref[...] = (u * cdf).astype(bf16)
    slope_ref[...] = cdf + u * jnp.exp(-0.5 * u * u) * 0.3989422804014327


def up_product(h, w, bias):
    tile = min(256, h.shape[0])
    deep, wide = w.shape
    return pl.pallas_call(
        up_kernel,
        grid=(h.shape[0] // tile,),
        in_specs=[
            pl.BlockSpec((tile, deep), lambda i: (i, 0)),
            pl.BlockSpec((deep, wide), lambda i: (0, 0)),
            pl.BlockSpec((1, wide), lambda i: (0, 0)),
        ],
        out_specs=[pl.BlockSpec((tile, wide), lambda i: (i, 0))] * 2,
        out_shape=[jax.ShapeDtypeStruct((h.shape[0], wide), kind) for kind in (bf16, fp32)],
        compiler_params=pltpu.CompilerParams(vmem_limit_bytes=48 * 2**20),
        cost_estimate=LIGHT,
    )(h, w, bias)


def product_kernel(dims, *refs):
    term = lax.dot_general(refs[0][...], refs[1][...], dims, preferred_element_type=fp32)
    refs[-1][...] = (term + refs[2][...] if len(refs) == 4 else term).astype(bf16)


def product(v, w, dims=(((1,), (0,)), ((), ())), bias=(), deps=()):
    tile = min(256, v.shape[0])
    wide = w.shape[1 - dims[0][1][0]]
    return pl.pallas_call(
        ordered(lambda *refs: product_kernel(dims, *refs), 2 + len(bias), deps),
        grid=(v.shape[0] // tile,),
        in_specs=[pl.BlockSpec((tile, v.shape[1]), lambda i: (i, 0)), pl.BlockSpec(w.shape, lambda i: (0, 0))]
        + [pl.BlockSpec((1, wide), lambda i: (0, 0))] * len(bias)
        + [UNREAD] * len(deps),
        out_specs=pl.BlockSpec((tile, wide), lambda i: (i, 0)),
        out_shape=jax.ShapeDtypeStruct((v.shape[0], wide), bf16),
        compiler_params=pltpu.CompilerParams(vmem_limit_bytes=48 * 2**20),
        cost_estimate=LIGHT,
    )(v, w, *bias, *deps)


def down_kernel(g_ref, out_w_ref, slope_ref, up_w_ref, pre_ref, two_ref, sums_ref):
    grad = lax.dot_general(g_ref[...], out_w_ref[...], ACROSS, preferred_element_type=fp32)
    low = (grad * slope_ref[...]).astype(bf16)
    pre_ref[...] = low
    two_ref[...] = lax.dot_general(low, up_w_ref[...], ACROSS, preferred_element_type=fp32).astype(bf16)

    @pl.when(pl.program_id(0) == 0)
    def _():
        sums_ref[...] = jnp.zeros_like(sums_ref)

    sums_ref[0:1, :] += jnp.sum(low.astype(fp32), axis=0, keepdims=True)


def down_product(g, out_w, slope, up_w, deps=()):
    tile = min(256, g.shape[0])
    wide, deep = out_w.shape
    tokens = g.shape[0]

    def tiles(width):
        return pl.BlockSpec((tile, width), lambda i: (i, 0))

    def whole(a, b):
        return pl.BlockSpec((a, b), lambda i: (0, 0))

    return pl.pallas_call(
        ordered(down_kernel, 4, deps),
        grid=(tokens // tile,),
        in_specs=[tiles(deep), whole(wide, deep), tiles(wide), whole(deep, wide)] + [UNREAD] * len(deps),
        out_specs=[tiles(wide), tiles(deep), whole(8, wide)],
        out_shape=[
            jax.ShapeDtypeStruct((tokens, wide), bf16),
            jax.ShapeDtypeStruct((tokens, deep), bf16),
            jax.ShapeDtypeStruct((8, wide), fp32),
        ],
        compiler_params=pltpu.CompilerParams(vmem_limit_bytes=48 * 2**20),
        cost_estimate=LIGHT,
    )(g, out_w, slope, up_w, *deps)


def attend_kernel(heads, own_ref, a_ref, b_ref, c_ref, d_ref, out_ref, q_ref, k_ref, v_ref):
    s, r = own_ref[0], own_ref[1]
    T, n, width = out_ref.shape
    S = q_ref.shape[0] // n
    parts = (a_ref, b_ref, c_ref, d_ref)
    for jr in range(T // S):
        for h in range(heads):
            cols = slice(h * HEAD_DIM, (h + 1) * HEAD_DIM)
            for js in range(S):
                part, k = place(js + 4 * jr)
                at = pl.ds(pl.multiple_of((s ^ js) * n, n), n)
                for i, ref in enumerate((q_ref, k_ref, v_ref)):
                    first = i * width + h * HEAD_DIM
                    ref[at, :] = parts[part][k * n : (k + 1) * n, first : first + HEAD_DIM]
            for a in range(S):
                upto = (a + 1) * n
                q = q_ref[a * n : upto, :]
                scores = lax.dot_general(q, k_ref[:upto, :], ACROSS, preferred_element_type=fp32)
                expons = jnp.exp((scores - jnp.max(scores, axis=-1, keepdims=True)) * HEAD_DIM ** (-0.5))
                probs = (expons * (1.0 / jnp.sum(expons, axis=-1, keepdims=True))).astype(bf16)
                out_ref[a * (T // S) + (r ^ jr), :, cols] = jnp.dot(
                    probs, v_ref[:upto, :], preferred_element_type=fp32
                ).astype(bf16)


def attend_back_kernel(
    heads, own_ref, a_ref, b_ref, c_ref, d_ref, grad_ref, oa_ref, ob_ref, oc_ref, od_ref, sums_ref,
    q_ref, k_ref, v_ref, gq_ref, gk_ref, gv_ref,
):
    s, r = own_ref[0], own_ref[1]
    T, n, width = grad_ref.shape
    S = q_ref.shape[0] // n
    parts = (a_ref, b_ref, c_ref, d_ref)
    outs = (oa_ref, ob_ref, oc_ref, od_ref)
    scaling = HEAD_DIM ** (-0.5)
    sums_ref[...] = jnp.zeros_like(sums_ref)
    for jr in range(T // S):
        for h in range(heads):
            cols = slice(h * HEAD_DIM, (h + 1) * HEAD_DIM)
            for js in range(S):
                part, k = place(js + 4 * jr)
                at = pl.ds(pl.multiple_of((s ^ js) * n, n), n)
                for i, ref in enumerate((q_ref, k_ref, v_ref)):
                    first = i * width + h * HEAD_DIM
                    ref[at, :] = parts[part][k * n : (k + 1) * n, first : first + HEAD_DIM]
            for a in reversed(range(S)):
                upto = (a + 1) * n
                q = q_ref[a * n : upto, :]
                g = grad_ref[a * (T // S) + (r ^ jr), :, cols]
                k = k_ref[:upto, :]
                v = v_ref[:upto, :]
                scores = lax.dot_general(q, k, ACROSS, preferred_element_type=fp32)
                expons = jnp.exp((scores - jnp.max(scores, axis=-1, keepdims=True)) * scaling)
                probs = expons * (1.0 / jnp.sum(expons, axis=-1, keepdims=True))
                grad_probs = lax.dot_general(g, v, ACROSS, preferred_element_type=fp32)
                inner = jnp.sum(probs * grad_probs, axis=-1, keepdims=True)
                grad_scores = (probs * (grad_probs - inner)).astype(bf16)
                gq_ref[a * n : upto, :] = jnp.dot(grad_scores, k, preferred_element_type=fp32)
                gk = lax.dot_general(grad_scores, q, DOWN, preferred_element_type=fp32)
                gv = lax.dot_general(probs.astype(bf16), g, DOWN, preferred_element_type=fp32)
                if a == S - 1:
                    gk_ref[...] = gk
                    gv_ref[...] = gv
                else:
                    gk_ref[:upto, :] += gk
                    gv_ref[:upto, :] += gv
            for js in range(S):
                part, k = place(js + 4 * jr)
                at = pl.ds(pl.multiple_of((s ^ js) * n, n), n)
                for i, (ref, factor) in enumerate(((gq_ref, scaling), (gk_ref, scaling), (gv_ref, 1.0))):
                    first = i * width + h * HEAD_DIM
                    low = (ref[at, :] * factor).astype(bf16)
                    outs[part][k * n : (k + 1) * n, first : first + HEAD_DIM] = low
                    sums_ref[0:1, first : first + HEAD_DIM] += jnp.sum(low.astype(fp32), axis=0, keepdims=True)


def pack_kernel(*refs):
    at = 0
    for ref in refs[:-1]:
        refs[-1][:, at : at + ref.shape[1]] = ref[...].astype(bf16)
        at += ref.shape[1]


def unpack_rows_kernel(own_ref, mine_ref, other_ref, out_ref):
    r, n = own_ref[1], mine_ref.shape[0]
    out_ref[pl.ds(pl.multiple_of(r * n, n), n), :] = mine_ref[...].astype(fp32)
    out_ref[pl.ds(pl.multiple_of((r ^ 1) * n, n), n), :] = other_ref[...].astype(fp32)


def unpack_columns_kernel(groups, S, R, own_ref, mine_ref, other_ref, out_ref):
    r = own_ref[1]
    a, c = groups
    width = mine_ref.shape[-1] // (a * c)
    for s in range(S):
        for i in range(a):
            for k in range(c):
                cols = slice((i * c + k) * width, (i * c + k + 1) * width)
                base = ((i * S + s) * c + k) * R
                for ref, at in ((mine_ref, r), (other_ref, r ^ 1)):
                    out_ref[:, pl.ds(pl.multiple_of((base + at) * width, 128), width)] = ref[s, :, cols].astype(fp32)


def small_call(kernel, out_shape, operands, scratch=(), first_rows=(), deps=()):
    specs = []
    for i, v in enumerate(operands):
        if v.dtype == jnp.int32:
            specs.append(SCALARS)
        elif dict(first_rows).get(i, v.shape[0]) != v.shape[0]:
            specs.append(pl.BlockSpec((dict(first_rows)[i], v.shape[1]), lambda g: (0, 0)))
        else:
            specs.append(pl.BlockSpec(v.shape, lambda g, rank=v.ndim: (0,) * rank))
    many = isinstance(out_shape, list)
    outs = out_shape if many else [out_shape]
    out_specs = [pl.BlockSpec(v.shape, lambda g, rank=len(v.shape): (0,) * rank) for v in outs]
    return pl.pallas_call(
        ordered(kernel, len(operands), deps),
        grid=(1,),
        in_specs=specs + [UNREAD] * len(deps),
        out_specs=out_specs if many else out_specs[0],
        out_shape=out_shape,
        scratch_shapes=scratch,
        compiler_params=pltpu.CompilerParams(vmem_limit_bytes=56 * 2**20),
        cost_estimate=LIGHT,
    )(*operands, *deps)


def on_device(
    inputs,
    cotangent,
    norm1_gain,
    norm1_bias,
    w_qkv,
    query_bias,
    value_bias,
    w_attn_out,
    attn_out_bias,
    norm2_gain,
    norm2_bias,
    w_hidden,
    hidden_bias,
    w_output,
    output_bias,
):
    S, Z, R = lax.axis_size("seq"), lax.axis_size("shard"), lax.axis_size("replica")
    s, z, r = lax.axis_index("seq"), lax.axis_index("shard"), lax.axis_index("replica")
    odd = r != 0
    _, n, D = inputs.shape
    rows = norm1_gain.shape[0]
    F = hidden_bias.shape[0] * S * Z
    T = S * R
    hw = D // T
    fw = F // T
    fr = fw // Z
    heads = hw // HEAD_DIM
    grid = (S, Z)
    own = jnp.stack([s, r]).astype(jnp.int32)

    def shape(*dims, kind=bf16):
        return jax.ShapeDtypeStruct(dims, kind)

    def by_shard(v):
        return v if rows % 128 == 0 else v.reshape(-1, S, Z, rows).swapaxes(1, 2).reshape(-1, D)

    def by_seq(v):
        return v if rows % 128 == 0 else v.reshape(-1, Z, S, rows).swapaxes(1, 2).reshape(-1, D)

    x = inputs.reshape(n, D)
    g_low = cotangent.reshape(n, D)
    t = s * R + r
    attn_part = lax.dynamic_index_in_dim(w_attn_out.reshape(rows, R, D // R), r, 1, keepdims=False).astype(bf16)
    small = (norm1_gain, norm1_bias, query_bias, value_bias, attn_out_bias, norm2_gain, norm2_bias, output_bias, hidden_bias)
    attn_part, *small = tie(attn_part, *small)
    attn_part = line_gather(attn_part)
    small = [v.reshape(1, -1) for v in small]
    if rows % 128 == 0:
        table = small_call(pack_kernel, shape(1, sum(v.size for v in small)), small)
    else:
        table = jnp.concatenate([v.astype(bf16) for v in small], axis=1)
    table = gather_table(gather_table(table, "shard"), "seq")
    qkv_pieces = lax.dynamic_index_in_dim(w_qkv.reshape(rows, 3, S, R, hw), r, 3, keepdims=False).astype(bf16)
    qkv_rows = seq_exchange(qkv_pieces.transpose(2, 0, 1, 3).reshape(S, rows, 3 * hw)).reshape(S * rows, 3 * hw)
    hidden_pieces = lax.dynamic_index_in_dim(w_hidden.reshape(rows, S, Z, R, fr), r, 3, keepdims=False).astype(bf16)
    hidden_pieces, qkv_rows = tie(hidden_pieces.transpose(1, 0, 2, 3).reshape(S, rows, fw), qkv_rows)
    qkv_matrix = line_gather(qkv_rows)
    hidden_rows = seq_exchange(hidden_pieces).reshape(S * rows, fw)
    output_part = lax.dynamic_index_in_dim(w_output.reshape(R, fr, D), r, 0, keepdims=False).astype(bf16)

    table = table.astype(fp32)
    gain_one, shift_one, query_shift, value_shift, attn_shift, gain_two, shift_two, output_shift = (
        table[:, i * rows : (i + 1) * rows].reshape(1, D) for i in range(8)
    )
    hidden_shift = lax.dynamic_index_in_dim(
        lax.dynamic_index_in_dim(table[:, 8 * rows :].reshape(S, Z, R, fr), s, 0, keepdims=False), r, 1, keepdims=False
    ).reshape(1, fw)
    bias_row = jnp.concatenate(
        [
            lax.dynamic_slice_in_dim(query_shift[0], t * hw, hw),
            jnp.zeros((hw,), fp32),
            lax.dynamic_slice_in_dim(value_shift[0], t * hw, hw),
        ]
    ).reshape(1, 3 * hw)

    hidden_in = by_shard(
        small_call(lambda *refs: norm_kernel(grid, rows, *refs), shape(n, D), (x, gain_one, shift_one))
    )
    in_near = gather_near(hidden_in)
    hidden_rows, output_part, in_near = tie(hidden_rows, output_part, in_near)
    hidden_matrix = line_gather(hidden_rows)
    output_matrix = line_gather(output_part)
    hidden_in_parts = gather_parts(in_near, gather_diagonal(*in_near))
    hidden_in_parts, attn_part = tie(hidden_in_parts, attn_part)
    attn_near = gather_near(attn_part)
    qkv_parts = [product(v, qkv_matrix, bias=(bias_row,)) for v in hidden_in_parts]
    qkv_parts, attn_near = tie(qkv_parts, attn_near)
    attn_far = gather_diagonal(*attn_near)
    head_block = pltpu.VMEM((S * n, HEAD_DIM), bf16)
    head_sums = pltpu.VMEM((S * n, HEAD_DIM), fp32)
    attended = small_call(
        lambda *refs: attend_kernel(heads, *refs), shape(T, n, hw), (own, *qkv_parts), [head_block] * 3
    )
    attended, attn_far, attn_near = tie(attended, attn_far, attn_near)
    attn_parts = gather_parts(attn_near, attn_far)
    attended = lax.all_to_all(attended, ("seq", "replica"), 0, 0, tiled=True)
    attended, g_low = tie(attended, g_low)
    g_near = gather_near(g_low)
    mid_rows, hidden_two, attended_rel = small_call(
        lambda *refs: mid_kernel(grid, rows, *refs),
        [shape(n, D, kind=fp32), shape(n, D), shape(n, D)],
        (own, attended, *attn_parts, x, attn_shift, gain_two, shift_two),
    )

    two_near = gather_near(by_shard(hidden_two))
    two_near, g_near = tie(two_near, g_near)
    two_diagonal = gather_diagonal(*two_near)
    two_first = jnp.concatenate(two_near)
    up_first = up_product(two_first, hidden_matrix, hidden_shift)
    up_first, two_diagonal = tie(up_first, two_diagonal)
    two_second = jnp.concatenate(two_diagonal)
    hidden_two_parts = (two_first, flip(two_first, CORE), two_second, flip(two_second, CORE))
    two_second, g_near = tie(two_second, g_near)
    g_far = gather_diagonal(*g_near)
    ups = [up_first] + [up_product(v, hidden_matrix, hidden_shift) for v in hidden_two_parts[1:]]
    ups[1:], g_far = tie(ups[1:], g_far)
    activated_parts, slope_parts = zip(*ups)
    g_parts = gather_parts(g_near, g_far)
    grad_output = tall_product(activated_parts, g_parts)
    down = [None] * 4
    down[3] = down_product(g_parts[3], output_matrix, slope_parts[3], hidden_matrix, (grad_output,))
    down[2] = down_product(g_parts[2], output_matrix, slope_parts[2], hidden_matrix, (down[3][0],))
    two_far = far_sum(down[2][1], down[3][1])
    down[1] = down_product(g_parts[1], output_matrix, slope_parts[1], hidden_matrix, (two_far,))
    two_got = flip(down[1][1], CORE)
    down[0] = down_product(g_parts[0], output_matrix, slope_parts[0], hidden_matrix, (down[1][0],))
    grad_pre_parts, grad_two_parts, hidden_sums = zip(*down)
    grad_output = line_scatter(grad_output)
    grad_two = scatter_relay(grad_two_parts[0], two_got, scatter_diagonal(two_far))
    out_parts = [None] * 4
    deps = ()
    for i in (3, 2):
        out_parts[i] = product(activated_parts[i], output_matrix, deps=(grad_two[3], *deps))
        deps = (out_parts[i],)
    grad_hidden = tall_product(hidden_two_parts, grad_pre_parts, deps)
    out_far = far_sum(out_parts[2], out_parts[3])
    grad_two = scatter_last(*grad_two)

    grad_mid, grad_mid_rel, grad_heads, sums_two = small_call(
        lambda *refs: back_mid_kernel(grid, rows, *refs),
        [shape(n, D, kind=fp32), shape(n, D), shape(T, n, hw), shape(8, D, kind=fp32)],
        (own, *map(by_seq, grad_two), mid_rows, g_low, gain_two, *attn_parts),
        first_rows=((1, n), (2, n)),
        deps=(out_far, grad_hidden),
    )
    grad_hidden, grad_mid = tie(grad_hidden, grad_mid)
    grad_hidden = line_scatter(grad_hidden)
    out_parts[1] = product(activated_parts[1], output_matrix, deps=(grad_mid,))
    out_parts[0] = product(activated_parts[0], output_matrix, deps=(grad_mid,))
    grad_heads = lax.all_to_all(grad_heads, ("seq", "replica"), 0, 0, tiled=True)
    grad_heads, out_theirs, out_mine, grad_output, out_far = tie(
        grad_heads, out_parts[1], out_parts[0], grad_output, out_far
    )
    out_diagonal = scatter_diagonal_by_row(out_far)
    *grad_qkv_parts, sums_qkv = small_call(
        lambda *refs: attend_back_kernel(heads, *refs),
        [shape(v.shape[0], 3 * hw) for v in qkv_parts] + [shape(8, 3 * hw, kind=fp32)],
        (own, *qkv_parts, grad_heads),
        [head_block] * 3 + [head_sums] * 3,
    )
    out_got = flip(out_theirs, CORE)
    other_output = flip(grad_output, COL)
    into = [None] * 4
    into[3] = product(grad_qkv_parts[3], qkv_matrix, ACROSS)
    into[2] = product(grad_qkv_parts[2], qkv_matrix, ACROSS, deps=(into[3], other_output, *out_diagonal))
    out_terms = scatter_relay(out_mine, out_got, out_diagonal, deps=(into[2],))
    into_far = far_sum(into[2], into[3])
    into[1] = product(grad_qkv_parts[1], qkv_matrix, ACROSS, deps=(into_far, out_terms[3]))
    into[0] = product(grad_qkv_parts[0], qkv_matrix, ACROSS, deps=(into[1],))
    into_got = flip(into[1], CORE)
    grad_attn_parts = small_call(
        outer_kernel, [shape(*v.shape) for v in attn_parts], (attended_rel, grad_mid_rel), deps=(into[0],)
    )
    grad_in = scatter_relay(into[0], into_got, scatter_diagonal(into_far), deps=(grad_attn_parts[0],))
    grad_qkv = tall_product(hidden_in_parts, grad_qkv_parts, (grad_in[3],))
    attn_got = flip(grad_attn_parts[1], CORE)
    attn_far = far_sum(grad_attn_parts[2], grad_attn_parts[3])
    attn_far, grad_qkv = tie(attn_far, grad_qkv)
    grad_qkv = line_scatter(grad_qkv).reshape(S, rows, 3 * hw)
    attn_diagonal = scatter_diagonal(attn_far)
    grad_attn = scatter_relay(grad_attn_parts[0], attn_got, attn_diagonal)
    grad_hidden, in_send = tie(grad_hidden, grad_in[3])
    grad_in = scatter_last(*grad_in[:3], in_send)
    grad_hidden = seq_exchange(grad_hidden.reshape(S, rows, fw))
    grad_hidden, attn_send = tie(grad_hidden, grad_attn[3])
    grad_attn = scatter_last(*grad_attn[:3], attn_send)
    other_hidden = flip(grad_hidden, COL)
    grad_inputs, sums_one = small_call(
        lambda *refs: back_in_kernel(grid, rows, *refs),
        [shape(n, D, kind=fp32), shape(8, D, kind=fp32)],
        (*map(by_seq, grad_in), x, grad_mid, gain_one),
        first_rows=((0, n), (1, n)),
        deps=(attn_send,),
    )
    out_terms = scatter_last(*out_terms)
    layer_out = small_call(
        out_kernel, shape(n, D), (*out_terms, mid_rows, output_shift), first_rows=((0, n), (1, n))
    )

    def columns_of_both(v, groups, other=None):
        v = v.reshape(-1, rows, v.shape[-1])
        other = flip(v, COL) if other is None else other
        a, c = groups
        count, width = v.shape[0], v.shape[-1] // (a * c)
        if width % 128 == 0:
            return small_call(
                lambda *refs: unpack_columns_kernel(groups, count, R, *refs),
                shape(rows, count * R * v.shape[-1], kind=fp32),
                (own, v, other),
            )
        pair = jnp.stack([jnp.where(odd, other, v), jnp.where(odd, v, other)]).reshape(R, count, rows, a, c, width)
        return pair.transpose(2, 3, 1, 4, 0, 5).reshape(rows, -1).astype(fp32)

    grad_output_matrix = small_call(
        unpack_rows_kernel, shape(R * fr, D, kind=fp32), (own, grad_output, other_output)
    )
    grad_hidden_matrix = columns_of_both(grad_hidden, (1, Z), other_hidden)
    grad_qkv_matrix = columns_of_both(seq_exchange(grad_qkv), (3, 1))
    deep = D // S
    p, q, u, w = (v[:deep].astype(fp32) for v in grad_attn)
    grad_attn = line_scatter((p + q + u + w).astype(bf16))
    grad_attn_matrix = columns_of_both(grad_attn, (1, 1))

    hidden_sums = sum(v[0] for v in hidden_sums).reshape(1, Z, 1, fr)
    hidden_sums = lax.dynamic_update_slice(jnp.zeros((S, Z, R, fr), fp32), hidden_sums, (s, 0, r, 0))
    none = jnp.zeros((D,), fp32)
    sums = total(
        jnp.concatenate(
            [sums_one[i].reshape(S * Z, rows) for i in range(2)]
            + [
                lax.dynamic_update_slice_in_dim(none, sums_qkv[0, i * hw : (i + 1) * hw], t * hw, 0).reshape(S * Z, rows)
                for i in (0, 2)
            ]
            + [sums_two[i].reshape(S * Z, rows) for i in range(4)]
            + [hidden_sums.reshape(S * Z, R * fr)],
            axis=1,
        )
    )
    sums = lax.dynamic_index_in_dim(sums, s * Z + z, 0, keepdims=False)

    def part(i):
        return sums[i * rows : (i + 1) * rows]

    return (
        layer_out.reshape(inputs.shape),
        grad_inputs.reshape(inputs.shape),
        part(0),
        part(1),
        grad_qkv_matrix,
        part(2),
        part(3),
        grad_attn_matrix,
        part(6),
        part(4),
        part(5),
        grad_hidden_matrix,
        sums[8 * rows :],
        grad_output_matrix,
        part(7),
    )


def solution(mesh):
    tokens = P(("shard", "replica"), "seq", None)
    vector = P(("seq", "shard"))
    matrix = P(("seq", "shard"), None)
    weights = (
        vector,
        vector,
        matrix,
        vector,
        vector,
        matrix,
        vector,
        vector,
        vector,
        matrix,
        vector,
        matrix,
        vector,
    )
    return jax.shard_map(
        on_device,
        mesh=mesh,
        in_specs=(tokens, tokens) + weights,
        out_specs=(tokens, tokens) + weights,
        check_vma=False,
    )
```

```python
import jax
import jax.numpy as jnp
from jax import lax
from jax.experimental import pallas as pl
from jax.experimental.pallas import tpu as pltpu
from jax.sharding import PartitionSpec as P

HEAD_DIM = 128
bf16 = jnp.bfloat16
fp32 = jnp.float32

CORE = ("seq", 1)
ROW = ("seq", 2)
COL = ("replica", 1)


PARTS = ((0, 2, 4), (1, 3, 5), (6,), (7,))
ACROSS = (((1,), (1,)), ((), ()))
DOWN = (((0,), (0,)), ((), ()))
WHOLE = pl.BlockSpec(memory_space=pltpu.VMEM)
SCALARS = pl.BlockSpec(memory_space=pltpu.SMEM)


LIGHT = pl.CostEstimate(flops=1, bytes_accessed=1, transcendentals=0)


def place(j):
    return next((i, part.index(j)) for i, part in enumerate(PARTS) if j in part)


def tie(*groups):
    return lax.optimization_barrier(groups)


def ordered(kernel, count, deps):
    return lambda *refs: kernel(*refs[:count], *refs[count + len(deps) :])


UNREAD = pl.BlockSpec(memory_space=pl.ANY)


def flip(v, link):
    axis, bit = link
    return lax.ppermute(v, axis, [(i, i ^ bit) for i in range(lax.axis_size(axis))])


def gather_near(v):
    return v, flip(v, ROW), flip(v, COL)


def gather_diagonal(v, py, px):
    h = v.shape[0] // 2
    return flip(py[:h], COL), flip(px[h:], ROW)


def gather_parts(near, diagonal):
    first, second = jnp.concatenate(near), jnp.concatenate(diagonal)
    return first, flip(first, CORE), second, flip(second, CORE)


def relay_kernel(y_ref, gy_ref, x_ref, gx_ref, ra_ref, rb_ref, ys_ref, xs_ref):
    h = ra_ref.shape[0]
    top, bot = slice(0, h), slice(h, 2 * h)
    ys_ref[top, :] = (
        y_ref[top, :].astype(fp32) + gy_ref[top, :].astype(fp32) + ra_ref[...].astype(fp32)
    ).astype(bf16)
    ys_ref[bot, :] = (y_ref[bot, :].astype(fp32) + gy_ref[bot, :].astype(fp32)).astype(bf16)
    xs_ref[top, :] = (x_ref[top, :].astype(fp32) + gx_ref[top, :].astype(fp32)).astype(bf16)
    xs_ref[bot, :] = (
        x_ref[bot, :].astype(fp32) + gx_ref[bot, :].astype(fp32) + rb_ref[...].astype(fp32)
    ).astype(bf16)


def relay_by_row_kernel(y_ref, gy_ref, x_ref, gx_ref, rb_ref, ys_ref, xs_ref):
    ys_ref[...] = (y_ref[...].astype(fp32) + gy_ref[...].astype(fp32)).astype(bf16)
    xs_ref[...] = (x_ref[...].astype(fp32) + gx_ref[...].astype(fp32) + rb_ref[...].astype(fp32)).astype(bf16)


def far_sum(far, far_theirs):
    return (far.astype(fp32) + flip(far_theirs, CORE).astype(fp32)).astype(bf16)


def scatter_diagonal(far):
    h = far.shape[0] // 2
    return flip(far[:h], COL), flip(far[h:], ROW)


def scatter_diagonal_by_row(far):
    return (flip(far, ROW),)


def scatter_relay(mine, got, diagonal, deps=()):
    width = diagonal[0].shape[1]
    n = sum(v.shape[0] for v in diagonal)

    def rows(i):
        return pl.BlockSpec((n, width), lambda g: (i, 0))

    diagonal_specs = [pl.BlockSpec(v.shape, lambda g: (0, 0)) for v in diagonal]
    y_send, x_send = pl.pallas_call(
        ordered(relay_kernel if len(diagonal) == 2 else relay_by_row_kernel, 4 + len(diagonal), deps),
        grid=(1,),
        in_specs=[rows(1), rows(1), rows(2), rows(2), *diagonal_specs] + [UNREAD] * len(deps),
        out_specs=[rows(0), rows(0)],
        out_shape=[jax.ShapeDtypeStruct((n, width), bf16)] * 2,
        compiler_params=pltpu.CompilerParams(vmem_limit_bytes=40 * 2**20),
        cost_estimate=LIGHT,
    )(mine, got, mine, got, *diagonal, *deps)
    return mine, got, y_send, x_send


def scatter_last(mine, got, y_send, x_send):
    return mine, got, flip(y_send, ROW), flip(x_send, COL)


def line_gather(v):
    return lax.all_gather(v, "shard", axis=0, tiled=True)


def line_scatter(v):
    return lax.psum_scatter(v, "shard", scatter_dimension=0, tiled=True)


def seq_exchange(v):
    return lax.all_to_all(v, "seq", 0, 0, tiled=True)


def gather_table(table, axis):
    index, bit = lax.axis_index(axis), 1
    while bit < lax.axis_size(axis):
        other = flip(table, (axis, bit))
        odd = (index & bit) != 0
        table = jnp.concatenate([jnp.where(odd, other, table), jnp.where(odd, table, other)])
        bit *= 2
    return table


def total(v):
    for axis in ("shard", "seq", "replica"):
        bit = 1
        while bit < lax.axis_size(axis):
            v = v + flip(v, (axis, bit))
            bit *= 2
    return v


def row_loop(n):
    step = 64 if n % 64 == 0 else n
    return pl.loop(0, n, step=step), step


def statistics(v):
    centred = v - jnp.mean(v, axis=1, keepdims=True)
    scale = lax.rsqrt(jnp.mean(centred * centred, axis=1, keepdims=True) + 1e-05)
    return centred * scale, scale


def norm_back(grad, normed, scale):
    first = jnp.mean(grad, axis=1, keepdims=True)
    second = jnp.mean(grad * normed, axis=1, keepdims=True)
    return scale * (grad - first - normed * second)


def transposed_columns(v, grid, rows):
    a, b = grid
    if rows % 128 or a == 1 or b == 1:
        return v
    return jnp.concatenate(
        [v[:, (i * b + k) * rows : (i * b + k + 1) * rows] for k in range(b) for i in range(a)], axis=1
    )


def norm_kernel(grid, rows, x_ref, gain_ref, shift_ref, out_ref):
    loop, step = row_loop(x_ref.shape[0])

    @loop
    def _(i):
        at = pl.ds(pl.multiple_of(i, step), step)
        normed, _ = statistics(x_ref[at, :].astype(fp32))
        hidden = (normed * gain_ref[...] + shift_ref[...]).astype(bf16)
        out_ref[at, :] = transposed_columns(hidden, grid, rows)


def mid_kernel(
    grid, rows, own_ref, att_ref, a_ref, b_ref, c_ref, d_ref, x_ref, bias_ref, gain_ref, shift_ref,
    mid_ref, hidden_ref, rel_ref,
):
    S = grid[0]
    T, n, hw = att_ref.shape
    R = T // S
    s, r = own_ref[0], own_ref[1]
    parts = (a_ref, b_ref, c_ref, d_ref)
    deep, wide = d_ref.shape
    for js in range(S):
        for i in range(R):
            rel_ref[:, (js * R + i) * hw : (js * R + i + 1) * hw] = att_ref[(s ^ js) * R + i]
    for jr in range(R):
        acc = jnp.zeros((n, wide), fp32)
        for js in range(S):
            part, k = place(js + 4 * jr)
            acc += jnp.dot(
                rel_ref[:, js * deep : (js + 1) * deep],
                parts[part][k * deep : (k + 1) * deep, :],
                preferred_element_type=fp32,
            )
        mid_ref[:, pl.ds(pl.multiple_of((r ^ jr) * wide, 128), wide)] = acc
    loop, step = row_loop(n)

    @loop
    def _(i):
        at = pl.ds(pl.multiple_of(i, step), step)
        mid = x_ref[at, :].astype(fp32) + (mid_ref[at, :] + bias_ref[...])
        mid_ref[at, :] = mid
        normed, _ = statistics(mid)
        hidden = (normed * gain_ref[...] + shift_ref[...]).astype(bf16)
        hidden_ref[at, :] = transposed_columns(hidden, grid, rows)


def back_mid_kernel(
    grid, rows, own_ref, p_ref, q_ref, u_ref, w_ref, mid_ref, g_ref, gain_ref, a_ref, b_ref, c_ref, d_ref,
    grad_ref, rel_ref, att_ref, sums_ref,
):
    S = grid[0]
    T, n, hw = att_ref.shape
    R = T // S
    s, r = own_ref[0], own_ref[1]
    parts = (a_ref, b_ref, c_ref, d_ref)
    deep, wide = d_ref.shape
    sums_ref[...] = jnp.zeros_like(sums_ref)
    loop, step = row_loop(n)

    @loop
    def _(i):
        at = pl.ds(pl.multiple_of(i, step), step)
        grad = p_ref[at, :].astype(fp32) + q_ref[at, :].astype(fp32)
        grad += u_ref[at, :].astype(fp32) + w_ref[at, :].astype(fp32)
        grad = transposed_columns(grad, grid[::-1], rows)
        normed, scale = statistics(mid_ref[at, :])
        g = g_ref[at, :].astype(fp32)
        sums_ref[0:1, :] += jnp.sum(grad * normed, axis=0, keepdims=True)
        sums_ref[1:2, :] += jnp.sum(grad, axis=0, keepdims=True)
        grad_mid = g + norm_back(grad * gain_ref[...], normed, scale)
        grad_ref[at, :] = grad_mid
        low = grad_mid.astype(bf16)
        sums_ref[2:3, :] += jnp.sum(low.astype(fp32), axis=0, keepdims=True)
        sums_ref[3:4, :] += jnp.sum(g, axis=0, keepdims=True)
        for k in range(R):
            rel_ref[at, pl.ds(pl.multiple_of((r ^ k) * wide, 128), wide)] = low[:, k * wide : (k + 1) * wide]

    for js in range(S):
        acc = jnp.zeros((n, deep), fp32)
        for jr in range(R):
            part, k = place(js + 4 * jr)
            acc += lax.dot_general(
                rel_ref[:, jr * wide : (jr + 1) * wide],
                parts[part][k * deep : (k + 1) * deep, :],
                ACROSS,
                preferred_element_type=fp32,
            )
        for i in range(R):
            att_ref[(s ^ js) * R + i] = acc[:, i * hw : (i + 1) * hw].astype(bf16)


def back_in_kernel(grid, rows, p_ref, q_ref, u_ref, w_ref, x_ref, g_ref, gain_ref, out_ref, sums_ref):
    sums_ref[...] = jnp.zeros_like(sums_ref)
    loop, step = row_loop(x_ref.shape[0])

    @loop
    def _(i):
        at = pl.ds(pl.multiple_of(i, step), step)
        grad = p_ref[at, :].astype(fp32) + q_ref[at, :].astype(fp32)
        grad += u_ref[at, :].astype(fp32) + w_ref[at, :].astype(fp32)
        grad = transposed_columns(grad, grid[::-1], rows)
        normed, scale = statistics(x_ref[at, :].astype(fp32))
        sums_ref[0:1, :] += jnp.sum(grad * normed, axis=0, keepdims=True)
        sums_ref[1:2, :] += jnp.sum(grad, axis=0, keepdims=True)
        out_ref[at, :] = g_ref[at, :] + norm_back(grad * gain_ref[...], normed, scale)


def out_kernel(p_ref, q_ref, u_ref, w_ref, mid_ref, bias_ref, out_ref):
    loop, step = row_loop(mid_ref.shape[0])

    @loop
    def _(i):
        at = pl.ds(pl.multiple_of(i, step), step)
        term = p_ref[at, :].astype(fp32) + q_ref[at, :].astype(fp32)
        term += u_ref[at, :].astype(fp32) + w_ref[at, :].astype(fp32)
        out_ref[at, :] = (mid_ref[at, :] + (term + bias_ref[...])).astype(bf16)


def outer_kernel(rel_ref, low_ref, *outs):
    deep, wide = outs[3].shape
    for out_ref, part in zip(outs, PARTS):
        for k, j in enumerate(part):
            js, jr = j & 3, j >> 2
            out_ref[k * deep : (k + 1) * deep, :] = lax.dot_general(
                rel_ref[:, js * deep : (js + 1) * deep],
                low_ref[:, jr * wide : (jr + 1) * wide],
                DOWN,
                preferred_element_type=fp32,
            ).astype(bf16)


def tall_kernel(*refs):
    half = len(refs) // 2
    acc = 0.0
    for left, right in zip(refs[:half], refs[half:-1]):
        acc += lax.dot_general(left[...], right[...], DOWN, preferred_element_type=fp32)
    refs[-1][...] = acc.astype(bf16)


def tall_product(lefts, rights, deps=()):
    deep, wide = lefts[0].shape[1], rights[0].shape[1]
    tokens = sum(v.shape[0] for v in lefts)
    tile = min(256, deep)
    return pl.pallas_call(
        ordered(tall_kernel, 2 * len(lefts), deps),
        grid=(deep // tile,),
        in_specs=[pl.BlockSpec((v.shape[0], tile), lambda i: (0, i)) for v in lefts]
        + [pl.BlockSpec(v.shape, lambda i: (0, 0)) for v in rights]
        + [UNREAD] * len(deps),
        out_specs=pl.BlockSpec((tile, wide), lambda i: (i, 0)),
        out_shape=jax.ShapeDtypeStruct((deep, wide), bf16),
        compiler_params=pltpu.CompilerParams(vmem_limit_bytes=48 * 2**20),
        cost_estimate=LIGHT,
    )(*lefts, *rights, *deps)


def up_kernel(h_ref, w_ref, bias_ref, act_ref, slope_ref):
    u = jnp.dot(h_ref[...], w_ref[...], preferred_element_type=fp32) + bias_ref[...]
    cdf = 0.5 * (1.0 + lax.erf(u * 0.7071067811865476))
    act_ref[...] = (u * cdf).astype(bf16)
    slope_ref[...] = cdf + u * jnp.exp(-0.5 * u * u) * 0.3989422804014327


def up_product(h, w, bias):
    tile = min(256, h.shape[0])
    deep, wide = w.shape
    return pl.pallas_call(
        up_kernel,
        grid=(h.shape[0] // tile,),
        in_specs=[
            pl.BlockSpec((tile, deep), lambda i: (i, 0)),
            pl.BlockSpec((deep, wide), lambda i: (0, 0)),
            pl.BlockSpec((1, wide), lambda i: (0, 0)),
        ],
        out_specs=[pl.BlockSpec((tile, wide), lambda i: (i, 0))] * 2,
        out_shape=[jax.ShapeDtypeStruct((h.shape[0], wide), kind) for kind in (bf16, fp32)],
        compiler_params=pltpu.CompilerParams(vmem_limit_bytes=48 * 2**20),
        cost_estimate=LIGHT,
    )(h, w, bias)


def product_kernel(dims, *refs):
    term = lax.dot_general(refs[0][...], refs[1][...], dims, preferred_element_type=fp32)
    refs[-1][...] = (term + refs[2][...] if len(refs) == 4 else term).astype(bf16)


def product(v, w, dims=(((1,), (0,)), ((), ())), bias=(), deps=()):
    tile = min(256, v.shape[0])
    wide = w.shape[1 - dims[0][1][0]]
    return pl.pallas_call(
        ordered(lambda *refs: product_kernel(dims, *refs), 2 + len(bias), deps),
        grid=(v.shape[0] // tile,),
        in_specs=[pl.BlockSpec((tile, v.shape[1]), lambda i: (i, 0)), pl.BlockSpec(w.shape, lambda i: (0, 0))]
        + [pl.BlockSpec((1, wide), lambda i: (0, 0))] * len(bias)
        + [UNREAD] * len(deps),
        out_specs=pl.BlockSpec((tile, wide), lambda i: (i, 0)),
        out_shape=jax.ShapeDtypeStruct((v.shape[0], wide), bf16),
        compiler_params=pltpu.CompilerParams(vmem_limit_bytes=48 * 2**20),
        cost_estimate=LIGHT,
    )(v, w, *bias, *deps)


def down_kernel(g_ref, out_w_ref, slope_ref, up_w_ref, pre_ref, two_ref, sums_ref):
    grad = lax.dot_general(g_ref[...], out_w_ref[...], ACROSS, preferred_element_type=fp32)
    low = (grad * slope_ref[...]).astype(bf16)
    pre_ref[...] = low
    two_ref[...] = lax.dot_general(low, up_w_ref[...], ACROSS, preferred_element_type=fp32).astype(bf16)

    @pl.when(pl.program_id(0) == 0)
    def _():
        sums_ref[...] = jnp.zeros_like(sums_ref)

    sums_ref[0:1, :] += jnp.sum(low.astype(fp32), axis=0, keepdims=True)


def down_product(g, out_w, slope, up_w, deps=()):
    tile = min(256, g.shape[0])
    wide, deep = out_w.shape
    tokens = g.shape[0]

    def tiles(width):
        return pl.BlockSpec((tile, width), lambda i: (i, 0))

    def whole(a, b):
        return pl.BlockSpec((a, b), lambda i: (0, 0))

    return pl.pallas_call(
        ordered(down_kernel, 4, deps),
        grid=(tokens // tile,),
        in_specs=[tiles(deep), whole(wide, deep), tiles(wide), whole(deep, wide)] + [UNREAD] * len(deps),
        out_specs=[tiles(wide), tiles(deep), whole(8, wide)],
        out_shape=[
            jax.ShapeDtypeStruct((tokens, wide), bf16),
            jax.ShapeDtypeStruct((tokens, deep), bf16),
            jax.ShapeDtypeStruct((8, wide), fp32),
        ],
        compiler_params=pltpu.CompilerParams(vmem_limit_bytes=48 * 2**20),
        cost_estimate=LIGHT,
    )(g, out_w, slope, up_w, *deps)


def attend_kernel(heads, own_ref, a_ref, b_ref, c_ref, d_ref, out_ref, q_ref, k_ref, v_ref):
    s, r = own_ref[0], own_ref[1]
    T, n, width = out_ref.shape
    S = q_ref.shape[0] // n
    parts = (a_ref, b_ref, c_ref, d_ref)
    for jr in range(T // S):
        for h in range(heads):
            cols = slice(h * HEAD_DIM, (h + 1) * HEAD_DIM)
            for js in range(S):
                part, k = place(js + 4 * jr)
                at = pl.ds(pl.multiple_of((s ^ js) * n, n), n)
                for i, ref in enumerate((q_ref, k_ref, v_ref)):
                    first = i * width + h * HEAD_DIM
                    ref[at, :] = parts[part][k * n : (k + 1) * n, first : first + HEAD_DIM]
            for a in range(S):
                upto = (a + 1) * n
                q = q_ref[a * n : upto, :]
                scores = lax.dot_general(q, k_ref[:upto, :], ACROSS, preferred_element_type=fp32)
                expons = jnp.exp((scores - jnp.max(scores, axis=-1, keepdims=True)) * HEAD_DIM ** (-0.5))
                probs = (expons * (1.0 / jnp.sum(expons, axis=-1, keepdims=True))).astype(bf16)
                out_ref[a * (T // S) + (r ^ jr), :, cols] = jnp.dot(
                    probs, v_ref[:upto, :], preferred_element_type=fp32
                ).astype(bf16)


def attend_back_kernel(
    heads, own_ref, a_ref, b_ref, c_ref, d_ref, grad_ref, oa_ref, ob_ref, oc_ref, od_ref, sums_ref,
    q_ref, k_ref, v_ref, gq_ref, gk_ref, gv_ref,
):
    s, r = own_ref[0], own_ref[1]
    T, n, width = grad_ref.shape
    S = q_ref.shape[0] // n
    parts = (a_ref, b_ref, c_ref, d_ref)
    outs = (oa_ref, ob_ref, oc_ref, od_ref)
    scaling = HEAD_DIM ** (-0.5)
    sums_ref[...] = jnp.zeros_like(sums_ref)
    for jr in range(T // S):
        for h in range(heads):
            cols = slice(h * HEAD_DIM, (h + 1) * HEAD_DIM)
            for js in range(S):
                part, k = place(js + 4 * jr)
                at = pl.ds(pl.multiple_of((s ^ js) * n, n), n)
                for i, ref in enumerate((q_ref, k_ref, v_ref)):
                    first = i * width + h * HEAD_DIM
                    ref[at, :] = parts[part][k * n : (k + 1) * n, first : first + HEAD_DIM]
            for a in reversed(range(S)):
                upto = (a + 1) * n
                q = q_ref[a * n : upto, :]
                g = grad_ref[a * (T // S) + (r ^ jr), :, cols]
                k = k_ref[:upto, :]
                v = v_ref[:upto, :]
                scores = lax.dot_general(q, k, ACROSS, preferred_element_type=fp32)
                expons = jnp.exp((scores - jnp.max(scores, axis=-1, keepdims=True)) * scaling)
                probs = expons * (1.0 / jnp.sum(expons, axis=-1, keepdims=True))
                grad_probs = lax.dot_general(g, v, ACROSS, preferred_element_type=fp32)
                inner = jnp.sum(probs * grad_probs, axis=-1, keepdims=True)
                grad_scores = (probs * (grad_probs - inner)).astype(bf16)
                gq_ref[a * n : upto, :] = jnp.dot(grad_scores, k, preferred_element_type=fp32)
                gk = lax.dot_general(grad_scores, q, DOWN, preferred_element_type=fp32)
                gv = lax.dot_general(probs.astype(bf16), g, DOWN, preferred_element_type=fp32)
                if a == S - 1:
                    gk_ref[...] = gk
                    gv_ref[...] = gv
                else:
                    gk_ref[:upto, :] += gk
                    gv_ref[:upto, :] += gv
            for js in range(S):
                part, k = place(js + 4 * jr)
                at = pl.ds(pl.multiple_of((s ^ js) * n, n), n)
                for i, (ref, factor) in enumerate(((gq_ref, scaling), (gk_ref, scaling), (gv_ref, 1.0))):
                    first = i * width + h * HEAD_DIM
                    low = (ref[at, :] * factor).astype(bf16)
                    outs[part][k * n : (k + 1) * n, first : first + HEAD_DIM] = low
                    sums_ref[0:1, first : first + HEAD_DIM] += jnp.sum(low.astype(fp32), axis=0, keepdims=True)


def pack_kernel(*refs):
    at = 0
    for ref in refs[:-1]:
        refs[-1][:, at : at + ref.shape[1]] = ref[...].astype(bf16)
        at += ref.shape[1]


def unpack_rows_kernel(own_ref, mine_ref, other_ref, out_ref):
    r, n = own_ref[1], mine_ref.shape[0]
    out_ref[pl.ds(pl.multiple_of(r * n, n), n), :] = mine_ref[...].astype(fp32)
    out_ref[pl.ds(pl.multiple_of((r ^ 1) * n, n), n), :] = other_ref[...].astype(fp32)


def unpack_columns_kernel(groups, S, R, own_ref, mine_ref, other_ref, out_ref):
    r = own_ref[1]
    a, c = groups
    width = mine_ref.shape[-1] // (a * c)
    for s in range(S):
        for i in range(a):
            for k in range(c):
                cols = slice((i * c + k) * width, (i * c + k + 1) * width)
                base = ((i * S + s) * c + k) * R
                for ref, at in ((mine_ref, r), (other_ref, r ^ 1)):
                    out_ref[:, pl.ds(pl.multiple_of((base + at) * width, 128), width)] = ref[s, :, cols].astype(fp32)


def small_call(kernel, out_shape, operands, scratch=(), first_rows=(), deps=()):
    specs = []
    for i, v in enumerate(operands):
        if v.dtype == jnp.int32:
            specs.append(SCALARS)
        elif dict(first_rows).get(i, v.shape[0]) != v.shape[0]:
            specs.append(pl.BlockSpec((dict(first_rows)[i], v.shape[1]), lambda g: (0, 0)))
        else:
            specs.append(pl.BlockSpec(v.shape, lambda g, rank=v.ndim: (0,) * rank))
    many = isinstance(out_shape, list)
    outs = out_shape if many else [out_shape]
    out_specs = [pl.BlockSpec(v.shape, lambda g, rank=len(v.shape): (0,) * rank) for v in outs]
    return pl.pallas_call(
        ordered(kernel, len(operands), deps),
        grid=(1,),
        in_specs=specs + [UNREAD] * len(deps),
        out_specs=out_specs if many else out_specs[0],
        out_shape=out_shape,
        scratch_shapes=scratch,
        compiler_params=pltpu.CompilerParams(vmem_limit_bytes=56 * 2**20),
        cost_estimate=LIGHT,
    )(*operands, *deps)


def on_device(
    inputs,
    cotangent,
    norm1_gain,
    norm1_bias,
    w_qkv,
    query_bias,
    value_bias,
    w_attn_out,
    attn_out_bias,
    norm2_gain,
    norm2_bias,
    w_hidden,
    hidden_bias,
    w_output,
    output_bias,
):
    S, Z, R = lax.axis_size("seq"), lax.axis_size("shard"), lax.axis_size("replica")
    s, z, r = lax.axis_index("seq"), lax.axis_index("shard"), lax.axis_index("replica")
    odd = r != 0
    _, n, D = inputs.shape
    rows = norm1_gain.shape[0]
    F = hidden_bias.shape[0] * S * Z
    T = S * R
    hw = D // T
    fw = F // T
    fr = fw // Z
    heads = hw // HEAD_DIM
    grid = (S, Z)
    own = jnp.stack([s, r]).astype(jnp.int32)

    def shape(*dims, kind=bf16):
        return jax.ShapeDtypeStruct(dims, kind)

    def by_shard(v):
        return v if rows % 128 == 0 else v.reshape(-1, S, Z, rows).swapaxes(1, 2).reshape(-1, D)

    def by_seq(v):
        return v if rows % 128 == 0 else v.reshape(-1, Z, S, rows).swapaxes(1, 2).reshape(-1, D)

    x = inputs.reshape(n, D)
    g_low = cotangent.reshape(n, D)
    t = s * R + r
    attn_part = lax.dynamic_index_in_dim(w_attn_out.reshape(rows, R, D // R), r, 1, keepdims=False).astype(bf16)
    small = (norm1_gain, norm1_bias, query_bias, value_bias, attn_out_bias, norm2_gain, norm2_bias, output_bias, hidden_bias)
    attn_part, *small = tie(attn_part, *small)
    attn_part = line_gather(attn_part)
    small = [v.reshape(1, -1) for v in small]
    if rows % 128 == 0:
        table = small_call(pack_kernel, shape(1, sum(v.size for v in small)), small)
    else:
        table = jnp.concatenate([v.astype(bf16) for v in small], axis=1)
    table = gather_table(gather_table(table, "shard"), "seq")
    qkv_pieces = lax.dynamic_index_in_dim(w_qkv.reshape(rows, 3, S, R, hw), r, 3, keepdims=False).astype(bf16)
    qkv_rows = seq_exchange(qkv_pieces.transpose(2, 0, 1, 3).reshape(S, rows, 3 * hw)).reshape(S * rows, 3 * hw)
    hidden_pieces = lax.dynamic_index_in_dim(w_hidden.reshape(rows, S, Z, R, fr), r, 3, keepdims=False).astype(bf16)
    hidden_pieces, qkv_rows = tie(hidden_pieces.transpose(1, 0, 2, 3).reshape(S, rows, fw), qkv_rows)
    qkv_matrix = line_gather(qkv_rows)
    hidden_rows = seq_exchange(hidden_pieces).reshape(S * rows, fw)
    output_part = lax.dynamic_index_in_dim(w_output.reshape(R, fr, D), r, 0, keepdims=False).astype(bf16)

    table = table.astype(fp32)
    gain_one, shift_one, query_shift, value_shift, attn_shift, gain_two, shift_two, output_shift = (
        table[:, i * rows : (i + 1) * rows].reshape(1, D) for i in range(8)
    )
    hidden_shift = lax.dynamic_index_in_dim(
        lax.dynamic_index_in_dim(table[:, 8 * rows :].reshape(S, Z, R, fr), s, 0, keepdims=False), r, 1, keepdims=False
    ).reshape(1, fw)
    bias_row = jnp.concatenate(
        [
            lax.dynamic_slice_in_dim(query_shift[0], t * hw, hw),
            jnp.zeros((hw,), fp32),
            lax.dynamic_slice_in_dim(value_shift[0], t * hw, hw),
        ]
    ).reshape(1, 3 * hw)

    hidden_in = by_shard(
        small_call(lambda *refs: norm_kernel(grid, rows, *refs), shape(n, D), (x, gain_one, shift_one))
    )
    in_near = gather_near(hidden_in)
    hidden_rows, output_part, in_near = tie(hidden_rows, output_part, in_near)
    hidden_matrix = line_gather(hidden_rows)
    output_matrix = line_gather(output_part)
    hidden_in_parts = gather_parts(in_near, gather_diagonal(*in_near))
    hidden_in_parts, attn_part = tie(hidden_in_parts, attn_part)
    attn_near = gather_near(attn_part)
    qkv_parts = [product(v, qkv_matrix, bias=(bias_row,)) for v in hidden_in_parts]
    qkv_parts, attn_near = tie(qkv_parts, attn_near)
    attn_far = gather_diagonal(*attn_near)
    head_block = pltpu.VMEM((S * n, HEAD_DIM), bf16)
    head_sums = pltpu.VMEM((S * n, HEAD_DIM), fp32)
    attended = small_call(
        lambda *refs: attend_kernel(heads, *refs), shape(T, n, hw), (own, *qkv_parts), [head_block] * 3
    )
    attended, attn_far, attn_near = tie(attended, attn_far, attn_near)
    attn_parts = gather_parts(attn_near, attn_far)
    attended = lax.all_to_all(attended, ("seq", "replica"), 0, 0, tiled=True)
    attended, g_low = tie(attended, g_low)
    g_near = gather_near(g_low)
    mid_rows, hidden_two, attended_rel = small_call(
        lambda *refs: mid_kernel(grid, rows, *refs),
        [shape(n, D, kind=fp32), shape(n, D), shape(n, D)],
        (own, attended, *attn_parts, x, attn_shift, gain_two, shift_two),
    )

    two_near = gather_near(by_shard(hidden_two))
    two_near, g_near = tie(two_near, g_near)
    two_diagonal = gather_diagonal(*two_near)
    two_first = jnp.concatenate(two_near)
    up_first = up_product(two_first, hidden_matrix, hidden_shift)
    up_first, two_diagonal = tie(up_first, two_diagonal)
    two_second = jnp.concatenate(two_diagonal)
    hidden_two_parts = (two_first, flip(two_first, CORE), two_second, flip(two_second, CORE))
    two_second, g_near = tie(two_second, g_near)
    g_far = gather_diagonal(*g_near)
    ups = [up_first] + [up_product(v, hidden_matrix, hidden_shift) for v in hidden_two_parts[1:]]
    ups[1:], g_far = tie(ups[1:], g_far)
    activated_parts, slope_parts = zip(*ups)
    g_parts = gather_parts(g_near, g_far)
    grad_output = tall_product(activated_parts, g_parts)
    down = [None] * 4
    down[3] = down_product(g_parts[3], output_matrix, slope_parts[3], hidden_matrix, (grad_output,))
    down[2] = down_product(g_parts[2], output_matrix, slope_parts[2], hidden_matrix, (down[3][0],))
    two_far = far_sum(down[2][1], down[3][1])
    down[1] = down_product(g_parts[1], output_matrix, slope_parts[1], hidden_matrix, (two_far,))
    two_got = flip(down[1][1], CORE)
    down[0] = down_product(g_parts[0], output_matrix, slope_parts[0], hidden_matrix, (down[1][0],))
    grad_pre_parts, grad_two_parts, hidden_sums = zip(*down)
    grad_output = line_scatter(grad_output)
    grad_two = scatter_relay(grad_two_parts[0], two_got, scatter_diagonal(two_far))
    out_parts = [None] * 4
    deps = ()
    for i in (3, 2):
        out_parts[i] = product(activated_parts[i], output_matrix, deps=(grad_two[3], *deps))
        deps = (out_parts[i],)
    grad_hidden = tall_product(hidden_two_parts, grad_pre_parts, deps)
    out_far = far_sum(out_parts[2], out_parts[3])
    grad_two = scatter_last(*grad_two)

    grad_mid, grad_mid_rel, grad_heads, sums_two = small_call(
        lambda *refs: back_mid_kernel(grid, rows, *refs),
        [shape(n, D, kind=fp32), shape(n, D), shape(T, n, hw), shape(8, D, kind=fp32)],
        (own, *map(by_seq, grad_two), mid_rows, g_low, gain_two, *attn_parts),
        first_rows=((1, n), (2, n)),
        deps=(out_far, grad_hidden),
    )
    grad_hidden, grad_mid = tie(grad_hidden, grad_mid)
    grad_hidden = line_scatter(grad_hidden)
    out_parts[1] = product(activated_parts[1], output_matrix, deps=(grad_mid,))
    grad_heads = lax.all_to_all(grad_heads, ("seq", "replica"), 0, 0, tiled=True)
    grad_attn_parts = small_call(
        outer_kernel, [shape(*v.shape) for v in attn_parts], (attended_rel, grad_mid_rel), deps=(out_parts[1],)
    )
    grad_heads, out_theirs, grad_attn_parts, grad_output, out_far = tie(
        grad_heads, out_parts[1], grad_attn_parts, grad_output, out_far
    )
    attn_far = far_sum(grad_attn_parts[2], grad_attn_parts[3])
    out_diagonal = scatter_diagonal_by_row(out_far)
    *grad_qkv_parts, sums_qkv = small_call(
        lambda *refs: attend_back_kernel(heads, *refs),
        [shape(v.shape[0], 3 * hw) for v in qkv_parts] + [shape(8, 3 * hw, kind=fp32)],
        (own, *qkv_parts, grad_heads),
        [head_block] * 3 + [head_sums] * 3,
    )
    other_output = flip(grad_output, COL)
    into = [None] * 4
    into[3] = product(grad_qkv_parts[3], qkv_matrix, ACROSS)
    into[2] = product(grad_qkv_parts[2], qkv_matrix, ACROSS, deps=(into[3], other_output, *out_diagonal))
    into_far = far_sum(into[2], into[3])
    into[1] = product(grad_qkv_parts[1], qkv_matrix, ACROSS, deps=(into_far,))
    into[0] = product(grad_qkv_parts[0], qkv_matrix, ACROSS, deps=(into[1],))
    into_got = flip(into[1], CORE)
    grad_qkv = tall_product(hidden_in_parts, grad_qkv_parts, (into[0],))
    grad_in = scatter_relay(into[0], into_got, scatter_diagonal(into_far))
    *grad_in, grad_qkv = tie(*grad_in, grad_qkv)
    grad_qkv = line_scatter(grad_qkv).reshape(S, rows, 3 * hw)
    attn_far, in_send, attn_theirs = tie(attn_far, grad_in[3], grad_attn_parts[1])
    grad_in[3] = in_send
    attn_diagonal = scatter_diagonal(attn_far)
    attn_got = flip(attn_theirs, CORE)
    grad_attn = scatter_relay(grad_attn_parts[0], attn_got, attn_diagonal)
    attn_send, out_theirs = tie(grad_attn[3], out_theirs)
    grad_attn = (*grad_attn[:3], attn_send)
    out_got = flip(out_theirs, CORE)
    out_parts[0] = product(activated_parts[0], output_matrix, deps=(attn_send,))
    grad_in = scatter_last(*grad_in)
    out_terms = scatter_relay(out_parts[0], out_got, out_diagonal)
    grad_hidden, attn_send = tie(grad_hidden, attn_send)
    grad_attn = scatter_last(*grad_attn[:3], attn_send)
    grad_hidden = seq_exchange(grad_hidden.reshape(S, rows, fw))
    other_hidden = flip(grad_hidden, COL)
    grad_inputs, sums_one = small_call(
        lambda *refs: back_in_kernel(grid, rows, *refs),
        [shape(n, D, kind=fp32), shape(8, D, kind=fp32)],
        (*map(by_seq, grad_in), x, grad_mid, gain_one),
        first_rows=((0, n), (1, n)),
        deps=(attn_send,),
    )
    out_terms = scatter_last(*out_terms)
    sums_one, out_last, other_hidden = tie(sums_one, out_terms[2:], other_hidden)
    out_terms = (*out_terms[:2], *out_last)
    layer_out = small_call(
        out_kernel, shape(n, D), (*out_terms, mid_rows, output_shift), first_rows=((0, n), (1, n))
    )

    def columns_of_both(v, groups, other=None):
        v = v.reshape(-1, rows, v.shape[-1])
        other = flip(v, COL) if other is None else other
        a, c = groups
        count, width = v.shape[0], v.shape[-1] // (a * c)
        if width % 128 == 0:
            return small_call(
                lambda *refs: unpack_columns_kernel(groups, count, R, *refs),
                shape(rows, count * R * v.shape[-1], kind=fp32),
                (own, v, other),
            )
        pair = jnp.stack([jnp.where(odd, other, v), jnp.where(odd, v, other)]).reshape(R, count, rows, a, c, width)
        return pair.transpose(2, 3, 1, 4, 0, 5).reshape(rows, -1).astype(fp32)

    grad_output_matrix = small_call(
        unpack_rows_kernel, shape(R * fr, D, kind=fp32), (own, grad_output, other_output)
    )
    grad_hidden_matrix = columns_of_both(grad_hidden, (1, Z), other_hidden)
    grad_qkv_matrix = columns_of_both(seq_exchange(grad_qkv), (3, 1))
    deep = D // S
    p, q, u, w = (v[:deep].astype(fp32) for v in grad_attn)
    grad_attn = line_scatter((p + q + u + w).astype(bf16))
    grad_attn_matrix = columns_of_both(grad_attn, (1, 1))

    hidden_sums = sum(v[0] for v in hidden_sums).reshape(1, Z, 1, fr)
    hidden_sums = lax.dynamic_update_slice(jnp.zeros((S, Z, R, fr), fp32), hidden_sums, (s, 0, r, 0))
    none = jnp.zeros((D,), fp32)
    sums = total(
        jnp.concatenate(
            [sums_one[i].reshape(S * Z, rows) for i in range(2)]
            + [
                lax.dynamic_update_slice_in_dim(none, sums_qkv[0, i * hw : (i + 1) * hw], t * hw, 0).reshape(S * Z, rows)
                for i in (0, 2)
            ]
            + [sums_two[i].reshape(S * Z, rows) for i in range(4)]
            + [hidden_sums.reshape(S * Z, R * fr)],
            axis=1,
        )
    )
    sums = lax.dynamic_index_in_dim(sums, s * Z + z, 0, keepdims=False)

    def part(i):
        return sums[i * rows : (i + 1) * rows]

    return (
        layer_out.reshape(inputs.shape),
        grad_inputs.reshape(inputs.shape),
        part(0),
        part(1),
        grad_qkv_matrix,
        part(2),
        part(3),
        grad_attn_matrix,
        part(6),
        part(4),
        part(5),
        grad_hidden_matrix,
        sums[8 * rows :],
        grad_output_matrix,
        part(7),
    )


def solution(mesh):
    tokens = P(("shard", "replica"), "seq", None)
    vector = P(("seq", "shard"))
    matrix = P(("seq", "shard"), None)
    weights = (
        vector,
        vector,
        matrix,
        vector,
        vector,
        matrix,
        vector,
        vector,
        vector,
        matrix,
        vector,
        matrix,
        vector,
    )
    return jax.shard_map(
        on_device,
        mesh=mesh,
        in_specs=(tokens, tokens) + weights,
        out_specs=(tokens, tokens) + weights,
        check_vma=False,
    )
```

```python
import jax
import jax.numpy as jnp
from jax import lax
from jax.experimental import pallas as pl
from jax.experimental.pallas import tpu as pltpu
from jax.sharding import PartitionSpec as P

HEAD_DIM = 128
bf16 = jnp.bfloat16
fp32 = jnp.float32

CORE = ("seq", 1)
ROW = ("seq", 2)
COL = ("replica", 1)


PARTS = ((0, 2, 4), (1, 3, 5), (6,), (7,))
ACROSS = (((1,), (1,)), ((), ()))
DOWN = (((0,), (0,)), ((), ()))
WHOLE = pl.BlockSpec(memory_space=pltpu.VMEM)
SCALARS = pl.BlockSpec(memory_space=pltpu.SMEM)


LIGHT = pl.CostEstimate(flops=1, bytes_accessed=1, transcendentals=0)


def place(j):
    return next((i, part.index(j)) for i, part in enumerate(PARTS) if j in part)


def tie(*groups):
    return lax.optimization_barrier(groups)


def ordered(kernel, count, deps):
    return lambda *refs: kernel(*refs[:count], *refs[count + len(deps) :])


UNREAD = pl.BlockSpec(memory_space=pl.ANY)


def flip(v, link):
    axis, bit = link
    return lax.ppermute(v, axis, [(i, i ^ bit) for i in range(lax.axis_size(axis))])


def gather_near(v):
    return v, flip(v, ROW), flip(v, COL)


def gather_diagonal(v, py, px):
    h = v.shape[0] // 2
    return flip(py[:h], COL), flip(px[h:], ROW)


def gather_parts(near, diagonal):
    first, second = jnp.concatenate(near), jnp.concatenate(diagonal)
    return first, flip(first, CORE), second, flip(second, CORE)


def relay_kernel(y_ref, gy_ref, x_ref, gx_ref, ra_ref, rb_ref, ys_ref, xs_ref):
    h = ra_ref.shape[0]
    top, bot = slice(0, h), slice(h, 2 * h)
    ys_ref[top, :] = (
        y_ref[top, :].astype(fp32) + gy_ref[top, :].astype(fp32) + ra_ref[...].astype(fp32)
    ).astype(bf16)
    ys_ref[bot, :] = (y_ref[bot, :].astype(fp32) + gy_ref[bot, :].astype(fp32)).astype(bf16)
    xs_ref[top, :] = (x_ref[top, :].astype(fp32) + gx_ref[top, :].astype(fp32)).astype(bf16)
    xs_ref[bot, :] = (
        x_ref[bot, :].astype(fp32) + gx_ref[bot, :].astype(fp32) + rb_ref[...].astype(fp32)
    ).astype(bf16)


def relay_by_row_kernel(y_ref, gy_ref, x_ref, gx_ref, rb_ref, ys_ref, xs_ref):
    ys_ref[...] = (y_ref[...].astype(fp32) + gy_ref[...].astype(fp32)).astype(bf16)
    xs_ref[...] = (x_ref[...].astype(fp32) + gx_ref[...].astype(fp32) + rb_ref[...].astype(fp32)).astype(bf16)


def far_sum(far, far_theirs):
    return (far.astype(fp32) + flip(far_theirs, CORE).astype(fp32)).astype(bf16)


def scatter_diagonal(far):
    h = far.shape[0] // 2
    return flip(far[:h], COL), flip(far[h:], ROW)


def scatter_diagonal_by_row(far):
    return (flip(far, ROW),)


def scatter_relay(mine, got, diagonal, deps=()):
    width = diagonal[0].shape[1]
    n = sum(v.shape[0] for v in diagonal)

    def rows(i):
        return pl.BlockSpec((n, width), lambda g: (i, 0))

    diagonal_specs = [pl.BlockSpec(v.shape, lambda g: (0, 0)) for v in diagonal]
    y_send, x_send = pl.pallas_call(
        ordered(relay_kernel if len(diagonal) == 2 else relay_by_row_kernel, 4 + len(diagonal), deps),
        grid=(1,),
        in_specs=[rows(1), rows(1), rows(2), rows(2), *diagonal_specs] + [UNREAD] * len(deps),
        out_specs=[rows(0), rows(0)],
        out_shape=[jax.ShapeDtypeStruct((n, width), bf16)] * 2,
        compiler_params=pltpu.CompilerParams(vmem_limit_bytes=40 * 2**20),
        cost_estimate=LIGHT,
    )(mine, got, mine, got, *diagonal, *deps)
    return mine, got, y_send, x_send


def scatter_last(mine, got, y_send, x_send):
    return mine, got, flip(y_send, ROW), flip(x_send, COL)


def line_gather(v):
    return lax.all_gather(v, "shard", axis=0, tiled=True)


def line_scatter(v):
    return lax.psum_scatter(v, "shard", scatter_dimension=0, tiled=True)


def seq_exchange(v):
    return lax.all_to_all(v, "seq", 0, 0, tiled=True)


def gather_table(table, axis):
    index, bit = lax.axis_index(axis), 1
    while bit < lax.axis_size(axis):
        other = flip(table, (axis, bit))
        odd = (index & bit) != 0
        table = jnp.concatenate([jnp.where(odd, other, table), jnp.where(odd, table, other)])
        bit *= 2
    return table


def total(v):
    for axis in ("shard", "seq", "replica"):
        bit = 1
        while bit < lax.axis_size(axis):
            v = v + flip(v, (axis, bit))
            bit *= 2
    return v


def row_loop(n):
    step = 128 if n % 128 == 0 else n
    return pl.loop(0, n, step=step), step


def statistics(v):
    centred = v - jnp.mean(v, axis=1, keepdims=True)
    scale = lax.rsqrt(jnp.mean(centred * centred, axis=1, keepdims=True) + 1e-05)
    return centred * scale, scale


def norm_back(grad, normed, scale):
    first = jnp.mean(grad, axis=1, keepdims=True)
    second = jnp.mean(grad * normed, axis=1, keepdims=True)
    return scale * (grad - first - normed * second)


def transposed_columns(v, grid, rows):
    a, b = grid
    if rows % 128 or a == 1 or b == 1:
        return v
    return jnp.concatenate(
        [v[:, (i * b + k) * rows : (i * b + k + 1) * rows] for k in range(b) for i in range(a)], axis=1
    )


def norm_kernel(grid, rows, x_ref, gain_ref, shift_ref, out_ref):
    loop, step = row_loop(x_ref.shape[0])

    @loop
    def _(i):
        at = pl.ds(pl.multiple_of(i, step), step)
        normed, _ = statistics(x_ref[at, :].astype(fp32))
        hidden = (normed * gain_ref[...] + shift_ref[...]).astype(bf16)
        out_ref[at, :] = transposed_columns(hidden, grid, rows)


def mid_kernel(
    grid, rows, own_ref, att_ref, a_ref, b_ref, c_ref, d_ref, x_ref, bias_ref, gain_ref, shift_ref,
    mid_ref, hidden_ref, rel_ref,
):
    S = grid[0]
    T, n, hw = att_ref.shape
    R = T // S
    s, r = own_ref[0], own_ref[1]
    parts = (a_ref, b_ref, c_ref, d_ref)
    deep, wide = d_ref.shape
    for js in range(S):
        for i in range(R):
            rel_ref[:, (js * R + i) * hw : (js * R + i + 1) * hw] = att_ref[(s ^ js) * R + i]
    for jr in range(R):
        acc = jnp.zeros((n, wide), fp32)
        for js in range(S):
            part, k = place(js + 4 * jr)
            acc += jnp.dot(
                rel_ref[:, js * deep : (js + 1) * deep],
                parts[part][k * deep : (k + 1) * deep, :],
                preferred_element_type=fp32,
            )
        mid_ref[:, pl.ds(pl.multiple_of((r ^ jr) * wide, 128), wide)] = acc
    loop, step = row_loop(n)

    @loop
    def _(i):
        at = pl.ds(pl.multiple_of(i, step), step)
        mid = x_ref[at, :].astype(fp32) + (mid_ref[at, :] + bias_ref[...])
        mid_ref[at, :] = mid
        normed, _ = statistics(mid)
        hidden = (normed * gain_ref[...] + shift_ref[...]).astype(bf16)
        hidden_ref[at, :] = transposed_columns(hidden, grid, rows)


def back_mid_kernel(
    grid, rows, own_ref, p_ref, q_ref, u_ref, w_ref, mid_ref, g_ref, gain_ref, a_ref, b_ref, c_ref, d_ref,
    grad_ref, rel_ref, att_ref, sums_ref,
):
    S = grid[0]
    T, n, hw = att_ref.shape
    R = T // S
    s, r = own_ref[0], own_ref[1]
    parts = (a_ref, b_ref, c_ref, d_ref)
    deep, wide = d_ref.shape
    sums_ref[...] = jnp.zeros_like(sums_ref)
    loop, step = row_loop(n)

    @loop
    def _(i):
        at = pl.ds(pl.multiple_of(i, step), step)
        grad = p_ref[at, :].astype(fp32) + q_ref[at, :].astype(fp32)
        grad += u_ref[at, :].astype(fp32) + w_ref[at, :].astype(fp32)
        grad = transposed_columns(grad, grid[::-1], rows)
        normed, scale = statistics(mid_ref[at, :])
        g = g_ref[at, :].astype(fp32)
        sums_ref[0:1, :] += jnp.sum(grad * normed, axis=0, keepdims=True)
        sums_ref[1:2, :] += jnp.sum(grad, axis=0, keepdims=True)
        grad_mid = g + norm_back(grad * gain_ref[...], normed, scale)
        grad_ref[at, :] = grad_mid
        low = grad_mid.astype(bf16)
        sums_ref[2:3, :] += jnp.sum(low.astype(fp32), axis=0, keepdims=True)
        sums_ref[3:4, :] += jnp.sum(g, axis=0, keepdims=True)
        for k in range(R):
            rel_ref[at, pl.ds(pl.multiple_of((r ^ k) * wide, 128), wide)] = low[:, k * wide : (k + 1) * wide]

    for js in range(S):
        acc = jnp.zeros((n, deep), fp32)
        for jr in range(R):
            part, k = place(js + 4 * jr)
            acc += lax.dot_general(
                rel_ref[:, jr * wide : (jr + 1) * wide],
                parts[part][k * deep : (k + 1) * deep, :],
                ACROSS,
                preferred_element_type=fp32,
            )
        for i in range(R):
            att_ref[(s ^ js) * R + i] = acc[:, i * hw : (i + 1) * hw].astype(bf16)


def back_in_kernel(grid, rows, p_ref, q_ref, u_ref, w_ref, x_ref, g_ref, gain_ref, out_ref, sums_ref):
    sums_ref[...] = jnp.zeros_like(sums_ref)
    loop, step = row_loop(x_ref.shape[0])

    @loop
    def _(i):
        at = pl.ds(pl.multiple_of(i, step), step)
        grad = p_ref[at, :].astype(fp32) + q_ref[at, :].astype(fp32)
        grad += u_ref[at, :].astype(fp32) + w_ref[at, :].astype(fp32)
        grad = transposed_columns(grad, grid[::-1], rows)
        normed, scale = statistics(x_ref[at, :].astype(fp32))
        sums_ref[0:1, :] += jnp.sum(grad * normed, axis=0, keepdims=True)
        sums_ref[1:2, :] += jnp.sum(grad, axis=0, keepdims=True)
        out_ref[at, :] = g_ref[at, :] + norm_back(grad * gain_ref[...], normed, scale)


def out_kernel(p_ref, q_ref, u_ref, w_ref, mid_ref, bias_ref, out_ref):
    loop, step = row_loop(mid_ref.shape[0])

    @loop
    def _(i):
        at = pl.ds(pl.multiple_of(i, step), step)
        term = p_ref[at, :].astype(fp32) + q_ref[at, :].astype(fp32)
        term += u_ref[at, :].astype(fp32) + w_ref[at, :].astype(fp32)
        out_ref[at, :] = (mid_ref[at, :] + (term + bias_ref[...])).astype(bf16)


def outer_kernel(rel_ref, low_ref, *outs):
    deep, wide = outs[3].shape
    for out_ref, part in zip(outs, PARTS):
        for k, j in enumerate(part):
            js, jr = j & 3, j >> 2
            out_ref[k * deep : (k + 1) * deep, :] = lax.dot_general(
                rel_ref[:, js * deep : (js + 1) * deep],
                low_ref[:, jr * wide : (jr + 1) * wide],
                DOWN,
                preferred_element_type=fp32,
            ).astype(bf16)


def tall_kernel(*refs):
    half = len(refs) // 2
    acc = 0.0
    for left, right in zip(refs[:half], refs[half:-1]):
        acc += lax.dot_general(left[...], right[...], DOWN, preferred_element_type=fp32)
    refs[-1][...] = acc.astype(bf16)


def tall_product(lefts, rights, deps=()):
    deep, wide = lefts[0].shape[1], rights[0].shape[1]
    tokens = sum(v.shape[0] for v in lefts)
    tile = min(256, deep)
    return pl.pallas_call(
        ordered(tall_kernel, 2 * len(lefts), deps),
        grid=(deep // tile,),
        in_specs=[pl.BlockSpec((v.shape[0], tile), lambda i: (0, i)) for v in lefts]
        + [pl.BlockSpec(v.shape, lambda i: (0, 0)) for v in rights]
        + [UNREAD] * len(deps),
        out_specs=pl.BlockSpec((tile, wide), lambda i: (i, 0)),
        out_shape=jax.ShapeDtypeStruct((deep, wide), bf16),
        compiler_params=pltpu.CompilerParams(vmem_limit_bytes=48 * 2**20),
        cost_estimate=LIGHT,
    )(*lefts, *rights, *deps)


def up_kernel(h_ref, w_ref, bias_ref, act_ref, slope_ref):
    u = jnp.dot(h_ref[...], w_ref[...], preferred_element_type=fp32) + bias_ref[...]
    cdf = 0.5 * (1.0 + lax.erf(u * 0.7071067811865476))
    act_ref[...] = (u * cdf).astype(bf16)
    slope_ref[...] = cdf + u * jnp.exp(-0.5 * u * u) * 0.3989422804014327


def up_product(h, w, bias):
    tile = min(256, h.shape[0])
    deep, wide = w.shape
    return pl.pallas_call(
        up_kernel,
        grid=(h.shape[0] // tile,),
        in_specs=[
            pl.BlockSpec((tile, deep), lambda i: (i, 0)),
            pl.BlockSpec((deep, wide), lambda i: (0, 0)),
            pl.BlockSpec((1, wide), lambda i: (0, 0)),
        ],
        out_specs=[pl.BlockSpec((tile, wide), lambda i: (i, 0))] * 2,
        out_shape=[jax.ShapeDtypeStruct((h.shape[0], wide), kind) for kind in (bf16, fp32)],
        compiler_params=pltpu.CompilerParams(vmem_limit_bytes=48 * 2**20),
        cost_estimate=LIGHT,
    )(h, w, bias)


def product_kernel(dims, *refs):
    term = lax.dot_general(refs[0][...], refs[1][...], dims, preferred_element_type=fp32)
    refs[-1][...] = (term + refs[2][...] if len(refs) == 4 else term).astype(bf16)


def product(v, w, dims=(((1,), (0,)), ((), ())), bias=(), deps=()):
    tile = min(256, v.shape[0])
    wide = w.shape[1 - dims[0][1][0]]
    return pl.pallas_call(
        ordered(lambda *refs: product_kernel(dims, *refs), 2 + len(bias), deps),
        grid=(v.shape[0] // tile,),
        in_specs=[pl.BlockSpec((tile, v.shape[1]), lambda i: (i, 0)), pl.BlockSpec(w.shape, lambda i: (0, 0))]
        + [pl.BlockSpec((1, wide), lambda i: (0, 0))] * len(bias)
        + [UNREAD] * len(deps),
        out_specs=pl.BlockSpec((tile, wide), lambda i: (i, 0)),
        out_shape=jax.ShapeDtypeStruct((v.shape[0], wide), bf16),
        compiler_params=pltpu.CompilerParams(vmem_limit_bytes=48 * 2**20),
        cost_estimate=LIGHT,
    )(v, w, *bias, *deps)


def down_kernel(g_ref, out_w_ref, slope_ref, up_w_ref, pre_ref, two_ref, sums_ref):
    grad = lax.dot_general(g_ref[...], out_w_ref[...], ACROSS, preferred_element_type=fp32)
    low = (grad * slope_ref[...]).astype(bf16)
    pre_ref[...] = low
    two_ref[...] = lax.dot_general(low, up_w_ref[...], ACROSS, preferred_element_type=fp32).astype(bf16)

    @pl.when(pl.program_id(0) == 0)
    def _():
        sums_ref[...] = jnp.zeros_like(sums_ref)

    sums_ref[0:1, :] += jnp.sum(low.astype(fp32), axis=0, keepdims=True)


def down_product(g, out_w, slope, up_w, deps=()):
    tile = min(256, g.shape[0])
    wide, deep = out_w.shape
    tokens = g.shape[0]

    def tiles(width):
        return pl.BlockSpec((tile, width), lambda i: (i, 0))

    def whole(a, b):
        return pl.BlockSpec((a, b), lambda i: (0, 0))

    return pl.pallas_call(
        ordered(down_kernel, 4, deps),
        grid=(tokens // tile,),
        in_specs=[tiles(deep), whole(wide, deep), tiles(wide), whole(deep, wide)] + [UNREAD] * len(deps),
        out_specs=[tiles(wide), tiles(deep), whole(8, wide)],
        out_shape=[
            jax.ShapeDtypeStruct((tokens, wide), bf16),
            jax.ShapeDtypeStruct((tokens, deep), bf16),
            jax.ShapeDtypeStruct((8, wide), fp32),
        ],
        compiler_params=pltpu.CompilerParams(vmem_limit_bytes=48 * 2**20),
        cost_estimate=LIGHT,
    )(g, out_w, slope, up_w, *deps)


def attend_kernel(heads, own_ref, a_ref, b_ref, c_ref, d_ref, out_ref, q_ref, k_ref, v_ref):
    s, r = own_ref[0], own_ref[1]
    T, n, width = out_ref.shape
    S = q_ref.shape[0] // n
    parts = (a_ref, b_ref, c_ref, d_ref)
    for jr in range(T // S):
        for h in range(heads):
            cols = slice(h * HEAD_DIM, (h + 1) * HEAD_DIM)
            for js in range(S):
                part, k = place(js + 4 * jr)
                at = pl.ds(pl.multiple_of((s ^ js) * n, n), n)
                for i, ref in enumerate((q_ref, k_ref, v_ref)):
                    first = i * width + h * HEAD_DIM
                    ref[at, :] = parts[part][k * n : (k + 1) * n, first : first + HEAD_DIM]
            for a in range(S):
                upto = (a + 1) * n
                q = q_ref[a * n : upto, :]
                scores = lax.dot_general(q, k_ref[:upto, :], ACROSS, preferred_element_type=fp32)
                expons = jnp.exp((scores - jnp.max(scores, axis=-1, keepdims=True)) * HEAD_DIM ** (-0.5))
                probs = (expons * (1.0 / jnp.sum(expons, axis=-1, keepdims=True))).astype(bf16)
                out_ref[a * (T // S) + (r ^ jr), :, cols] = jnp.dot(
                    probs, v_ref[:upto, :], preferred_element_type=fp32
                ).astype(bf16)


def attend_back_kernel(
    heads, own_ref, a_ref, b_ref, c_ref, d_ref, grad_ref, oa_ref, ob_ref, oc_ref, od_ref, sums_ref,
    q_ref, k_ref, v_ref, gq_ref, gk_ref, gv_ref,
):
    s, r = own_ref[0], own_ref[1]
    T, n, width = grad_ref.shape
    S = q_ref.shape[0] // n
    parts = (a_ref, b_ref, c_ref, d_ref)
    outs = (oa_ref, ob_ref, oc_ref, od_ref)
    scaling = HEAD_DIM ** (-0.5)
    sums_ref[...] = jnp.zeros_like(sums_ref)
    for jr in range(T // S):
        for h in range(heads):
            cols = slice(h * HEAD_DIM, (h + 1) * HEAD_DIM)
            for js in range(S):
                part, k = place(js + 4 * jr)
                at = pl.ds(pl.multiple_of((s ^ js) * n, n), n)
                for i, ref in enumerate((q_ref, k_ref, v_ref)):
                    first = i * width + h * HEAD_DIM
                    ref[at, :] = parts[part][k * n : (k + 1) * n, first : first + HEAD_DIM]
            for a in reversed(range(S)):
                upto = (a + 1) * n
                q = q_ref[a * n : upto, :]
                g = grad_ref[a * (T // S) + (r ^ jr), :, cols]
                k = k_ref[:upto, :]
                v = v_ref[:upto, :]
                scores = lax.dot_general(q, k, ACROSS, preferred_element_type=fp32)
                expons = jnp.exp((scores - jnp.max(scores, axis=-1, keepdims=True)) * scaling)
                probs = expons * (1.0 / jnp.sum(expons, axis=-1, keepdims=True))
                grad_probs = lax.dot_general(g, v, ACROSS, preferred_element_type=fp32)
                inner = jnp.sum(probs * grad_probs, axis=-1, keepdims=True)
                grad_scores = (probs * (grad_probs - inner)).astype(bf16)
                gq_ref[a * n : upto, :] = jnp.dot(grad_scores, k, preferred_element_type=fp32)
                gk = lax.dot_general(grad_scores, q, DOWN, preferred_element_type=fp32)
                gv = lax.dot_general(probs.astype(bf16), g, DOWN, preferred_element_type=fp32)
                if a == S - 1:
                    gk_ref[...] = gk
                    gv_ref[...] = gv
                else:
                    gk_ref[:upto, :] += gk
                    gv_ref[:upto, :] += gv
            for js in range(S):
                part, k = place(js + 4 * jr)
                at = pl.ds(pl.multiple_of((s ^ js) * n, n), n)
                for i, (ref, factor) in enumerate(((gq_ref, scaling), (gk_ref, scaling), (gv_ref, 1.0))):
                    first = i * width + h * HEAD_DIM
                    low = (ref[at, :] * factor).astype(bf16)
                    outs[part][k * n : (k + 1) * n, first : first + HEAD_DIM] = low
                    sums_ref[0:1, first : first + HEAD_DIM] += jnp.sum(low.astype(fp32), axis=0, keepdims=True)


def pack_kernel(*refs):
    at = 0
    for ref in refs[:-1]:
        refs[-1][:, at : at + ref.shape[1]] = ref[...].astype(bf16)
        at += ref.shape[1]


def unpack_rows_kernel(own_ref, mine_ref, other_ref, out_ref):
    r, n = own_ref[1], mine_ref.shape[0]
    out_ref[pl.ds(pl.multiple_of(r * n, n), n), :] = mine_ref[...].astype(fp32)
    out_ref[pl.ds(pl.multiple_of((r ^ 1) * n, n), n), :] = other_ref[...].astype(fp32)


def unpack_columns_kernel(groups, S, R, own_ref, mine_ref, other_ref, out_ref):
    r = own_ref[1]
    a, c = groups
    width = mine_ref.shape[-1] // (a * c)
    for s in range(S):
        for i in range(a):
            for k in range(c):
                cols = slice((i * c + k) * width, (i * c + k + 1) * width)
                base = ((i * S + s) * c + k) * R
                for ref, at in ((mine_ref, r), (other_ref, r ^ 1)):
                    out_ref[:, pl.ds(pl.multiple_of((base + at) * width, 128), width)] = ref[s, :, cols].astype(fp32)


def small_call(kernel, out_shape, operands, scratch=(), first_rows=(), deps=()):
    specs = []
    for i, v in enumerate(operands):
        if v.dtype == jnp.int32:
            specs.append(SCALARS)
        elif dict(first_rows).get(i, v.shape[0]) != v.shape[0]:
            specs.append(pl.BlockSpec((dict(first_rows)[i], v.shape[1]), lambda g: (0, 0)))
        else:
            specs.append(pl.BlockSpec(v.shape, lambda g, rank=v.ndim: (0,) * rank))
    many = isinstance(out_shape, list)
    outs = out_shape if many else [out_shape]
    out_specs = [pl.BlockSpec(v.shape, lambda g, rank=len(v.shape): (0,) * rank) for v in outs]
    return pl.pallas_call(
        ordered(kernel, len(operands), deps),
        grid=(1,),
        in_specs=specs + [UNREAD] * len(deps),
        out_specs=out_specs if many else out_specs[0],
        out_shape=out_shape,
        scratch_shapes=scratch,
        compiler_params=pltpu.CompilerParams(vmem_limit_bytes=56 * 2**20),
        cost_estimate=LIGHT,
    )(*operands, *deps)


def on_device(
    inputs,
    cotangent,
    norm1_gain,
    norm1_bias,
    w_qkv,
    query_bias,
    value_bias,
    w_attn_out,
    attn_out_bias,
    norm2_gain,
    norm2_bias,
    w_hidden,
    hidden_bias,
    w_output,
    output_bias,
):
    S, Z, R = lax.axis_size("seq"), lax.axis_size("shard"), lax.axis_size("replica")
    s, z, r = lax.axis_index("seq"), lax.axis_index("shard"), lax.axis_index("replica")
    odd = r != 0
    _, n, D = inputs.shape
    rows = norm1_gain.shape[0]
    F = hidden_bias.shape[0] * S * Z
    T = S * R
    hw = D // T
    fw = F // T
    fr = fw // Z
    heads = hw // HEAD_DIM
    grid = (S, Z)
    own = jnp.stack([s, r]).astype(jnp.int32)

    def shape(*dims, kind=bf16):
        return jax.ShapeDtypeStruct(dims, kind)

    def by_shard(v):
        return v if rows % 128 == 0 else v.reshape(-1, S, Z, rows).swapaxes(1, 2).reshape(-1, D)

    def by_seq(v):
        return v if rows % 128 == 0 else v.reshape(-1, Z, S, rows).swapaxes(1, 2).reshape(-1, D)

    x = inputs.reshape(n, D)
    g_low = cotangent.reshape(n, D)
    t = s * R + r
    attn_part = lax.dynamic_index_in_dim(w_attn_out.reshape(rows, R, D // R), r, 1, keepdims=False).astype(bf16)
    small = (norm1_gain, norm1_bias, query_bias, value_bias, attn_out_bias, norm2_gain, norm2_bias, output_bias, hidden_bias)
    attn_part, *small = tie(attn_part, *small)
    attn_part = line_gather(attn_part)
    small = [v.reshape(1, -1) for v in small]
    if rows % 128 == 0:
        table = small_call(pack_kernel, shape(1, sum(v.size for v in small)), small)
    else:
        table = jnp.concatenate([v.astype(bf16) for v in small], axis=1)
    table = gather_table(gather_table(table, "shard"), "seq")
    qkv_pieces = lax.dynamic_index_in_dim(w_qkv.reshape(rows, 3, S, R, hw), r, 3, keepdims=False).astype(bf16)
    qkv_rows = seq_exchange(qkv_pieces.transpose(2, 0, 1, 3).reshape(S, rows, 3 * hw)).reshape(S * rows, 3 * hw)
    hidden_pieces = lax.dynamic_index_in_dim(w_hidden.reshape(rows, S, Z, R, fr), r, 3, keepdims=False).astype(bf16)
    hidden_pieces, qkv_rows = tie(hidden_pieces.transpose(1, 0, 2, 3).reshape(S, rows, fw), qkv_rows)
    qkv_matrix = line_gather(qkv_rows)
    hidden_rows = seq_exchange(hidden_pieces).reshape(S * rows, fw)
    output_part = lax.dynamic_index_in_dim(w_output.reshape(R, fr, D), r, 0, keepdims=False).astype(bf16)

    table = table.astype(fp32)
    gain_one, shift_one, query_shift, value_shift, attn_shift, gain_two, shift_two, output_shift = (
        table[:, i * rows : (i + 1) * rows].reshape(1, D) for i in range(8)
    )
    hidden_shift = lax.dynamic_index_in_dim(
        lax.dynamic_index_in_dim(table[:, 8 * rows :].reshape(S, Z, R, fr), s, 0, keepdims=False), r, 1, keepdims=False
    ).reshape(1, fw)
    bias_row = jnp.concatenate(
        [
            lax.dynamic_slice_in_dim(query_shift[0], t * hw, hw),
            jnp.zeros((hw,), fp32),
            lax.dynamic_slice_in_dim(value_shift[0], t * hw, hw),
        ]
    ).reshape(1, 3 * hw)

    hidden_in = by_shard(
        small_call(lambda *refs: norm_kernel(grid, rows, *refs), shape(n, D), (x, gain_one, shift_one))
    )
    in_near = gather_near(hidden_in)
    hidden_rows, output_part, in_near = tie(hidden_rows, output_part, in_near)
    hidden_matrix = line_gather(hidden_rows)
    output_matrix = line_gather(output_part)
    hidden_in_parts = gather_parts(in_near, gather_diagonal(*in_near))
    hidden_in_parts, attn_part = tie(hidden_in_parts, attn_part)
    attn_near = gather_near(attn_part)
    qkv_parts = [product(v, qkv_matrix, bias=(bias_row,)) for v in hidden_in_parts]
    qkv_parts, attn_near = tie(qkv_parts, attn_near)
    attn_far = gather_diagonal(*attn_near)
    head_block = pltpu.VMEM((S * n, HEAD_DIM), bf16)
    head_sums = pltpu.VMEM((S * n, HEAD_DIM), fp32)
    attended = small_call(
        lambda *refs: attend_kernel(heads, *refs), shape(T, n, hw), (own, *qkv_parts), [head_block] * 3
    )
    attended, attn_far, attn_near = tie(attended, attn_far, attn_near)
    attn_parts = gather_parts(attn_near, attn_far)
    attended = lax.all_to_all(attended, ("seq", "replica"), 0, 0, tiled=True)
    attended, g_low = tie(attended, g_low)
    g_near = gather_near(g_low)
    mid_rows, hidden_two, attended_rel = small_call(
        lambda *refs: mid_kernel(grid, rows, *refs),
        [shape(n, D, kind=fp32), shape(n, D), shape(n, D)],
        (own, attended, *attn_parts, x, attn_shift, gain_two, shift_two),
    )

    two_near = gather_near(by_shard(hidden_two))
    two_near, g_near = tie(two_near, g_near)
    two_diagonal = gather_diagonal(*two_near)
    two_first = jnp.concatenate(two_near)
    up_first = up_product(two_first, hidden_matrix, hidden_shift)
    up_first, two_diagonal = tie(up_first, two_diagonal)
    two_second = jnp.concatenate(two_diagonal)
    hidden_two_parts = (two_first, flip(two_first, CORE), two_second, flip(two_second, CORE))
    two_second, g_near = tie(two_second, g_near)
    g_far = gather_diagonal(*g_near)
    ups = [up_first] + [up_product(v, hidden_matrix, hidden_shift) for v in hidden_two_parts[1:]]
    ups[1:], g_far = tie(ups[1:], g_far)
    activated_parts, slope_parts = zip(*ups)
    g_parts = gather_parts(g_near, g_far)
    grad_output = tall_product(activated_parts, g_parts)
    down = [None] * 4
    down[3] = down_product(g_parts[3], output_matrix, slope_parts[3], hidden_matrix, (grad_output,))
    down[2] = down_product(g_parts[2], output_matrix, slope_parts[2], hidden_matrix, (down[3][0],))
    two_far = far_sum(down[2][1], down[3][1])
    down[1] = down_product(g_parts[1], output_matrix, slope_parts[1], hidden_matrix, (two_far,))
    two_got = flip(down[1][1], CORE)
    down[0] = down_product(g_parts[0], output_matrix, slope_parts[0], hidden_matrix, (down[1][0],))
    grad_pre_parts, grad_two_parts, hidden_sums = zip(*down)
    grad_output = line_scatter(grad_output)
    grad_two = scatter_relay(grad_two_parts[0], two_got, scatter_diagonal(two_far))
    out_parts = [None] * 4
    deps = ()
    for i in (3, 2):
        out_parts[i] = product(activated_parts[i], output_matrix, deps=(grad_two[3], *deps))
        deps = (out_parts[i],)
    grad_hidden = tall_product(hidden_two_parts, grad_pre_parts, deps)
    out_far = far_sum(out_parts[2], out_parts[3])
    grad_two = scatter_last(*grad_two)

    grad_mid, grad_mid_rel, grad_heads, sums_two = small_call(
        lambda *refs: back_mid_kernel(grid, rows, *refs),
        [shape(n, D, kind=fp32), shape(n, D), shape(T, n, hw), shape(8, D, kind=fp32)],
        (own, *map(by_seq, grad_two), mid_rows, g_low, gain_two, *attn_parts),
        first_rows=((1, n), (2, n)),
        deps=(out_far, grad_hidden),
    )
    grad_hidden, grad_mid = tie(grad_hidden, grad_mid)
    grad_hidden = line_scatter(grad_hidden)
    out_parts[1] = product(activated_parts[1], output_matrix, deps=(grad_mid,))
    out_parts[0] = product(activated_parts[0], output_matrix, deps=(grad_mid,))
    grad_heads = lax.all_to_all(grad_heads, ("seq", "replica"), 0, 0, tiled=True)
    grad_heads, out_theirs, out_mine, grad_output, out_far = tie(
        grad_heads, out_parts[1], out_parts[0], grad_output, out_far
    )
    out_diagonal = scatter_diagonal_by_row(out_far)
    *grad_qkv_parts, sums_qkv = small_call(
        lambda *refs: attend_back_kernel(heads, *refs),
        [shape(v.shape[0], 3 * hw) for v in qkv_parts] + [shape(8, 3 * hw, kind=fp32)],
        (own, *qkv_parts, grad_heads),
        [head_block] * 3 + [head_sums] * 3,
    )
    out_got = flip(out_theirs, CORE)
    other_output = flip(grad_output, COL)
    into = [None] * 4
    into[3] = product(grad_qkv_parts[3], qkv_matrix, ACROSS)
    into[2] = product(grad_qkv_parts[2], qkv_matrix, ACROSS, deps=(into[3], other_output, *out_diagonal))
    out_terms = scatter_relay(out_mine, out_got, out_diagonal, deps=(into[2],))
    into_far = far_sum(into[2], into[3])
    into[1] = product(grad_qkv_parts[1], qkv_matrix, ACROSS, deps=(into_far, out_terms[3]))
    into[0] = product(grad_qkv_parts[0], qkv_matrix, ACROSS, deps=(into[1],))
    into_got = flip(into[1], CORE)
    grad_attn_parts = small_call(
        outer_kernel, [shape(*v.shape) for v in attn_parts], (attended_rel, grad_mid_rel), deps=(into[0],)
    )
    grad_in = scatter_relay(into[0], into_got, scatter_diagonal(into_far), deps=(grad_attn_parts[0],))
    grad_qkv = tall_product(hidden_in_parts, grad_qkv_parts, (grad_in[3],))
    attn_got = flip(grad_attn_parts[1], CORE)
    attn_far = far_sum(grad_attn_parts[2], grad_attn_parts[3])
    attn_far, grad_qkv = tie(attn_far, grad_qkv)
    grad_qkv = line_scatter(grad_qkv).reshape(S, rows, 3 * hw)
    attn_diagonal = scatter_diagonal(attn_far)
    grad_attn = scatter_relay(grad_attn_parts[0], attn_got, attn_diagonal)
    grad_hidden, in_send = tie(grad_hidden, grad_in[3])
    grad_in = scatter_last(*grad_in[:3], in_send)
    grad_hidden = seq_exchange(grad_hidden.reshape(S, rows, fw))
    grad_hidden, attn_send = tie(grad_hidden, grad_attn[3])
    grad_attn = scatter_last(*grad_attn[:3], attn_send)
    other_hidden = flip(grad_hidden, COL)
    grad_inputs, sums_one = small_call(
        lambda *refs: back_in_kernel(grid, rows, *refs),
        [shape(n, D, kind=fp32), shape(8, D, kind=fp32)],
        (*map(by_seq, grad_in), x, grad_mid, gain_one),
        first_rows=((0, n), (1, n)),
        deps=(attn_send,),
    )
    out_terms = scatter_last(*out_terms)
    layer_out = small_call(
        out_kernel, shape(n, D), (*out_terms, mid_rows, output_shift), first_rows=((0, n), (1, n))
    )

    def columns_of_both(v, groups, other=None):
        v = v.reshape(-1, rows, v.shape[-1])
        other = flip(v, COL) if other is None else other
        a, c = groups
        count, width = v.shape[0], v.shape[-1] // (a * c)
        if width % 128 == 0:
            return small_call(
                lambda *refs: unpack_columns_kernel(groups, count, R, *refs),
                shape(rows, count * R * v.shape[-1], kind=fp32),
                (own, v, other),
            )
        pair = jnp.stack([jnp.where(odd, other, v), jnp.where(odd, v, other)]).reshape(R, count, rows, a, c, width)
        return pair.transpose(2, 3, 1, 4, 0, 5).reshape(rows, -1).astype(fp32)

    grad_output_matrix = small_call(
        unpack_rows_kernel, shape(R * fr, D, kind=fp32), (own, grad_output, other_output)
    )
    grad_hidden_matrix = columns_of_both(grad_hidden, (1, Z), other_hidden)
    grad_qkv_matrix = columns_of_both(seq_exchange(grad_qkv), (3, 1))
    deep = D // S
    p, q, u, w = (v[:deep].astype(fp32) for v in grad_attn)
    grad_attn = line_scatter((p + q + u + w).astype(bf16))
    grad_attn_matrix = columns_of_both(grad_attn, (1, 1))

    hidden_sums = sum(v[0] for v in hidden_sums).reshape(1, Z, 1, fr)
    hidden_sums = lax.dynamic_update_slice(jnp.zeros((S, Z, R, fr), fp32), hidden_sums, (s, 0, r, 0))
    none = jnp.zeros((D,), fp32)
    sums = total(
        jnp.concatenate(
            [sums_one[i].reshape(S * Z, rows) for i in range(2)]
            + [
                lax.dynamic_update_slice_in_dim(none, sums_qkv[0, i * hw : (i + 1) * hw], t * hw, 0).reshape(S * Z, rows)
                for i in (0, 2)
            ]
            + [sums_two[i].reshape(S * Z, rows) for i in range(4)]
            + [hidden_sums.reshape(S * Z, R * fr)],
            axis=1,
        )
    )
    sums = lax.dynamic_index_in_dim(sums, s * Z + z, 0, keepdims=False)

    def part(i):
        return sums[i * rows : (i + 1) * rows]

    return (
        layer_out.reshape(inputs.shape),
        grad_inputs.reshape(inputs.shape),
        part(0),
        part(1),
        grad_qkv_matrix,
        part(2),
        part(3),
        grad_attn_matrix,
        part(6),
        part(4),
        part(5),
        grad_hidden_matrix,
        sums[8 * rows :],
        grad_output_matrix,
        part(7),
    )


def solution(mesh):
    tokens = P(("shard", "replica"), "seq", None)
    vector = P(("seq", "shard"))
    matrix = P(("seq", "shard"), None)
    weights = (
        vector,
        vector,
        matrix,
        vector,
        vector,
        matrix,
        vector,
        vector,
        vector,
        matrix,
        vector,
        matrix,
        vector,
    )
    return jax.shard_map(
        on_device,
        mesh=mesh,
        in_specs=(tokens, tokens) + weights,
        out_specs=(tokens, tokens) + weights,
        check_vma=False,
    )
```
